32 devices in a mesh: dp: 16 (over z, y, x), tensor: 2 (over core).
Axes of the slice: x: 2, y: 2, z: 4, core: 2. Of those that a mesh axis runs over, the one named last changes fastest.
Arguments:
- layer_input: bfloat16 [32, 1024, 1024], P('dp', 'tensor'), may hold values from -6 to 6
- cotangent: bfloat16 [32, 1024, 1024], P('dp', 'tensor'), may hold values from -6 to 6
- norm_in: bfloat16 [1024], replicated, may hold values from 0.099609375 to 1.8984375
- norm_mid: bfloat16 [1024], replicated, may hold values from 0.099609375 to 1.8984375
- query_key_value_weight: bfloat16 [1024, 3, 1024], P(None, None, 'tensor'), may hold values from -0.1875 to 0.1875
- attention_out_weight: bfloat16 [1024, 1024], P('tensor'), may hold values from -1.5 to 1.5
- geglu_input_weight: bfloat16 [1024, 2, 2624], P(None, None, 'tensor'), may hold values from -0.1875 to 0.1875
- feedforward_out_weight: bfloat16 [2624, 1024], P('tensor'), may hold values from -0.125 to 0.125
- query_key_value_down: bfloat16 [8, 1024, 16], replicated, may hold values from -0.1875 to 0.1875
- qkv_up: bfloat16 [8, 16, 3, 1024], P(None, None, None, 'tensor'), may hold values from -1.5 to 1.5
- output_down_factor: bfloat16 [8, 1024, 16], P(None, 'tensor'), may hold values from -1.5 to 1.5
- output_up_factor: bfloat16 [8, 16, 1024], replicated, may hold values from -1.5 to 1.5
- input_down_factor: bfloat16 [8, 1024, 16], replicated, may hold values from -0.1875 to 0.1875
- in_up: bfloat16 [8, 16, 2, 2624], P(None, None, None, 'tensor'), may hold values from -1.5 to 1.5
- mlp_down: bfloat16 [8, 2624, 16], P(None, 'tensor'), may hold values from -0.125 to 0.125
- feedforward_up_factor: bfloat16 [8, 16, 1024], replicated, may hold values from -1.5 to 1.5
- segment_ids: int32 [32, 1024], P('dp'), may hold values from 0 to 127, as said below
- adapter_ids: int32 [32], P('dp'), may hold values from 0 to 7, as said below
Outputs:
- output: bfloat16 [32, 1024, 1024], P('dp', 'tensor')
- grad_input: float32 [32, 1024, 1024], P('dp', 'tensor')
- grad_qkv_down: float32 [8, 1024, 16], replicated
- grad_qkv_up: float32 [8, 16, 3, 1024], P(None, None, None, 'tensor')
- grad_out_down: float32 [8, 1024, 16], P(None, 'tensor')
- grad_out_up: float32 [8, 16, 1024], replicated
- grad_in_down: float32 [8, 1024, 16], replicated
- grad_in_up: float32 [8, 16, 2, 2624], P(None, None, None, 'tensor')
- grad_mlp_down: float32 [8, 2624, 16], P(None, 'tensor')
- grad_mlp_up: float32 [8, 16, 1024], replicated
The draws below stay inside these ranges and needn't reach their ends.
Inputs may be any that keep to these rules, and one draw needn't show every extreme that they name: `segment_ids`: along each sequence the numbers start at 0 and never fall; in each aligned block of 2 sequences, one sequence is a single document. `adapter_ids`: every adapter is named by some sequence.
All inputs are finite; a program needn't handle non-finite values.
Results may differ from the reference program's by a relative error of at most 0.023.
The reference program's roundings to bfloat16 on the way count: a program that leaves them out, or rounds other values in their place, can miss the bound.
Values may be sent and summed in bfloat16 or wider, within the bound.
No kernel may reach another device: no remote copies, remote signals or barrier semaphores. Data moves between devices by JAX's collectives and lax.ppermute only.
A program may use at most 384 MiB of HBM per device.

```python
import math
import jax
import jax.numpy as jnp
from jax import lax

D = 1024
HEADS = 16
FF = 2624
HEAD_DIM = 64
RANK = 16
ADAPTERS = 8
LEN = 1024
SEQ_GRP = 2
SEQS = 32


def draw_segment_ids(key, part):
    key = jax.random.fold_in(key, 11)
    level_key, break_key, whole_key, pick_key = jax.random.split(key, 4)
    levels = jax.random.randint(level_key, (SEQS, 1), 0, 4)
    spacing = jnp.power(4, levels) * 8
    drawn = jax.random.randint(break_key, (SEQS, LEN), 0, 1 << 30)
    breaks = (drawn % spacing == 0).astype(jnp.int32)
    breaks = breaks.at[:, 0].set(0)
    groups = SEQS // SEQ_GRP
    single = jax.random.randint(whole_key, (groups, 1), 0, SEQ_GRP)
    places = jnp.arange(LEN, dtype=jnp.int32)
    regular = ((places % 8 == 0) & (places > 0)).astype(jnp.int32)
    chosen_group = jax.random.randint(pick_key, (), 0, groups)
    partner = (single[chosen_group, 0] + 1) % SEQ_GRP
    target = chosen_group * SEQ_GRP + partner
    rows = jnp.arange(SEQS, dtype=jnp.int32)[:, None]
    breaks = jnp.where(rows == target, regular[None, :], breaks)
    owner = jnp.arange(SEQ_GRP, dtype=jnp.int32)[None, :] == single
    breaks = jnp.where(owner.reshape(SEQS, 1), 0, breaks)
    numbered = jnp.cumsum(breaks, axis=1)
    return jnp.minimum(numbered, LEN // 8 - 1).astype(jnp.int32)


def draw_adapter_ids(key, part):
    key = jax.random.fold_in(key, 23)
    pick_key, place_key = jax.random.split(key)
    chosen = jax.random.randint(pick_key, (SEQS,), 0, ADAPTERS)
    spots = jax.random.permutation(place_key, SEQS)[:ADAPTERS]
    return chosen.at[spots].set(jnp.arange(ADAPTERS, dtype=jnp.int32)).astype(jnp.int32)


def shard_levels(rng, dims, cuts, least, high):
    level, own = 1.0, jax.random.fold_in(rng, 6)
    for axis_at, blocks in cuts:
        heights = jnp.exp(jax.random.uniform(jax.random.fold_in(own, axis_at), (blocks,), jnp.float32, least / len(cuts), high / len(cuts)))
        level = level * jnp.repeat(heights, dims[axis_at] // blocks).reshape([-1 if axis == axis_at else 1 for axis in range(len(dims))])
    return level


def gaussian(own_key, extent, spread, most, shards=(), kind=jnp.bfloat16):
    level = shard_levels(own_key, extent, shards, -0.22, 0.18) if shards else 1.0
    values = jax.random.normal(own_key, extent, jnp.float32) * spread * level
    return jnp.minimum(jnp.maximum(values, -most), most).astype(kind)


def setup_inputs(seed: int = 0) -> dict:
    splits = jax.random.split(jax.random.key(seed), 19)
    layer_input = gaussian(splits[0], (SEQS, LEN, D), 1.0, 6.0, ((0, 16), (1, 2)))
    cotangent = gaussian(splits[1], (SEQS, LEN, D), 1.0, 6.0, ((0, 16), (1, 2)))
    norm_in = jnp.clip(1.0 + 0.18 * jax.random.normal(splits[2], (D,), jnp.float32), 0.099609375, 1.8984375).astype(jnp.bfloat16)
    norm_mid = jnp.clip(1.0 + 0.18 * jax.random.normal(splits[3], (D,), jnp.float32), 0.099609375, 1.8984375).astype(jnp.bfloat16)
    query_key_value_weight = gaussian(splits[4], (D, 3, D), D ** -0.5, 0.1875, ((2, 2),))
    attention_out_weight = gaussian(splits[5], (D, D), (max(D // 64, 1)) ** -0.5, 1.5, ((0, 2),))
    geglu_input_weight = gaussian(splits[6], (D, 2, FF), D ** -0.5, 0.1875, ((2, 2),))
    feedforward_out_weight = gaussian(splits[7], (FF, D), FF ** -0.5, 0.125, ((0, 2),))
    query_key_value_down = gaussian(splits[8], (ADAPTERS, D, RANK), D ** -0.5, 0.1875)
    qkv_up = gaussian(splits[9], (ADAPTERS, RANK, 3, D), RANK ** -0.5, 1.5, ((3, 2),))
    output_down_factor = gaussian(splits[10], (ADAPTERS, D, RANK), (max(D // 64, 1)) ** -0.5, 1.5, ((1, 2),))
    output_up_factor = gaussian(splits[11], (ADAPTERS, RANK, D), RANK ** -0.5, 1.5)
    input_down_factor = gaussian(splits[12], (ADAPTERS, D, RANK), D ** -0.5, 0.1875)
    in_up = gaussian(splits[13], (ADAPTERS, RANK, 2, FF), RANK ** -0.5, 1.5, ((3, 2),))
    mlp_down = gaussian(splits[14], (ADAPTERS, FF, RANK), FF ** -0.5, 0.125, ((1, 2),))
    feedforward_up_factor = gaussian(splits[15], (ADAPTERS, RANK, D), RANK ** -0.5, 1.5)
    segment_ids = draw_segment_ids(jax.random.fold_in(splits[18], 71), 0)
    adapter_ids = draw_adapter_ids(jax.random.fold_in(splits[18], 71), 0)
    return dict(layer_input=layer_input, cotangent=cotangent, norm_in=norm_in, norm_mid=norm_mid, query_key_value_weight=query_key_value_weight, attention_out_weight=attention_out_weight, geglu_input_weight=geglu_input_weight, feedforward_out_weight=feedforward_out_weight, query_key_value_down=query_key_value_down, qkv_up=qkv_up, output_down_factor=output_down_factor, output_up_factor=output_up_factor, input_down_factor=input_down_factor, in_up=in_up, mlp_down=mlp_down, feedforward_up_factor=feedforward_up_factor, segment_ids=segment_ids, adapter_ids=adapter_ids)


norm_eps = 1e-05
rope_base = 160000.0
highest_precision = lax.Precision.HIGHEST

@jax.custom_vjp
def reduced_dtype(v):
    return lax.optimization_barrier(v.astype(jnp.bfloat16)).astype(jnp.float32)

@jax.custom_vjp
def reduced_backward(v):
    return v

def low_keep(v):
    return (reduced_dtype(v), None)

def low_pass(kept, grad):
    return (grad,)

def back_keep(v):
    return (v, None)

def back_low(kept, grad):
    return (reduced_dtype(grad),)
reduced_dtype.defvjp(low_keep, low_pass)
reduced_backward.defvjp(back_keep, back_low)

def layer_norm(values, gain):
    average = lax.optimization_barrier(jnp.mean(values, axis=-1, keepdims=True))
    centered = values - average
    variance = lax.optimization_barrier(jnp.mean(centered * centered, axis=-1, keepdims=True))
    return centered * lax.rsqrt(variance + norm_eps) * gain

def rotary_tables(length, head_dim):
    exponent = jnp.arange(0, head_dim, 2, dtype=jnp.float32) / head_dim
    inverse = 1.0 / rope_base ** exponent
    angles = jnp.arange(length, dtype=jnp.float32)[:, None] * inverse[None, :]
    angles = jnp.concatenate([angles, angles], axis=-1)
    return (jnp.cos(angles), jnp.sin(angles))

def rotate(values, cosine_table, sine_table):
    middle_dim = values.shape[-1] // 2
    turned = jnp.concatenate([-values[..., middle_dim:], values[..., :middle_dim]], axis=-1)
    return values * cosine_table[:, None, :] + turned * sine_table[:, None, :]

def gated_gelu(wide_output):
    return jax.nn.gelu(wide_output[:, :, 0], approximate=False) * wide_output[:, :, 1]

def choose_tables(choose, table):
    flat = table.reshape(table.shape[0], -1)
    chosen = jnp.dot(choose, flat, precision=highest_precision)
    return chosen.reshape((choose.shape[0],) + table.shape[1:])

def attend(queries, key_heads, value_heads, segments):
    length = queries.shape[1]
    rows_per = min(512, length)
    blocks = length // rows_per
    score_scale = 1.0 / math.sqrt(queries.shape[-1])

    def one_block(block_index):
        first_row = (block_index * rows_per).astype(jnp.int32)
        query_rows = lax.dynamic_slice_in_dim(queries, first_row, rows_per, 1)
        query_segs = lax.dynamic_slice_in_dim(segments, first_row, rows_per, 1)
        scores = jnp.einsum('sqhe,skhe->shqk', query_rows, key_heads, precision=highest_precision) * score_scale
        scores = reduced_backward(scores)
        allowed = (query_segs[:, :, None] == segments[:, None, :])[:, None]
        masked = jnp.where(allowed, scores, -1e+30)
        largest = lax.optimization_barrier(jnp.max(masked, axis=-1, keepdims=True))
        powered = jnp.exp(masked - largest)
        probs = powered / lax.optimization_barrier(jnp.sum(powered, axis=-1, keepdims=True))
        return jnp.einsum('shqk,skhe->sqhe', reduced_dtype(probs), value_heads, precision=highest_precision)
    mapped = lax.map(jax.checkpoint(one_block), jnp.arange(blocks, dtype=jnp.int32))
    mapped = jnp.moveaxis(mapped, 0, 1)
    return mapped.reshape(queries.shape)

def forward(rows_value, norm_in, norm_mid, query_key_value_weight, attention_out_weight, geglu_input_weight, feedforward_out_weight, tables, segments, choose):
    query_key_value_down, qkv_up, output_down_factor, output_up_factor, input_down_factor, in_up, mlp_down, feedforward_up_factor = tuple((choose_tables(choose, table) for table in tables))
    sequences, length, model_width = rows_value.shape
    input_normalized = reduced_dtype(layer_norm(rows_value, norm_in))
    reduced_qkv_rows = reduced_backward(reduced_dtype(jnp.einsum('knc,kcq->knq', input_normalized, query_key_value_down, precision=highest_precision)))
    projected_rows = jnp.einsum('qzm,mbw->qzbw', input_normalized, query_key_value_weight, precision=highest_precision)
    projected_rows = reduced_backward(projected_rows + jnp.einsum('slr,srcf->slcf', reduced_qkv_rows, qkv_up, precision=highest_precision))
    cosine_table, sine_table = rotary_tables(length, HEAD_DIM)
    head_shape = (sequences, length, HEADS, HEAD_DIM)
    queries = reduced_dtype(rotate(projected_rows[:, :, 0].reshape(head_shape), cosine_table, sine_table))
    key_heads = reduced_dtype(rotate(projected_rows[:, :, 1].reshape(head_shape), cosine_table, sine_table))
    value_heads = reduced_dtype(projected_rows[:, :, 2].reshape(head_shape))
    context_rows = attend(queries, key_heads, value_heads, segments)
    context_rows = reduced_backward(reduced_dtype(context_rows.reshape(sequences, length, model_width)))
    reduced_output = reduced_backward(reduced_dtype(jnp.einsum('knc,kcq->knq', context_rows, output_down_factor, precision=highest_precision)))
    attention_result = jnp.einsum('ojt,tr->ojr', context_rows, attention_out_weight, precision=highest_precision)
    attention_result = reduced_backward(attention_result + jnp.einsum('ihq,iqx->ihx', reduced_output, output_up_factor, precision=highest_precision))
    middle = rows_value + attention_result
    middle_normalized = reduced_dtype(layer_norm(middle, norm_mid))
    reduced_input = reduced_backward(reduced_dtype(jnp.einsum('knc,kcq->knq', middle_normalized, input_down_factor, precision=highest_precision)))
    wide_output = jnp.einsum('qzm,mbw->qzbw', middle_normalized, geglu_input_weight, precision=highest_precision)
    wide_output = reduced_backward(wide_output + jnp.einsum('slr,srcf->slcf', reduced_input, in_up, precision=highest_precision))
    hidden_rows = reduced_dtype(gated_gelu(wide_output))
    reduced_feedforward = reduced_backward(reduced_dtype(jnp.einsum('slf,sfr->slr', hidden_rows, mlp_down, precision=highest_precision)))
    feedforward_output = jnp.einsum('waz,zx->wax', hidden_rows, feedforward_out_weight, precision=highest_precision)
    feedforward_output = reduced_backward(feedforward_output + jnp.einsum('ihq,iqx->ihx', reduced_feedforward, feedforward_up_factor, precision=highest_precision))
    return middle + feedforward_output

def reference(layer_input, cotangent, norm_in, norm_mid, query_key_value_weight, attention_out_weight, geglu_input_weight, feedforward_out_weight, query_key_value_down, qkv_up, output_down_factor, output_up_factor, input_down_factor, in_up, mlp_down, feedforward_up_factor, segment_ids, adapter_ids):
    frozen = tuple((item.astype(jnp.float32) for item in (norm_in, norm_mid, query_key_value_weight, attention_out_weight, geglu_input_weight, feedforward_out_weight)))
    tables = tuple((item.astype(jnp.float32) for item in (query_key_value_down, qkv_up, output_down_factor, output_up_factor, input_down_factor, in_up, mlp_down, feedforward_up_factor)))
    pack_size = math.gcd(SEQS, 4)
    groups = SEQS // pack_size

    def regroup(array):
        return array.reshape((groups, pack_size) + array.shape[1:])

    def one_group(running, inputs):
        rows_in, grads_in, segments, chosen = inputs
        choose = (chosen[:, None] == jnp.arange(ADAPTERS, dtype=jnp.int32)[None, :]).astype(jnp.float32)

        def group_forward(rows_value, tables_value):
            return forward(rows_value, *frozen, tables_value, segments, choose)
        result, pullback = jax.vjp(group_forward, rows_in, tables)
        grad_rows, grad_tables = pullback(grads_in)
        running = tuple((before + update for before, update in zip(running, grad_tables)))
        return (running, (result.astype(jnp.bfloat16), grad_rows))
    initial = tuple((jnp.zeros_like(table) for table in tables))
    running, (outputs, input_grads) = lax.scan(one_group, initial, (regroup(layer_input.astype(jnp.float32)), regroup(cotangent.astype(jnp.float32)), regroup(segment_ids), regroup(adapter_ids)))
    return (outputs.reshape(SEQS, LEN, D), input_grads.reshape(SEQS, LEN, D), running[0], running[1], running[2], running[3], running[4], running[5], running[6], running[7])
```

```python
import functools
import math

import jax
import jax.numpy as jnp
import numpy as np
from jax import lax
from jax.experimental import pallas as pl
from jax.experimental.pallas import tpu as pltpu
from jax.sharding import PartitionSpec as P

F32, BF = jnp.float32, jnp.bfloat16
EPS = 1e-05
VMEM_LIMIT = 62 * 1024 * 1024 - 2**20

def nn(a, b): return lax.dot_general(a, b, (((1,), (0,)), ((), ())), preferred_element_type=F32)
def nt(a, b): return lax.dot_general(a, b, (((1,), (1,)), ((), ())), preferred_element_type=F32)
def tn(a, b): return lax.dot_general(a, b, (((0,), (0,)), ((), ())), preferred_element_type=F32)

def norm_stats(v):
    mean = jnp.mean(v, axis=-1, keepdims=True)
    c = v - mean
    var = jnp.mean(c * c, axis=-1, keepdims=True)
    return c, lax.rsqrt(var + EPS)

def norm_back(e, c, rstd, gain):
    n = c * rstd
    h = e * gain
    return (h - jnp.mean(h, axis=-1, keepdims=True) - n * jnp.mean(h * n, axis=-1, keepdims=True)) * rstd

def mlp_kernel(chunk, main, tail,
        ids, x_ref, cm_ref, cr_ref, g_ref, gain_ref,
        od_ref, ou_ref, id_ref, iu_ref, md_ref, fu_ref,
        wo_own, wo_oth, wi_own, wi_oth, wf_own, wf_oth,
        out_ref, gmid_ref, gcm_ref, gco_ref, d_iu, d_md, d_fu, d_id, d_ou, d_od,
        wo, wi, wf, acc_o, acc_n, acc_lm, acc_li, nm_ref, mid_ref, sem):
    s = pl.program_id(0)
    half = wo_own.shape[0]
    ffh = main + tail
    copies = []
    def cp(src, dst):
        copies.append(pltpu.make_async_copy(src, dst, sem.at[len(copies)]))
    cp(wo_own, wo.at[pl.ds(0, half)])
    cp(wo_oth, wo.at[pl.ds(half, half)])
    for j, (wi_h, wf_h) in enumerate(((wi_own, wf_own), (wi_oth, wf_oth))):
        for b in range(2):
            cp(wi_h.at[b, pl.ds(0, main)], wi.at[b, pl.ds(j * main, main)])
        cp(wf_h.at[pl.ds(0, main)], wf.at[pl.ds(j * main, main)])
        for b in range(2):
            cp(wi_h.at[b, pl.ds(main, tail)], wi.at[b, pl.ds(2 * main + j * tail, tail)])
        cp(wf_h.at[pl.ds(main, tail)], wf.at[pl.ds(2 * main + j * tail, tail)])

    @pl.when(s == 0)
    def _():
        for c in copies: c.start()
        for c in copies[:2]: c.wait()

    cm, cr = cm_ref[0], cr_ref[0]
    od = od_ref[0]
    ou = ou_ref[0]
    low_out = (nt(cm, od[:, :half]) + nt(cr, od[:, half:])).astype(BF)
    att = nn(cm, wo[0:half]) + nn(cr, wo[half:]) + nn(low_out, ou)
    middle = x_ref[0].astype(F32) + att
    mid_ref[...] = middle
    c, rstd = norm_stats(middle)
    gain = gain_ref[...].astype(F32)
    nm = (c * rstd * gain).astype(BF)
    nm_ref[...] = nm
    g = g_ref[0]
    low_in = nt(nm, id_ref[0]).astype(BF)
    glm = nt(g, fu_ref[0]).astype(BF)
    acc_o[...] = jnp.zeros_like(acc_o)
    acc_n[...] = jnp.zeros_like(acc_n)
    acc_lm[...] = jnp.zeros_like(acc_lm)
    acc_li[...] = jnp.zeros_like(acc_li)

    @pl.when(s == 0)
    def _():
        for c_ in copies[2:]: c_.wait()

    def step(first, size):
        rows = pl.ds(first, size)
        nm = nm_ref[...]
        g = g_ref[0]
        w0, w1, wfc = wi[0, rows], wi[1, rows], wf[rows]
        iu0, iu1, md = iu_ref[0, 0, :, rows], iu_ref[0, 1, :, rows], md_ref[0, :, rows]
        u = nt(nm, w0) + nn(low_in, iu0)
        v = nt(nm, w1) + nn(low_in, iu1)
        gh = nt(g, wfc) + nn(glm, md)
        cdf = 0.5 * (1.0 + lax.erf(u * (1.0 / math.sqrt(2.0))))
        pdf = jnp.exp(-0.5 * u * u) * (1.0 / math.sqrt(2.0 * math.pi))
        gel = u * cdf
        h = (gel * v).astype(BF)
        gu = (gh * v * (cdf + u * pdf)).astype(BF)
        gv = (gh * gel).astype(BF)
        acc_o[...] += nn(h, wfc)
        acc_n[...] += nn(gu, w0) + nn(gv, w1)
        acc_lm[...] += nt(h, md)
        acc_li[...] += nt(gu, iu0) + nt(gv, iu1)
        d_iu[0, 0, :, rows] = tn(low_in, gu)
        d_iu[0, 1, :, rows] = tn(low_in, gv)
        d_md[0, :, rows] = tn(glm, h)

    def loop(i, carry):
        step(pl.multiple_of(i * chunk, chunk), chunk)
        return carry
    lax.fori_loop(0, 2 * main // chunk, loop, 0)
    step(2 * main, 2 * tail)

    fu = fu_ref[0]
    low_mlp = acc_lm[...].astype(BF)
    out_ref[0] = (mid_ref[...] + acc_o[...] + nn(low_mlp, fu)).astype(BF)
    g = g_ref[0]
    d_fu[0] = tn(low_mlp, g)
    gli = acc_li[...].astype(BF)
    d_id[0] = tn(gli, nm_ref[...])
    gnm = acc_n[...] + nn(gli, id_ref[0])
    c, rstd = norm_stats(mid_ref[...])
    gmid = g.astype(F32) + norm_back(gnm, c, rstd, gain)
    gmid_ref[0] = gmid
    ga = gmid.astype(BF)
    glo = nt(ga, ou).astype(BF)
    d_ou[0] = tn(low_out, ga)
    gcm_ref[0] = (nt(ga, wo[0:half]) + nn(glo, od[:, :half])).astype(BF)
    gco_ref[0] = (nt(ga, wo[half:]) + nn(glo, od[:, half:])).astype(BF)
    d_od[0, :, :half] = tn(glo, cm)
    d_od[0, :, half:] = tn(glo, cr)

def mlp_call(ids, x, cm, cr, g, gain, od, ou, idn, iu, md, fu, wo_own, wo_oth, wi_own, wi_oth, wf_own, wf_oth, chunk=512):
    S, R, D = x.shape
    half = wo_own.shape[0]
    ffh = wf_own.shape[0]
    main = ffh // 256 * 256
    tail = ffh - main
    rank = ou.shape[1]
    ff = 2 * ffh
    seq = lambda *bs: pl.BlockSpec((1,) + bs, lambda s, ids: (s,) + (0,) * len(bs))
    tab = lambda *bs: pl.BlockSpec((1,) + bs, lambda s, ids: (ids[s],) + (0,) * len(bs))
    any_ = pl.BlockSpec(memory_space=pl.ANY)
    in_specs = [seq(R, D), seq(R, half), seq(R, half), seq(R, D), pl.BlockSpec((1, D), lambda s, ids: (0, 0)),
        seq(rank, D), tab(rank, D), tab(rank, D), seq(2, rank, ff), seq(rank, ff), tab(rank, D)] + [any_] * 6
    out_specs = [seq(R, D), seq(R, D), seq(R, half), seq(R, half), seq(2, rank, ff), seq(rank, ff), seq(rank, D), seq(rank, D), seq(rank, D), seq(rank, D)]
    sd = jax.ShapeDtypeStruct
    out_shape = [sd((S, R, D), BF), sd((S, R, D), F32), sd((S, R, half), BF), sd((S, R, half), BF),
        sd((S, 2, rank, ff), F32), sd((S, rank, ff), F32)] + [sd((S, rank, D), F32)] * 4
    scratch = [pltpu.VMEM((2 * half, D), BF), pltpu.VMEM((2, ff, D), BF), pltpu.VMEM((ff, D), BF),
        pltpu.VMEM((R, D), F32), pltpu.VMEM((R, D), F32), pltpu.VMEM((R, rank), F32), pltpu.VMEM((R, rank), F32),
        pltpu.VMEM((R, D), BF), pltpu.VMEM((R, D), F32), pltpu.SemaphoreType.DMA((14,))]
    return pl.pallas_call(functools.partial(mlp_kernel, chunk, main, tail),
        grid_spec=pltpu.PrefetchScalarGridSpec(num_scalar_prefetch=1, grid=(S,), in_specs=in_specs, out_specs=out_specs, scratch_shapes=scratch),
        out_shape=out_shape,
        compiler_params=pltpu.CompilerParams(dimension_semantics=("arbitrary",), vmem_limit_bytes=VMEM_LIMIT),
        cost_estimate=pl.CostEstimate(flops=40 * 10**9, bytes_accessed=40 * 10**6, transcendentals=3 * 10**6),
        name="mlp")(ids, x, cm, cr, g, gain, od, ou, idn, iu, md, fu, wo_own, wo_oth, wi_own, wi_oth, wf_own, wf_oth)

LOG2E = 1.4426950408889634

def lanes_of(head, shape):
    return (lax.broadcasted_iota(jnp.int32, shape, len(shape) - 1) // 64) == head

def swap(u):
    lane = lax.broadcasted_iota(jnp.int32, u.shape, 1)
    return jnp.where((lane & 63) < 32, pltpu.roll(u, 96, 1), pltpu.roll(u, 32, 1))


def qkv_kernel(ids, half_ref, x_ref, gain_ref, w_ref, ad_ref, up_ref, cos_ref, sin_ref, *rest):
    q_ref, k_ref, v_ref, low_ref = rest[-4:]
    c, rstd = norm_stats(x_ref[0].astype(F32))
    nm = (c * rstd * gain_ref[...].astype(F32)).astype(BF)
    low = nt(nm, ad_ref[0]).astype(BF)
    low_ref[0] = low
    cos, sin = cos_ref[...], sin_ref[...]
    for b, ref in enumerate((q_ref, k_ref)):
        u = nn(nm, w_ref[b]) + nn(low, up_ref[0, b])
        for p in range(u.shape[1] // 128):
            t = u[:, p * 128:(p + 1) * 128]
            ref[0, :, p * 128:(p + 1) * 128] = (t * cos + swap(t) * sin).astype(BF)
    v_ref[0] = (nn(nm, w_ref[2]) + nn(low, up_ref[0, 2])).astype(BF)

def qkv_call(ids, half_index, x, gain, w, ad, up, cos, sin, before=None):
    S, R, D = x.shape
    W = w.shape[2]
    rank = ad.shape[1]
    L = cos.shape[0]
    tabl = lambda *bs: pl.BlockSpec((1,) + bs, lambda s, ids, h: (ids[s],) + (0,) * len(bs))
    in_specs = [pl.BlockSpec((1, R, D), lambda s, ids, h: (s, 0, 0)), pl.BlockSpec((1, D), lambda s, ids, h: (0, 0)),
        pl.BlockSpec((3, D, W), lambda s, ids, h: (0, 0, 0)), tabl(rank, D), tabl(3, rank, W),
        pl.BlockSpec((R, 128), lambda s, ids, h: (h[0], 0)), pl.BlockSpec((R, 128), lambda s, ids, h: (h[0], 0))]
    args = [ids, half_index, x, gain, w, ad, up, cos, sin]
    alias = {}
    if before is not None:
        for i, b in enumerate(before):
            alias[len(args)] = i
            args.append(b)
            in_specs.append(pl.BlockSpec(memory_space=pl.ANY))
    osp = pl.BlockSpec((1, R, W), lambda s, ids, h: (s, h[0], 0))
    sd = jax.ShapeDtypeStruct
    return pl.pallas_call(qkv_kernel,
        grid_spec=pltpu.PrefetchScalarGridSpec(num_scalar_prefetch=2, grid=(S,), in_specs=in_specs,
            out_specs=[osp, osp, osp, pl.BlockSpec((1, R, rank), lambda s, ids, h: (s, h[0], 0))]),
        out_shape=[sd((S, L, W), BF)] * 3 + [sd((S, L, rank), BF)],
        input_output_aliases=alias,
        compiler_params=pltpu.CompilerParams(dimension_semantics=("arbitrary",), vmem_limit_bytes=40 * 2**20),
        cost_estimate=pl.CostEstimate(flops=5 * 10**9, bytes_accessed=10**7, transcendentals=10**5),
        name="qkv")(*args)

def window(seg, s, i, blk, count):
    first, last = seg[s, i * blk], seg[s, i * blk + blk - 1]
    lo = jnp.int32(0); hi = jnp.int32(0)
    for j in range(count):
        lo += (seg[s, j * blk + blk - 1] < first).astype(jnp.int32)
        hi += (seg[s, j * blk] <= last).astype(jnp.int32)
    return lo, hi - lo

def att_kernel(blk, seg, half_ref, q_ref, k_ref, v_ref, sq_ref, sk_ref, o_ref, lse_ref):
    s = pl.program_id(0)
    R, L = q_ref.shape[1], k_ref.shape[1]
    count = L // blk
    scale = LOG2E / 8.0
    single = seg[s, 0] == seg[s, L - 1]

    def attend(r0, rows, k0, keys, masked):
        q = q_ref[0, pl.ds(r0, rows)]
        k = k_ref[0, pl.ds(k0, keys)]
        v = v_ref[0, pl.ds(k0, keys)]
        outs = []
        for h in range(2):
            qh = jnp.where(lanes_of(h, q.shape), q, jnp.zeros_like(q))
            sc = nt(qh, k)
            if masked:
                allowed = sq_ref[0, pl.ds(r0, rows)] == sk_ref[0, :, pl.ds(k0, keys)]
                sc = jnp.where(allowed, sc, -1e30)
            m = jnp.max(sc, axis=-1, keepdims=True)
            p = jnp.exp2(sc * scale - m * scale)
            l = jnp.sum(p, axis=-1, keepdims=True)
            o = nn(p.astype(BF), v) * (1.0 / l)
            outs.append(o)
            lse = jnp.broadcast_to(m * scale + jnp.log2(l), (rows, 128))
            lse_ref[0, 0, pl.ds(h, 1), pl.ds(r0, rows)] = lse.T[0:1]
        o_ref[0, pl.ds(r0, rows)] = jnp.where(lanes_of(0, outs[0].shape), outs[0], outs[1]).astype(BF)

    @pl.when(single)
    def _():
        attend(0, R, 0, L, False)

    @pl.when(jnp.logical_not(single))
    def _():
        def sub(i, carry):
            lo, n = window(seg, s, half_ref[0] * (R // blk) + i, blk, count)
            r0 = pl.multiple_of(i * blk, blk)
            k0 = pl.multiple_of(lo * blk, blk)
            for m in range(1, count + 1):
                @pl.when(n == m)
                def _():
                    attend(r0, blk, k0, m * blk, True)
            return carry
        lax.fori_loop(0, R // blk, sub, 0)

def att_call(seg, half_index, q, k, v, seg_col, seg_row, blk=256):
    S, L, W = q.shape
    R = L // 2
    P = W // 128
    sd = jax.ShapeDtypeStruct
    return pl.pallas_call(functools.partial(att_kernel, blk),
        grid_spec=pltpu.PrefetchScalarGridSpec(num_scalar_prefetch=2, grid=(S, P),
            in_specs=[pl.BlockSpec((1, R, 128), lambda s, p, seg, h: (s, h[0], p)),
                pl.BlockSpec((1, L, 128), lambda s, p, seg, h: (s, 0, p)), pl.BlockSpec((1, L, 128), lambda s, p, seg, h: (s, 0, p)),
                pl.BlockSpec((1, R, 1), lambda s, p, seg, h: (s, h[0], 0)), pl.BlockSpec((1, 1, L), lambda s, p, seg, h: (s, 0, 0))],
            out_specs=[pl.BlockSpec((1, R, 128), lambda s, p, seg, h: (s, 0, p)),
                pl.BlockSpec((1, 1, 2, R), lambda s, p, seg, h: (s, p, 0, 0))]),
        out_shape=[sd((S, R, W), BF), sd((S, P, 2, R), F32)],
        compiler_params=pltpu.CompilerParams(dimension_semantics=("arbitrary", "arbitrary"), vmem_limit_bytes=VMEM_LIMIT),
        cost_estimate=pl.CostEstimate(flops=8 * 10**9, bytes_accessed=8 * 10**6, transcendentals=8 * 10**6),
        name="attend")(seg, half_index, q, k, v, seg_col, seg_row)

def back_kernel(blk, seg, half_ref, ids, q_ref, k_ref, v_ref, dom_ref, doo_ref, om_ref, oo_ref, lsem_ref, lseo_ref, sc_ref, sr_ref,
        cos_ref, sin_ref, low_ref, up_ref,
        gpm_ref, gpo_ref, dup_ref, lgm_ref, lgo_ref, dq_acc, dk_acc, dv_acc):
    s, pair = pl.program_id(0), pl.program_id(1)
    L = q_ref.shape[1]
    R = L // 2
    count = L // blk
    scale = LOG2E / 8.0
    single = seg[s, 0] == seg[s, L - 1]
    mine = half_ref[0]
    dk_acc[...] = jnp.zeros_like(dk_acc)
    dv_acc[...] = jnp.zeros_like(dv_acc)

    def part(do_ref, o_ref, lse_ref, n0, r0, rows, k0, keys, masked):
        q = q_ref[0, pl.ds(n0, rows)]
        do = do_ref[0, pl.ds(r0, rows)]
        o = o_ref[0, pl.ds(r0, rows)]
        k = k_ref[0, pl.ds(k0, keys)]
        v = v_ref[0, pl.ds(k0, keys)]
        prod = (do.astype(F32) * o.astype(F32)).T
        zero = jnp.zeros_like(q)
        if masked:
            allowed = sc_ref[0, pl.ds(k0, keys)] == sr_ref[0, :, pl.ds(n0, rows)]
        ps, dss, dos, qs, ks = [], [], [], [], []
        for h in range(2):
            qh = jnp.where(lanes_of(h, q.shape), q, zero)
            doh = jnp.where(lanes_of(h, q.shape), do, zero)
            kh = jnp.where(lanes_of(h, k.shape), k, jnp.zeros_like(k))
            delta = jnp.sum(prod[h * 64:(h + 1) * 64], axis=0, keepdims=True)
            lse = lse_ref[0, 0, pl.ds(h, 1), pl.ds(r0, rows)]
            st = nt(k, qh)
            p = jnp.exp2(st * scale - lse)
            if masked:
                p = jnp.where(allowed, p, 0.0)
            ds = p * (nt(v, doh) - delta)
            ps.append(p.astype(BF)); dss.append(ds.astype(BF)); dos.append(doh); qs.append(qh); ks.append(kh)
        dv_acc[pl.ds(k0, keys)] += nn(jnp.concatenate(ps, 1), jnp.concatenate(dos, 0))
        dk_acc[pl.ds(k0, keys)] += nn(jnp.concatenate(dss, 1), jnp.concatenate(qs, 0))
        dq_acc[pl.ds(n0, rows)] = tn(jnp.concatenate(dss, 0), jnp.concatenate(ks, 0))

    halves = ((dom_ref, om_ref, lsem_ref, mine), (doo_ref, oo_ref, lseo_ref, 1 - mine))

    @pl.when(single)
    def _():
        for do_ref, o_ref, lse_ref, h in halves:
            part(do_ref, o_ref, lse_ref, pl.multiple_of(h * R, R), 0, R, 0, L, False)

    @pl.when(jnp.logical_not(single))
    def _():
        for do_ref, o_ref, lse_ref, h in halves:
            def sub(i, carry):
                lo, n = window(seg, s, h * (R // blk) + i, blk, count)
                r0 = pl.multiple_of(i * blk, blk)
                n0 = pl.multiple_of(h * R + i * blk, blk)
                k0 = pl.multiple_of(lo * blk, blk)
                for m in range(1, count + 1):
                    @pl.when(n == m)
                    def _():
                        part(do_ref, o_ref, lse_ref, n0, r0, blk, k0, m * blk, True)
                return carry
            lax.fori_loop(0, R // blk, sub, 0)

    cos, sin = cos_ref[...], sin_ref[...]
    def unrotate(g):
        g = g * 0.125
        return (g * cos - swap(g) * sin).astype(BF)
    dq_acc[...] = unrotate(dq_acc[...]).astype(F32)
    dk_acc[...] = unrotate(dk_acc[...]).astype(F32)
    lgs = None
    for b, acc in enumerate((dq_acc, dk_acc, dv_acc)):
        g = acc[...].astype(BF)
        dup_ref[0, b] = tn(low_ref[0], g)
        lg = nt(g, up_ref[0, b])
        lgs = lg if lgs is None else lgs + lg
        for ref, h in ((gpm_ref, mine), (gpo_ref, 1 - mine)):
            ref[0, b] = acc[pl.ds(pl.multiple_of(h * R, R), R)].astype(BF)
    dq_acc[:, :lgs.shape[1]] = lgs
    for ref, h in ((lgm_ref, mine), (lgo_ref, 1 - mine)):
        part_ = dq_acc[pl.ds(pl.multiple_of(h * R, R), R), :lgs.shape[1]]
        @pl.when(pair == 0)
        def _():
            ref[0] = part_
        @pl.when(pair > 0)
        def _():
            ref[0] += part_

def back_call(seg, half_index, ids, q, k, v, dom, doo, om, oo, lsem, lseo, seg_col, seg_row, cos, sin, low, up, blk=256):
    S, L, W = q.shape
    R = L // 2
    P = W // 128
    rank = low.shape[2]
    sd = jax.ShapeDtypeStruct
    full = pl.BlockSpec((1, L, 128), lambda s, p, *_: (s, 0, p))
    hlf = pl.BlockSpec((1, R, 128), lambda s, p, *_: (s, 0, p))
    ls = pl.BlockSpec((1, 1, 2, R), lambda s, p, *_: (s, p, 0, 0))
    tb = pl.BlockSpec((L, 128), lambda s, p, *_: (0, 0))
    gp = pl.BlockSpec((1, 3, R, 128), lambda s, p, *_: (s, 0, 0, p))
    lg = pl.BlockSpec((1, R, rank), lambda s, p, *_: (s, 0, 0))
    return pl.pallas_call(functools.partial(back_kernel, blk),
        grid_spec=pltpu.PrefetchScalarGridSpec(num_scalar_prefetch=3, grid=(S, P),
            in_specs=[full, full, full, hlf, hlf, hlf, hlf, ls, ls,
                pl.BlockSpec((1, L, 1), lambda s, p, *_: (s, 0, 0)), pl.BlockSpec((1, 1, L), lambda s, p, *_: (s, 0, 0)),
                tb, tb, pl.BlockSpec((1, L, rank), lambda s, p, *_: (s, 0, 0)),
                pl.BlockSpec((1, 3, rank, 128), lambda s, p, seg, h, ids: (ids[s], 0, 0, p))],
            out_specs=[gp, gp, pl.BlockSpec((1, 3, rank, 128), lambda s, p, *_: (s, 0, 0, p)), lg, lg],
            scratch_shapes=[pltpu.VMEM((L, 128), F32)] * 3),
        out_shape=[sd((S, 3, R, W), BF), sd((S, 3, R, W), BF), sd((S, 3, rank, W), F32), sd((S, R, rank), F32), sd((S, R, rank), F32)],
        compiler_params=pltpu.CompilerParams(dimension_semantics=("arbitrary", "arbitrary"), vmem_limit_bytes=VMEM_LIMIT),
        cost_estimate=pl.CostEstimate(flops=36 * 10**9, bytes_accessed=2 * 10**7, transcendentals=16 * 10**6),
        name="attend_back")(seg, half_index, ids, q, k, v, dom, doo, om, oo, lsem, lseo, seg_col, seg_row, cos, sin, low, up)

def final_kernel(ids, x_ref, gain_ref, gm_ref, gr_ref, wo_ref, wr_ref, lg_ref, ad_ref, mid_ref, out_ref):
    gn = nn(lg_ref[0], ad_ref[0])
    for b in range(3):
        gn += nt(gm_ref[0, b], wo_ref[b]) + nt(gr_ref[0, b], wr_ref[b])
    c, rstd = norm_stats(x_ref[0].astype(F32))
    out_ref[0] = mid_ref[0] + norm_back(gn, c, rstd, gain_ref[...].astype(F32))

def final_call(ids, x, gain, gm, gr, w_own, w_oth, lg, ad, mid, rows=256):
    S, R, D = x.shape
    W = w_own.shape[2]
    rank = lg.shape[2]
    gp = pl.BlockSpec((1, 3, rows, W), lambda s, i, ids: (s, 0, i, 0))
    wsp = pl.BlockSpec((3, D, W), lambda s, i, ids: (0, 0, 0))
    row = pl.BlockSpec((1, rows, D), lambda s, i, ids: (s, i, 0))
    return pl.pallas_call(final_kernel,
        grid_spec=pltpu.PrefetchScalarGridSpec(num_scalar_prefetch=1, grid=(S, R // rows),
            in_specs=[row, pl.BlockSpec((1, D), lambda s, i, ids: (0, 0)), gp, gp, wsp, wsp,
                pl.BlockSpec((1, rows, rank), lambda s, i, ids: (s, i, 0)), pl.BlockSpec((1, rank, D), lambda s, i, ids: (ids[s], 0, 0)), row],
            out_specs=row),
        out_shape=jax.ShapeDtypeStruct((S, R, D), F32),
        compiler_params=pltpu.CompilerParams(dimension_semantics=("arbitrary", "arbitrary"), vmem_limit_bytes=40 * 2**20),
        cost_estimate=pl.CostEstimate(flops=7 * 10**9, bytes_accessed=2 * 10**7, transcendentals=10**4),
        name="final")(ids, x, gain, gm, gr, w_own, w_oth, lg, ad, mid)

def down_kernel(lgm_ref, lgr_ref, x_ref, gain_ref, lg_ref, dd_ref):
    c, rstd = norm_stats(x_ref[0].astype(F32))
    nm = (c * rstd * gain_ref[...].astype(F32)).astype(BF)
    lg = (lgm_ref[0] + lgr_ref[0]).astype(BF)
    lg_ref[0] = lg
    dd_ref[0] = tn(lg, nm)

def down_call(lgm, lgr, x, gain):
    S, R, D = x.shape
    rank = lgm.shape[2]
    seq = lambda *bs: pl.BlockSpec((1,) + bs, lambda s: (s,) + (0,) * len(bs))
    return pl.pallas_call(down_kernel, grid=(S,), in_specs=[seq(R, rank), seq(R, rank), seq(R, D), pl.BlockSpec((1, D), lambda s: (0, 0))],
        out_specs=[seq(R, rank), seq(rank, D)],
        out_shape=[jax.ShapeDtypeStruct((S, R, rank), BF), jax.ShapeDtypeStruct((S, rank, D), F32)],
        compiler_params=pltpu.CompilerParams(dimension_semantics=("arbitrary",), vmem_limit_bytes=32 * 2**20),
        cost_estimate=pl.CostEstimate(flops=10**8, bytes_accessed=3 * 10**6, transcendentals=10**4),
        name="down")(lgm, lgr, x, gain)


HEAD_DIM = 64
ROPE_BASE = 160000.0


def rotary_tables(length):
    inverse = 1.0 / ROPE_BASE ** (np.arange(0, HEAD_DIM, 2) / HEAD_DIM)
    angles = np.arange(length)[:, None] * inverse[None, :]
    cos, sin = np.cos(angles), np.sin(angles)
    return (
        jnp.asarray(np.concatenate([cos, cos, cos, cos], 1), F32),
        jnp.asarray(np.concatenate([-sin, sin, -sin, sin], 1), F32),
    )


def pick(table, ids):
    return jnp.concatenate([lax.dynamic_slice_in_dim(table, ids[i], 1, 0) for i in range(ids.shape[0])], 0)


def body(x, cotangent, norm_in, norm_mid, w_qkv, w_out, w_in, w_ff, qkv_down, qkv_up, out_down, out_up, in_down, in_up,
         mlp_down, ff_up, segs, ids):
    other = lambda a: lax.ppermute(a, "tensor", [(0, 1), (1, 0)])
    t = lax.axis_index("tensor")
    shards = lax.axis_size("dp")
    mine, its = t.astype(jnp.int32).reshape(1), (1 - t).astype(jnp.int32).reshape(1)
    S, R, D = x.shape
    L = segs.shape[1]
    w_qkv = w_qkv.transpose(1, 0, 2)
    w_in = w_in.transpose(1, 2, 0)
    qkv_down, out_down, in_down, mlp_down = (a.transpose(0, 2, 1) for a in (qkv_down, out_down, in_down, mlp_down))
    qkv_up = qkv_up.transpose(0, 2, 1, 3)
    gain_in, gain_mid = norm_in.reshape(1, D), norm_mid.reshape(1, D)
    half = w_out.shape[0]
    ffh = w_ff.shape[0]
    main = ffh // 256 * 256
    rank = out_up.shape[1]
    adapters = out_up.shape[0]
    choose = (ids[:, None] == jnp.arange(adapters, dtype=jnp.int32)[None, :]).astype(BF)

    x_its = other(x)
    in_up_own = pick(in_up, ids).transpose(0, 2, 1, 3)
    own = [pick(out_down, ids), in_up_own[:, 0], in_up_own[:, 1], pick(mlp_down, ids)]
    got = other(jnp.concatenate(own, 2))
    oth = [got[:, :, :half]] + [got[:, :, half + i * ffh: half + (i + 1) * ffh] for i in range(3)]
    lay = lambda a, b: jnp.concatenate([a[..., :main], b[..., :main], a[..., main:], b[..., main:]], -1)
    od = jnp.concatenate([own[0], oth[0]], 2)
    iu = jnp.stack([lay(own[1], oth[1]), lay(own[2], oth[2])], 1)
    md = lay(own[3], oth[3])
    w_out_its, w_in_its, w_ff_its, w_qkv_its = other(w_out), other(w_in), other(w_ff), other(w_qkv)

    cos, sin = rotary_tables(L)
    seg_col, seg_row = segs[:, :, None], segs[:, None, :]
    first = qkv_call(ids, mine, x, gain_in, w_qkv, qkv_down, qkv_up, cos, sin)
    q, k, v, low = qkv_call(ids, its, x_its, gain_in, w_qkv, qkv_down, qkv_up, cos, sin, before=first)
    ctx_its, lse_its = att_call(segs, its, q, k, v, seg_col, seg_row)
    ctx_got = other(ctx_its)
    ctx_mine, lse_mine = att_call(segs, mine, q, k, v, seg_col, seg_row)
    output, grad_mid, gc_mine, gc_its, d_iu, d_md, d_fu, d_id, d_ou, d_od = mlp_call(
        ids, x, ctx_mine, ctx_got, cotangent, gain_mid, od, out_up, in_down, iu, md, ff_up,
        w_out, w_out_its, w_in, w_in_its, w_ff, w_ff_its)
    gc_got = other(gc_its)

    D2 = D // 2
    ff_own = lambda a: [a[..., :main], a[..., 2 * main: main + ffh]]
    ff_oth = lambda a: [a[..., main: 2 * main], a[..., main + ffh:]]
    cut = lambda a, at: lax.dynamic_slice_in_dim(a, at * D2, D2, 2)
    pack = lambda f, at, lo: jnp.concatenate(
        f(d_iu[:, 0]) + f(d_iu[:, 1]) + f(d_md) + [lo] + [cut(a, at) for a in (d_fu, d_id, d_ou)], -1)
    keep = pack(ff_own, t, d_od[:, :, :half])
    send = pack(ff_oth, 1 - t, d_od[:, :, half:])

    def spread(terms):
        flat = [a.astype(BF).reshape(S, shards, -1) for a in terms]
        tag = jnp.broadcast_to(choose[:, None, :], (S, shards, adapters))
        got = lax.all_to_all(jnp.concatenate(flat + [tag], -1), "dp", 1, 0, tiled=True).reshape(S * shards, -1)
        return lax.dot_general(got[:, -adapters:], got[:, :-adapters], (((0,), (0,)), ((), ())), preferred_element_type=F32)

    def collect(shares):
        wide = jnp.broadcast_to(shares.astype(BF)[None], (shards,) + shares.shape)
        return lax.all_to_all(wide, "dp", 0, 0, tiled=True).transpose(1, 0, 2)

    whole = lambda a: a.reshape(adapters, rank, -1).astype(F32)
    terms = keep + other(send.astype(BF)).astype(F32)
    sums = whole(collect(spread([terms])))
    g_in_up = jnp.stack([sums[..., :ffh], sums[..., ffh: 2 * ffh]], 2)
    g_mlp_down = sums[..., 2 * ffh: 3 * ffh].transpose(0, 2, 1)
    g_out_down = sums[..., 3 * ffh: 3 * ffh + half].transpose(0, 2, 1)
    part = sums[..., 3 * ffh + half:]
    part_its = other(part.astype(BF)).astype(F32)
    lo, hi = jnp.where(t == 0, part, part_its), jnp.where(t == 0, part_its, part)
    g_ff_up, g_in_down, g_out_up = (
        jnp.concatenate([lo[..., i * D2: (i + 1) * D2], hi[..., i * D2: (i + 1) * D2]], -1) for i in range(3))

    gp_mine, gp_its, d_up, lg_mine, lg_its = back_call(
        segs, mine, ids, q, k, v, gc_mine, gc_got, ctx_mine, ctx_its, lse_mine, lse_its, seg_col, seg_row, cos, sin, low, qkv_up)
    lg_got = other(lg_its)
    gp_got = other(gp_its)
    lg, d_down = down_call(lg_mine, lg_got, x, gain_in)
    d_up = jnp.concatenate([d_up[:, 0], d_up[:, 1], d_up[:, 2]], -1)
    shares = spread([d_up, d_down])
    ups = rank * d_up.shape[2] // shards
    downs = shares[:, ups:]
    shares = collect(jnp.concatenate([shares[:, :ups], downs + other(downs)], -1))
    g_qkv_up = whole(shares[:, :, :ups]).reshape(adapters, rank, 3, -1)
    g_qkv_down = whole(shares[:, :, ups:]).transpose(0, 2, 1)
    grad_input = final_call(ids, x, gain_in, gp_mine, gp_got, w_qkv, w_qkv_its, lg, qkv_down, grad_mid)
    return (output, grad_input, g_qkv_down, g_qkv_up, g_out_down, g_out_up, g_in_down.transpose(0, 2, 1), g_in_up, g_mlp_down, g_ff_up)


def solution(mesh):
    return jax.shard_map(
        body,
        mesh=mesh,
        in_specs=(
            P("dp", "tensor", None),
            P("dp", "tensor", None),
            P(),
            P(),
            P(None, None, "tensor"),
            P("tensor", None),
            P(None, None, "tensor"),
            P("tensor", None),
            P(),
            P(None, None, None, "tensor"),
            P(None, "tensor", None),
            P(),
            P(),
            P(None, None, None, "tensor"),
            P(None, "tensor", None),
            P(),
            P("dp", None),
            P("dp"),
        ),
        out_specs=(
            P("dp", "tensor", None),
            P("dp", "tensor", None),
            P(),
            P(None, None, None, "tensor"),
            P(None, "tensor", None),
            P(),
            P(),
            P(None, None, None, "tensor"),
            P(None, "tensor", None),
            P(),
        ),
        check_vma=False,
    )
```

```python
import functools
import math

import jax
import jax.numpy as jnp
import numpy as np
from jax import lax
from jax.experimental import pallas as pl
from jax.experimental.pallas import tpu as pltpu
from jax.sharding import PartitionSpec as P

F32, BF = jnp.float32, jnp.bfloat16
EPS = 1e-05
VMEM_LIMIT = 62 * 1024 * 1024 - 2**20

def nn(a, b): return lax.dot_general(a, b, (((1,), (0,)), ((), ())), preferred_element_type=F32)
def nt(a, b): return lax.dot_general(a, b, (((1,), (1,)), ((), ())), preferred_element_type=F32)
def tn(a, b): return lax.dot_general(a, b, (((0,), (0,)), ((), ())), preferred_element_type=F32)

def norm_stats(v):
    mean = jnp.mean(v, axis=-1, keepdims=True)
    c = v - mean
    var = jnp.mean(c * c, axis=-1, keepdims=True)
    return c, lax.rsqrt(var + EPS)

def norm_back(e, c, rstd, gain):
    n = c * rstd
    h = e * gain
    return (h - jnp.mean(h, axis=-1, keepdims=True) - n * jnp.mean(h * n, axis=-1, keepdims=True)) * rstd

def mlp_kernel(chunk, main, tail,
        ids, at_ref, x_ref, cm_ref, cr_ref, g_ref, gain_ref,
        od_own, od_its, iu_own, iu_its, md_own, md_its, ou_ref, id_ref, fu_ref,
        wo_own, wo_its, wi_own, wi_its, wf_own, wf_its,
        out_ref, gmid_ref, gcm_ref, gci_ref, keep_ref, send_ref,
        wo, wi, wf, acc_o, acc_n, acc_lm, acc_li, nm_ref, mid_ref, iu, md, d_iu, d_md, d_w, sem):
    s = pl.program_id(0)
    half = wo_own.shape[0]
    rank = ou_ref.shape[1]
    copies = []
    def cp(src, dst):
        copies.append(pltpu.make_async_copy(src, dst, sem.at[len(copies)]))
    cp(wo_own, wo.at[pl.ds(0, half)])
    cp(wo_its, wo.at[pl.ds(half, half)])
    for j, (wi_h, wf_h) in enumerate(((wi_own, wf_own), (wi_its, wf_its))):
        for b in range(2):
            cp(wi_h.at[b, pl.ds(0, main)], wi.at[b, pl.ds(j * main, main)])
        cp(wf_h.at[pl.ds(0, main)], wf.at[pl.ds(j * main, main)])
        for b in range(2):
            cp(wi_h.at[b, pl.ds(main, tail)], wi.at[b, pl.ds(2 * main + j * tail, tail)])
        cp(wf_h.at[pl.ds(main, tail)], wf.at[pl.ds(2 * main + j * tail, tail)])

    @pl.when(s == 0)
    def _():
        for c in copies: c.start()
        for c in copies[:2]: c.wait()

    for dst, own, its in ((iu.at[0], iu_own[0, 0], iu_its[0, 0]), (iu.at[1], iu_own[0, 1], iu_its[0, 1]), (md, md_own[0], md_its[0])):
        dst[:, :main] = own[:, :main]
        dst[:, main:2 * main] = its[:, :main]
        dst[:, 2 * main:] = jnp.concatenate([own[:, main:].astype(F32), its[:, main:].astype(F32)], 1).astype(BF)

    cm, cr = cm_ref[0], cr_ref[0]
    odo, odi = od_own[0], od_its[0]
    ou = ou_ref[0]
    low_out = (nt(cm, odo) + nt(cr, odi)).astype(BF)
    att = nn(cm, wo[0:half]) + nn(cr, wo[half:]) + nn(low_out, ou)
    middle = x_ref[0].astype(F32) + att
    mid_ref[...] = middle
    c, rstd = norm_stats(middle)
    gain = gain_ref[...].astype(F32)
    nm = (c * rstd * gain).astype(BF)
    nm_ref[...] = nm
    g = g_ref[0]
    low_in = nt(nm, id_ref[0]).astype(BF)
    glm = nt(g, fu_ref[0]).astype(BF)
    acc_o[...] = jnp.zeros_like(acc_o)
    acc_n[...] = jnp.zeros_like(acc_n)
    acc_lm[...] = jnp.zeros_like(acc_lm)
    acc_li[...] = jnp.zeros_like(acc_li)

    @pl.when(s == 0)
    def _():
        for c_ in copies[2:]: c_.wait()

    def step(first, size):
        rows = pl.ds(first, size)
        nm = nm_ref[...]
        g = g_ref[0]
        w0, w1, wfc = wi[0, rows], wi[1, rows], wf[rows]
        iu0, iu1, mdc = iu[0, :, rows], iu[1, :, rows], md[:, rows]
        u = nt(nm, w0) + nn(low_in, iu0)
        v = nt(nm, w1) + nn(low_in, iu1)
        gh = nt(g, wfc) + nn(glm, mdc)
        cdf = 0.5 * (1.0 + lax.erf(u * (1.0 / math.sqrt(2.0))))
        pdf = jnp.exp(-0.5 * u * u) * (1.0 / math.sqrt(2.0 * math.pi))
        gel = u * cdf
        h = (gel * v).astype(BF)
        gu = (gh * v * (cdf + u * pdf)).astype(BF)
        gv = (gh * gel).astype(BF)
        acc_o[...] += nn(h, wfc)
        acc_n[...] += nn(gu, w0) + nn(gv, w1)
        acc_lm[...] += nt(h, mdc)
        acc_li[...] += nt(gu, iu0) + nt(gv, iu1)
        d_iu[0, :, rows] = tn(low_in, gu)
        d_iu[1, :, rows] = tn(low_in, gv)
        d_md[:, rows] = tn(glm, h)

    def loop(i, carry):
        step(pl.multiple_of(i * chunk, chunk), chunk)
        return carry
    lax.fori_loop(0, 2 * main // chunk, loop, 0)
    step(2 * main, 2 * tail)

    fu = fu_ref[0]
    low_mlp = acc_lm[...].astype(BF)
    out_ref[0] = (mid_ref[...] + acc_o[...] + nn(low_mlp, fu)).astype(BF)
    g = g_ref[0]
    d_w[0] = tn(low_mlp, g)
    gli = acc_li[...].astype(BF)
    d_w[1] = tn(gli, nm_ref[...])
    gnm = acc_n[...] + nn(gli, id_ref[0])
    c, rstd = norm_stats(mid_ref[...])
    gmid = g.astype(F32) + norm_back(gnm, c, rstd, gain)
    gmid_ref[0] = gmid
    ga = gmid.astype(BF)
    glo = nt(ga, ou).astype(BF)
    d_w[2] = tn(low_out, ga)
    gcm_ref[0] = (nt(ga, wo[0:half]) + nn(glo, odo)).astype(BF)
    gci_ref[0] = (nt(ga, wo[half:]) + nn(glo, odi)).astype(BF)

    sides = ((keep_ref, 0, at_ref[0], cm, F32), (send_ref, 1, 1 - at_ref[0], cr, BF))
    for ref, j, at, ctx, kind in sides:
        parts = (d_iu.at[0], d_iu.at[1], d_md)
        for i, d in enumerate(parts):
            ref[0, :, i * main:(i + 1) * main] = d[:, j * main:(j + 1) * main].astype(kind)
        o = 3 * main
        ref[0, :, o:o + half] = tn(glo, ctx).astype(kind)
        o += half
        for i in range(3):
            ref[0, :, o:o + half] = d_w[i, :, pl.ds(pl.multiple_of(at * half, half), half)].astype(kind)
            o += half
        lane = lax.broadcasted_iota(jnp.int32, (rank, 128 - 3 * tail), 1)
        tag = jnp.where((lane == ids[s]) & (j == 0), 1.0, 0.0)
        ends = [d[:, 2 * main + j * tail:2 * main + (j + 1) * tail] for d in parts]
        ref[0, :, o:] = jnp.concatenate(ends + [tag], 1).astype(kind)


def mlp_call(ids, at, x, cm, cr, g, gain, od_own, od_its, iu_own, iu_its, md_own, md_its, ou, idn, fu,
             wo_own, wo_its, wi_own, wi_its, wf_own, wf_its, chunk=512):
    S, R, D = x.shape
    half = wo_own.shape[0]
    ffh = wf_own.shape[0]
    main = ffh // 256 * 256
    tail = ffh - main
    rank = ou.shape[1]
    ff = 2 * ffh
    packed = 3 * main + 4 * half + 128
    seq = lambda *bs: pl.BlockSpec((1,) + bs, lambda s, *_: (s,) + (0,) * len(bs))
    tab = lambda *bs: pl.BlockSpec((1,) + bs, lambda s, ids, at: (ids[s],) + (0,) * len(bs))
    any_ = pl.BlockSpec(memory_space=pl.ANY)
    in_specs = [seq(R, D), seq(R, half), seq(R, half), seq(R, D), pl.BlockSpec((1, D), lambda s, *_: (0, 0)),
        tab(rank, half), tab(rank, half), tab(2, rank, ffh), tab(2, rank, ffh), tab(rank, ffh), tab(rank, ffh),
        tab(rank, D), tab(rank, D), tab(rank, D)] + [any_] * 6
    out_specs = [seq(R, D), seq(R, D), seq(R, half), seq(R, half), seq(rank, packed), seq(rank, packed)]
    sd = jax.ShapeDtypeStruct
    out_shape = [sd((S, R, D), BF), sd((S, R, D), F32), sd((S, R, half), BF), sd((S, R, half), BF),
        sd((S, rank, packed), F32), sd((S, rank, packed), BF)]
    scratch = [pltpu.VMEM((2 * half, D), BF), pltpu.VMEM((2, ff, D), BF), pltpu.VMEM((ff, D), BF),
        pltpu.VMEM((R, D), F32), pltpu.VMEM((R, D), F32), pltpu.VMEM((R, rank), F32), pltpu.VMEM((R, rank), F32),
        pltpu.VMEM((R, D), BF), pltpu.VMEM((R, D), F32), pltpu.VMEM((2, rank, ff), BF), pltpu.VMEM((rank, ff), BF),
        pltpu.VMEM((2, rank, ff), F32), pltpu.VMEM((rank, ff), F32), pltpu.VMEM((3, rank, D), F32), pltpu.SemaphoreType.DMA((14,))]
    return pl.pallas_call(functools.partial(mlp_kernel, chunk, main, tail),
        grid_spec=pltpu.PrefetchScalarGridSpec(num_scalar_prefetch=2, grid=(S,), in_specs=in_specs, out_specs=out_specs, scratch_shapes=scratch),
        out_shape=out_shape,
        compiler_params=pltpu.CompilerParams(dimension_semantics=("arbitrary",), vmem_limit_bytes=VMEM_LIMIT),
        cost_estimate=pl.CostEstimate(flops=40 * 10**9, bytes_accessed=40 * 10**6, transcendentals=3 * 10**6),
        name="mlp")(ids, at, x, cm, cr, g, gain, od_own, od_its, iu_own, iu_its, md_own, md_its, ou, idn, fu,
                    wo_own, wo_its, wi_own, wi_its, wf_own, wf_its)


LOG2E = 1.4426950408889634
QUERY_SCALE = LOG2E / 8.0

def lanes_of(head, shape):
    return (lax.broadcasted_iota(jnp.int32, shape, len(shape) - 1) // 64) == head

def column(row):
    return jnp.broadcast_to(row.astype(F32), (8, row.shape[1])).T[:, :1]

def swap(u):
    lane = lax.broadcasted_iota(jnp.int32, u.shape, 1)
    return jnp.where((lane & 63) < 32, pltpu.roll(u, 96, 1), pltpu.roll(u, 32, 1))


def qkv_kernel(ids, half_ref, x_ref, gain_ref, w_ref, ad_ref, up_ref, cos_ref, sin_ref, *rest):
    q_ref, k_ref, v_ref, low_ref, nm_ref = rest[-5:]
    c, rstd = norm_stats(x_ref[0].astype(F32))
    nm = (c * rstd * gain_ref[...].astype(F32)).astype(BF)
    nm_ref[0] = nm
    low = nt(nm, ad_ref[0]).astype(BF)
    low_ref[0] = low
    cos, sin = cos_ref[...], sin_ref[...]
    for b, ref in enumerate((q_ref, k_ref)):
        u = nn(nm, w_ref[b]) + nn(low, up_ref[0, b])
        if b == 0:
            u = u * QUERY_SCALE
        for p in range(u.shape[1] // 128):
            t = u[:, p * 128:(p + 1) * 128]
            ref[0, :, p * 128:(p + 1) * 128] = (t * cos + swap(t) * sin).astype(BF)
    v_ref[0] = (nn(nm, w_ref[2]) + nn(low, up_ref[0, 2])).astype(BF)

QKV_ROWS = 512


def qkv_call(ids, half_index, x, gain, w, ad, up, cos, sin, before=None, rows=None):
    S, R, D = x.shape
    W = w.shape[2]
    rank = ad.shape[1]
    L = cos.shape[0]
    rows = rows or QKV_ROWS
    n = R // rows
    tabl = lambda *bs: pl.BlockSpec((1,) + bs, lambda s, i, ids, h: (ids[s],) + (0,) * len(bs))
    turn = pl.BlockSpec((rows, 128), lambda s, i, ids, h: (h[0] * n + i, 0))
    in_specs = [pl.BlockSpec((1, rows, D), lambda s, i, ids, h: (s, i, 0)), pl.BlockSpec((1, D), lambda s, i, ids, h: (0, 0)),
        pl.BlockSpec((3, D, W), lambda s, i, ids, h: (0, 0, 0)), tabl(rank, D), tabl(3, rank, W), turn, turn]
    args = [ids, half_index, x, gain, w, ad, up, cos, sin]
    alias = {}
    if before is not None:
        for i, b in enumerate(before):
            alias[len(args)] = i
            args.append(b)
            in_specs.append(pl.BlockSpec(memory_space=pl.ANY))
    out = lambda m: pl.BlockSpec((1, rows, m), lambda s, i, ids, h: (s, h[0] * n + i, 0))
    sd = jax.ShapeDtypeStruct
    return pl.pallas_call(qkv_kernel,
        grid_spec=pltpu.PrefetchScalarGridSpec(num_scalar_prefetch=2, grid=(S, n), in_specs=in_specs,
            out_specs=[out(W), out(W), out(W), out(rank), out(D)]),
        out_shape=[sd((S, L, W), BF)] * 3 + [sd((S, L, rank), BF), sd((S, L, D), BF)],
        input_output_aliases=alias,
        compiler_params=pltpu.CompilerParams(dimension_semantics=("arbitrary", "arbitrary"), vmem_limit_bytes=VMEM_LIMIT),
        cost_estimate=pl.CostEstimate(flops=5 * 10**9, bytes_accessed=10**7, transcendentals=10**5),
        name="qkv")(*args)

def window(seg, s, i, rows, blk, count):
    first, last = seg[s, i * rows], seg[s, i * rows + rows - 1]
    lo = jnp.int32(0); hi = jnp.int32(0)
    for j in range(count):
        lo += (seg[s, j * blk + blk - 1] < first).astype(jnp.int32)
        hi += (seg[s, j * blk] <= last).astype(jnp.int32)
    return lo, hi - lo

def att_kernel(blk, seg, half_ref, q_ref, k_ref, v_ref, seg_ref, o_ref, lse_ref):
    s = pl.program_id(0)
    R, L = q_ref.shape[1], k_ref.shape[1]
    count = L // blk
    single = seg[s, 0] == seg[s, L - 1]

    def attend(r0, rows, k0, keys, masked):
        k = k_ref[0, pl.ds(k0, keys)]
        v = v_ref[0, pl.ds(k0, keys)]
        sub = min(rows, 256)
        units = [(h, b) for b in range(rows // sub) for h in range(2)]

        def scores(h, b):
            q = q_ref[0, pl.ds(r0 + b * sub, sub)]
            sc = nt(jnp.where(lanes_of(h, q.shape), q, jnp.zeros_like(q)), k)
            if masked:
                allowed = column(seg_ref[pl.ds(s, 1), pl.ds(half_ref[0] * R + r0 + b * sub, sub)]) == seg_ref[pl.ds(s, 1), pl.ds(k0, keys)].astype(F32)
                sc = jnp.where(allowed, sc, -1e30)
            return sc

        ahead = scores(*units[0])
        outs = []
        for i, (h, b) in enumerate(units):
            sc = ahead
            if i + 1 < len(units):
                ahead = scores(*units[i + 1])
            m = jnp.max(sc, axis=-1, keepdims=True)
            p = jnp.exp2(sc - m)
            l = jnp.sum(p, axis=-1, keepdims=True)
            outs.append(nn(p.astype(BF), v) * (1.0 / l))
            lse = jnp.broadcast_to(m + jnp.log2(l), (sub, 128))
            lse_ref[0, 0, pl.ds(h, 1), pl.ds(r0 + b * sub, sub)] = lse.T[0:1]
            if h == 1:
                o_ref[0, pl.ds(r0 + b * sub, sub)] = jnp.where(lanes_of(0, outs[0].shape), outs[0], outs[1]).astype(BF)
                outs = []

    @pl.when(single)
    def _():
        attend(0, R, 0, L, False)

    @pl.when(jnp.logical_not(single))
    def _():
        def sub(i, carry):
            lo, n = window(seg, s, half_ref[0] * (R // blk) + i, blk, blk, count)
            r0 = pl.multiple_of(i * blk, blk)
            k0 = pl.multiple_of(lo * blk, blk)
            for m in range(1, count + 1):
                @pl.when(n == m)
                def _():
                    attend(r0, blk, k0, m * blk, True)
            return carry
        lax.fori_loop(0, R // blk, sub, 0)

def att_call(seg, half_index, q, k, v, blk=256):
    S, L, W = q.shape
    R = L // 2
    P = W // 128
    sd = jax.ShapeDtypeStruct
    return pl.pallas_call(functools.partial(att_kernel, blk),
        grid_spec=pltpu.PrefetchScalarGridSpec(num_scalar_prefetch=2, grid=(S, P),
            in_specs=[pl.BlockSpec((1, R, 128), lambda s, p, seg, h: (s, h[0], p)),
                pl.BlockSpec((1, L, 128), lambda s, p, seg, h: (s, 0, p)), pl.BlockSpec((1, L, 128), lambda s, p, seg, h: (s, 0, p)),
                pl.BlockSpec((S, L), lambda s, p, seg, h: (0, 0))],
            out_specs=[pl.BlockSpec((1, R, 128), lambda s, p, seg, h: (s, 0, p)),
                pl.BlockSpec((1, 1, 2, R), lambda s, p, seg, h: (s, p, 0, 0))]),
        out_shape=[sd((S, R, W), BF), sd((S, P, 2, R), F32)],
        compiler_params=pltpu.CompilerParams(dimension_semantics=("arbitrary", "arbitrary"), vmem_limit_bytes=VMEM_LIMIT),
        cost_estimate=pl.CostEstimate(flops=8 * 10**9, bytes_accessed=8 * 10**6, transcendentals=8 * 10**6),
        name="attend")(seg, half_index, q, k, v, seg)

def back_kernel(blk, s, seg, half_ref, ids, q_ref, k_ref, v_ref, dom_ref, doo_ref, om_ref, oo_ref, lsem_ref, lseo_ref, seg_ref,
        cos_ref, sin_ref, low_ref, up_ref, nm_hbm, *rest):
    gpm_ref, gpo_ref, pay_ref, lgm_ref, lgo_ref, dq_acc, dk_acc, dv_acc, lg_acc, nm_ref, sem = rest[-11:]
    pair = pl.program_id(0)
    L = q_ref.shape[1]
    R = L // 2
    count = L // blk
    single = seg[s, 0] == seg[s, L - 1]
    mine = half_ref[0]
    dk_acc[...] = jnp.zeros_like(dk_acc)
    dv_acc[...] = jnp.zeros_like(dv_acc)
    fetch = pltpu.make_async_copy(nm_hbm.at[s], nm_ref, sem)

    @pl.when(pair == 0)
    def _():
        fetch.start()

    def part(do_ref, o_ref, lse_ref, n0, r0, rows, k0, keys, masked):
        q = q_ref[0, pl.ds(n0, rows)]
        do = do_ref[0, pl.ds(r0, rows)]
        o = o_ref[0, pl.ds(r0, rows)]
        k = k_ref[0, pl.ds(k0, keys)]
        v = v_ref[0, pl.ds(k0, keys)]
        prod = (do.astype(F32) * o.astype(F32)).T
        zero = jnp.zeros_like(q)
        if masked:
            allowed = column(seg_ref[s:s + 1, pl.ds(k0, keys)]) == seg_ref[s:s + 1, pl.ds(n0, rows)].astype(F32)
        ps, dss, dos, qs, ks = [], [], [], [], []
        for h in range(2):
            qh = jnp.where(lanes_of(h, q.shape), q, zero)
            doh = jnp.where(lanes_of(h, q.shape), do, zero)
            kh = jnp.where(lanes_of(h, k.shape), k, jnp.zeros_like(k))
            delta = jnp.sum(prod[h * 64:(h + 1) * 64], axis=0, keepdims=True)
            lse = lse_ref[0, 0, pl.ds(h, 1), pl.ds(r0, rows)]
            st = nt(k, qh)
            p = jnp.exp2(st - lse)
            if masked:
                p = jnp.where(allowed, p, 0.0)
            ds = p * (nt(v, doh) - delta)
            ps.append(p.astype(BF)); dss.append(ds.astype(BF)); dos.append(doh); qs.append(qh); ks.append(kh)
        dv_acc[pl.ds(k0, keys)] += nn(jnp.concatenate(ps, 1), jnp.concatenate(dos, 0))
        dk_acc[pl.ds(k0, keys)] += nn(jnp.concatenate(dss, 1), jnp.concatenate(qs, 0))
        dq_acc[pl.ds(n0, rows)] = tn(jnp.concatenate(dss, 0), jnp.concatenate(ks, 0))

    halves = ((dom_ref, om_ref, lsem_ref, mine), (doo_ref, oo_ref, lseo_ref, 1 - mine))

    @pl.when(single)
    def _():
        for do_ref, o_ref, lse_ref, h in halves:
            part(do_ref, o_ref, lse_ref, pl.multiple_of(h * R, R), 0, R, 0, L, False)

    @pl.when(jnp.logical_not(single))
    def _():
        for do_ref, o_ref, lse_ref, h in halves:
            lo, n = window(seg, s, h, R, blk, count)
            for m in (count - 1, count):
                @pl.when(n == m)
                def _():
                    part(do_ref, o_ref, lse_ref, pl.multiple_of(h * R, R), 0, R, pl.multiple_of(lo * blk, blk), m * blk, True)

            @pl.when(n < count - 1)
            def _():
                def sub(i, carry):
                    lo, n = window(seg, s, h * (R // blk) + i, blk, blk, count)
                    r0 = pl.multiple_of(i * blk, blk)
                    n0 = pl.multiple_of(h * R + i * blk, blk)
                    k0 = pl.multiple_of(lo * blk, blk)
                    for m in range(1, count - 1):
                        @pl.when(n == m)
                        def _():
                            part(do_ref, o_ref, lse_ref, n0, r0, blk, k0, m * blk, True)
                    return carry
                lax.fori_loop(0, R // blk, sub, 0)

    cos, sin = cos_ref[...], sin_ref[...]
    def unrotate(g, factor):
        g = g * factor
        return (g * cos - swap(g) * sin).astype(BF)
    W = gpm_ref.shape[3] * pl.num_programs(0)
    grads = (unrotate(dq_acc[...], 0.125), unrotate(dk_acc[...], 1.0 / LOG2E), dv_acc[...].astype(BF))
    for h in range(2):
        @pl.when(mine == h)
        def _():
            for b, g in enumerate(grads):
                gpm_ref[0, b] = g[h * R:(h + 1) * R]
                gpo_ref[0, b] = g[(1 - h) * R:(2 - h) * R]
    grads = jnp.concatenate(grads, 1)
    lgs = nt(grads, jnp.concatenate([up_ref[0, b] for b in range(3)], 1))
    ups = tn(low_ref[0], grads).astype(BF)
    for b in range(3):
        pay_ref[0, :, pl.ds(pl.multiple_of(b * W + pair * 128, 128), 128)] = ups[:, b * 128:(b + 1) * 128]

    @pl.when(pair == 0)
    def _():
        lg_acc[...] = lgs

    @pl.when(pair > 0)
    def _():
        lg_acc[...] += lgs

    @pl.when(pair == pl.num_programs(0) - 1)
    def _():
        fetch.wait()
        D = nm_ref.shape[1]
        o = pay_ref.shape[2] - 128 - D
        pay_ref[0, :, o:o + D] = tn(lg_acc[...].astype(BF), nm_ref[...]).astype(BF)
        lane = lax.broadcasted_iota(jnp.int32, (lg_acc.shape[1], 128), 1)
        pay_ref[0, :, o + D:] = jnp.where(lane == ids[s], 1.0, 0.0).astype(BF)
        lgm_ref[0] = lg_acc[pl.ds(pl.multiple_of(mine * R, R), R)]
        lgo_ref[0] = lg_acc[pl.ds(pl.multiple_of((1 - mine) * R, R), R)]

def back_call(s, seg, half_index, ids, q, k, v, dom, doo, om, oo, lsem, lseo, cos, sin, low, up, nm, before=None, blk=256):
    S, L, W = q.shape
    R = L // 2
    P = W // 128
    rank = low.shape[2]
    sd = jax.ShapeDtypeStruct
    full = pl.BlockSpec((1, L, 128), lambda p, *_: (s, 0, p))
    hlf = pl.BlockSpec((1, R, 128), lambda p, *_: (s, 0, p))
    ls = pl.BlockSpec((1, 1, 2, R), lambda p, *_: (s, p, 0, 0))
    tb = pl.BlockSpec((L, 128), lambda p, *_: (0, 0))
    gp = pl.BlockSpec((1, 3, R, 128), lambda p, *_: (0, 0, 0, p))
    lg = pl.BlockSpec((1, R, rank), lambda p, *_: (0, 0, 0))
    pay = 3 * W + nm.shape[2] + 128
    any_ = pl.BlockSpec(memory_space=pl.ANY)
    args = [seg, half_index, ids, q, k, v, dom, doo, om, oo, lsem, lseo, seg, cos, sin, low, up, nm]
    alias = {}
    if before is not None:
        alias[len(args)] = 2
        args.append(before)
    return pl.pallas_call(functools.partial(back_kernel, blk, s),
        grid_spec=pltpu.PrefetchScalarGridSpec(num_scalar_prefetch=3, grid=(P,),
            in_specs=[full, full, full, hlf, hlf, hlf, hlf, ls, ls, pl.BlockSpec((S, L), lambda p, *_: (0, 0)),
                tb, tb, pl.BlockSpec((1, L, rank), lambda p, *_: (s, 0, 0)),
                pl.BlockSpec((1, 3, rank, 128), lambda p, seg, h, ids: (ids[s], 0, 0, p)), any_] + [any_] * len(alias),
            out_specs=[gp, gp, pl.BlockSpec((1, rank, pay), lambda p, *_: (s, 0, 0)), lg, lg],
            scratch_shapes=[pltpu.VMEM((L, 128), F32)] * 3 + [pltpu.VMEM((L, rank), F32), pltpu.VMEM(nm.shape[1:], BF), pltpu.SemaphoreType.DMA]),
        out_shape=[sd((1, 3, R, W), BF), sd((1, 3, R, W), BF), sd((S, rank, pay), BF), sd((1, R, rank), F32), sd((1, R, rank), F32)],
        input_output_aliases=alias,
        compiler_params=pltpu.CompilerParams(dimension_semantics=("arbitrary",), vmem_limit_bytes=VMEM_LIMIT),
        cost_estimate=pl.CostEstimate(flops=18 * 10**9, bytes_accessed=10**7, transcendentals=8 * 10**6),
        name="attend_back")(*args)

def final_kernel(steps, ids, x_ref, gain_ref, wo_ref, wr_ref, ad_ref, mid_ref, gm0, gr0, lm0, lr0, gm1, gr1, lm1, lr1, out_ref):
    def run(gm, gr, lm, lr):
        gn = nn((lm[0] + lr[0]).astype(BF), ad_ref[0])
        for b in range(3):
            gn += nt(gm[0, b], wo_ref[b]) + nt(gr[0, b], wr_ref[b])
        c, rstd = norm_stats(x_ref[0].astype(F32))
        out_ref[0] = mid_ref[0] + norm_back(gn, c, rstd, gain_ref[...].astype(F32))

    @pl.when(pl.program_id(0) < steps)
    def _():
        run(gm0, gr0, lm0, lr0)

    @pl.when(pl.program_id(0) >= steps)
    def _():
        run(gm1, gr1, lm1, lr1)

def final_call(ids, x, gain, w_own, w_its, ad, mid, first, second, rows=256):
    S, R, D = x.shape
    W = w_own.shape[2]
    rank = ad.shape[1]
    n = R // rows
    wsp = pl.BlockSpec((3, D, W), lambda i, ids: (0, 0, 0))
    row = pl.BlockSpec((1, rows, D), lambda i, ids: (i // n, i % n, 0))
    at = (lambda i: jnp.minimum(i, n - 1)), (lambda i: jnp.maximum(i - n, 0))
    parts = []
    for f in at:
        gp = pl.BlockSpec((1, 3, rows, W), lambda i, ids, f=f: (0, 0, f(i), 0))
        lg = pl.BlockSpec((1, rows, rank), lambda i, ids, f=f: (0, f(i), 0))
        parts += [gp, gp, lg, lg]
    in_specs = [row, pl.BlockSpec((1, D), lambda i, ids: (0, 0)), wsp, wsp, pl.BlockSpec((1, rank, D), lambda i, ids: (ids[i // n], 0, 0)), row] + parts
    return pl.pallas_call(functools.partial(final_kernel, n),
        grid_spec=pltpu.PrefetchScalarGridSpec(num_scalar_prefetch=1, grid=(2 * n,), in_specs=in_specs, out_specs=row),
        out_shape=jax.ShapeDtypeStruct((S, R, D), F32),
        compiler_params=pltpu.CompilerParams(dimension_semantics=("arbitrary",), vmem_limit_bytes=VMEM_LIMIT),
        cost_estimate=pl.CostEstimate(flops=7 * 10**9, bytes_accessed=2 * 10**7, transcendentals=10**4),
        name="final")(ids, x, gain, w_own, w_its, ad, mid, *first, *second)

def unpack_kernel(in_ref, up_ref, down_ref):
    rank = in_ref.shape[0]
    W = up_ref.shape[3]
    for r in range(rank):
        for b in range(3):
            up_ref[:, b, r, :] = in_ref[r, :, b * W:(b + 1) * W].astype(F32)
        down_ref[:, r, :] = in_ref[r, :, 3 * W:].astype(F32)

def unpack_call(shares, W, D):
    rank, adapters, _ = shares.shape
    vm = pl.BlockSpec(memory_space=pltpu.VMEM)
    return pl.pallas_call(unpack_kernel, in_specs=[vm], out_specs=[vm, vm],
        out_shape=[jax.ShapeDtypeStruct((adapters, 3, rank, W), F32), jax.ShapeDtypeStruct((adapters, rank, D), F32)],
        compiler_params=pltpu.CompilerParams(vmem_limit_bytes=VMEM_LIMIT),
        cost_estimate=pl.CostEstimate(flops=10**6, bytes_accessed=2 * 10**6, transcendentals=0),
        name="unpack")(shares)


HEAD_DIM = 64
ROPE_BASE = 160000.0


def rotary_tables(length):
    inverse = 1.0 / ROPE_BASE ** (np.arange(0, HEAD_DIM, 2) / HEAD_DIM)
    angles = np.arange(length)[:, None] * inverse[None, :]
    cos, sin = np.cos(angles), np.sin(angles)
    return (
        jnp.asarray(np.concatenate([cos, cos, cos, cos], 1), F32),
        jnp.asarray(np.concatenate([-sin, sin, -sin, sin], 1), F32),
    )


def spread(packed, tag_at, tags, groups, shards):
    S, rank, m = packed.shape
    if shards != rank:
        flat = [packed[:, :, a:b].reshape(S, shards, -1) for a, b in groups]
        packed = jnp.concatenate(flat + [jnp.broadcast_to(packed[:, :1, tag_at:tag_at + tags], (S, shards, tags))], -1)
        tag_at = packed.shape[2] - tags
    got = lax.all_to_all(packed, "dp", 1, 1, tiled=True).reshape(S * shards, -1)
    sums = lax.dot_general(got[:, tag_at:tag_at + tags], got, (((0,), (0,)), ((), ())), preferred_element_type=F32)
    if shards != rank:
        return sums[:, :tag_at]
    return jnp.concatenate([sums[:, a:b] for a, b in groups], -1)


def collect(shares, shards):
    wide = jnp.broadcast_to(shares.astype(BF), (shards,) + shares.shape)
    return lax.all_to_all(wide, "dp", 0, 0, tiled=True)


def body(x, cotangent, norm_in, norm_mid, w_qkv, w_out, w_in, w_ff, qkv_down, qkv_up, out_down, out_up, in_down, in_up,
         mlp_down, ff_up, segs, ids):
    other = lambda a: lax.ppermute(a, "tensor", [(0, 1), (1, 0)])
    tie = lax.optimization_barrier
    t = lax.axis_index("tensor")
    shards = lax.axis_size("dp")
    mine, its = t.astype(jnp.int32).reshape(1), (1 - t).astype(jnp.int32).reshape(1)
    S, R, D = x.shape
    L = segs.shape[1]
    x_its = other(x)
    w_qkv = w_qkv.transpose(1, 0, 2)
    w_in = w_in.transpose(1, 2, 0)
    qkv_down, out_down, in_down, mlp_down = (a.transpose(0, 2, 1) for a in (qkv_down, out_down, in_down, mlp_down))
    qkv_up, in_up = qkv_up.transpose(0, 2, 1, 3), in_up.transpose(0, 2, 1, 3)
    gain_in, gain_mid = norm_in.reshape(1, D), norm_mid.reshape(1, D)
    half = w_out.shape[0]
    ffh = w_ff.shape[0]
    main = ffh // 256 * 256
    tail = ffh - main
    rank = out_up.shape[1]
    adapters = out_up.shape[0]

    w_out_its, w_in_its, w_ff_its, w_qkv_its = other(w_out), other(w_in), other(w_ff), other(w_qkv)
    out_down_its, in_up_its, mlp_down_its = other(out_down), other(in_up), other(mlp_down)

    cos, sin = rotary_tables(L)
    first = qkv_call(ids, mine, x, gain_in, w_qkv, qkv_down, qkv_up, cos, sin)
    q, k, v, low, normed = qkv_call(ids, its, x_its, gain_in, w_qkv, qkv_down, qkv_up, cos, sin, before=first)
    ctx_its, lse_its = att_call(segs, its, q, k, v)
    ctx_got = other(ctx_its)
    ctx_mine, lse_mine = att_call(segs, mine, q, k, v)
    output, grad_mid, gc_mine, gc_its, keep, send = mlp_call(
        ids, mine, x, ctx_mine, ctx_got, cotangent, gain_mid, out_down, out_down_its, in_up, in_up_its, mlp_down, mlp_down_its,
        out_up, in_down, ff_up, w_out, w_out_its, w_in, w_in_its, w_ff, w_ff_its)
    gc_got = other(gc_its)

    packed = (keep + other(send).astype(F32)).astype(BF)
    lanes = 3 * main + 4 * half
    shares = spread(packed, lanes + 3 * tail, adapters, ((0, lanes), (lanes, lanes + 3 * tail)), shards)

    back = lambda s, gc_got, before=None: back_call(
        s, segs, mine, ids, q, k, v, gc_mine, gc_got, ctx_mine, ctx_its, lse_mine, lse_its, cos, sin, low, qkv_up, normed, before)
    gp_mine0, gp_its0, packed, lg_mine0, lg_its0 = back(0, gc_got)
    gp_got0, lg_got0 = other(gp_its0), other(lg_its0)
    shares, packed = tie((shares, packed))
    sums = collect(shares, shards)
    gp_mine1, gp_its1, packed, lg_mine1, lg_its1 = back(1, gc_got, packed)
    sums, packed = tie((sums, packed))
    gp_got1, lg_got1 = other(gp_its1), other(lg_its1)
    m = packed.shape[2] - 128
    shares = spread(packed, m, adapters, ((0, m - D), (m - D, m)), shards)
    grad_input = final_call(ids, x, gain_in, w_qkv, w_qkv_its, qkv_down, grad_mid,
        (gp_mine0, gp_got0, lg_mine0, lg_got0), (gp_mine1, gp_got1, lg_mine1, lg_got1))
    shares, grad_input = tie((shares, grad_input))
    cut = rank * (m - D) // shards
    downs = shares[:, cut:]
    shares = jnp.concatenate([shares[:, :cut], downs + other(downs)], -1)
    shares, sums = tie((shares, sums))
    qsums = collect(shares, shards)

    whole = lambda a: a.transpose(1, 0, 2).reshape(adapters, rank, -1)
    a, b = whole(sums[..., :rank * lanes // shards]), whole(sums[..., rank * lanes // shards:])
    unit = lambda i: jnp.concatenate([a[..., i * main:(i + 1) * main], b[..., i * tail:(i + 1) * tail]], -1).astype(F32)
    g_in_up = jnp.stack([unit(0), unit(1)], 2)
    g_mlp_down = unit(2).transpose(0, 2, 1)
    g_out_down = a[..., 3 * main:3 * main + half].astype(F32).transpose(0, 2, 1)
    part = a[..., 3 * main + half:]
    part_its = other(part)
    lo, hi = jnp.where(t == 0, part, part_its), jnp.where(t == 0, part_its, part)
    g_ff_up, g_in_down, g_out_up = (
        jnp.concatenate([lo[..., i * half:(i + 1) * half], hi[..., i * half:(i + 1) * half]], -1).astype(F32) for i in range(3))
    if shards == rank:
        g_qkv_up, g_qkv_down = unpack_call(qsums, (m - D) // 3, D)
    else:
        g_qkv_up = whole(qsums[..., :cut]).astype(F32).reshape(adapters, rank, 3, -1).transpose(0, 2, 1, 3)
        g_qkv_down = whole(qsums[..., cut:]).astype(F32)
    g_qkv_up, g_qkv_down = g_qkv_up.transpose(0, 2, 1, 3), g_qkv_down.transpose(0, 2, 1)
    return (output, grad_input, g_qkv_down, g_qkv_up, g_out_down, g_out_up, g_in_down.transpose(0, 2, 1), g_in_up, g_mlp_down, g_ff_up)


def solution(mesh):
    return jax.shard_map(
        body,
        mesh=mesh,
        in_specs=(
            P("dp", "tensor", None),
            P("dp", "tensor", None),
            P(),
            P(),
            P(None, None, "tensor"),
            P("tensor", None),
            P(None, None, "tensor"),
            P("tensor", None),
            P(),
            P(None, None, None, "tensor"),
            P(None, "tensor", None),
            P(),
            P(),
            P(None, None, None, "tensor"),
            P(None, "tensor", None),
            P(),
            P("dp", None),
            P("dp"),
        ),
        out_specs=(
            P("dp", "tensor", None),
            P("dp", "tensor", None),
            P(),
            P(None, None, None, "tensor"),
            P(None, "tensor", None),
            P(),
            P(),
            P(None, None, None, "tensor"),
            P(None, "tensor", None),
            P(),
        ),
        check_vma=False,
    )
```

```python
import functools
import math

import jax
import jax.numpy as jnp
import numpy as np
from jax import lax
from jax.experimental import pallas as pl
from jax.experimental.pallas import tpu as pltpu
from jax.sharding import PartitionSpec as P

F32, BF = jnp.float32, jnp.bfloat16
EPS = 1e-05
VMEM_LIMIT = 62 * 1024 * 1024 - 2**20

def nn(a, b): return lax.dot_general(a, b, (((1,), (0,)), ((), ())), preferred_element_type=F32)
def nt(a, b): return lax.dot_general(a, b, (((1,), (1,)), ((), ())), preferred_element_type=F32)
def tn(a, b): return lax.dot_general(a, b, (((0,), (0,)), ((), ())), preferred_element_type=F32)

def norm_stats(v):
    mean = jnp.mean(v, axis=-1, keepdims=True)
    c = v - mean
    var = jnp.mean(c * c, axis=-1, keepdims=True)
    return c, lax.rsqrt(var + EPS)

def norm_back(e, c, rstd, gain):
    n = c * rstd
    h = e * gain
    return (h - jnp.mean(h, axis=-1, keepdims=True) - n * jnp.mean(h * n, axis=-1, keepdims=True)) * rstd

def mlp_kernel(chunk, main, tail,
        ids, at_ref, x_ref, cm_ref, cr_ref, g_ref, gain_ref,
        od_own, od_its, iu_own, iu_its, md_own, md_its, ou_ref, id_ref, fu_ref,
        wo_own, wo_its, wi_own, wi_its, wf_own, wf_its,
        out_ref, gmid_ref, gcm_ref, gci_ref, keep_ref, send_ref,
        wo, wi, wf, acc_o, acc_n, acc_lm, acc_li, nm_ref, mid_ref, iu, md, d_iu, d_md, d_w, sem):
    s = pl.program_id(0)
    half = wo_own.shape[0]
    rank = ou_ref.shape[1]
    copies = []
    def cp(src, dst):
        copies.append(pltpu.make_async_copy(src, dst, sem.at[len(copies)]))
    cp(wo_own, wo.at[pl.ds(0, half)])
    cp(wo_its, wo.at[pl.ds(half, half)])
    for j, (wi_h, wf_h) in enumerate(((wi_own, wf_own), (wi_its, wf_its))):
        for b in range(2):
            cp(wi_h.at[b, pl.ds(0, main)], wi.at[b, pl.ds(j * main, main)])
        cp(wf_h.at[pl.ds(0, main)], wf.at[pl.ds(j * main, main)])
        for b in range(2):
            cp(wi_h.at[b, pl.ds(main, tail)], wi.at[b, pl.ds(2 * main + j * tail, tail)])
        cp(wf_h.at[pl.ds(main, tail)], wf.at[pl.ds(2 * main + j * tail, tail)])

    @pl.when(s == 0)
    def _():
        for c in copies: c.start()
        for c in copies[:2]: c.wait()

    for dst, own, its in ((iu.at[0], iu_own[0, 0], iu_its[0, 0]), (iu.at[1], iu_own[0, 1], iu_its[0, 1]), (md, md_own[0], md_its[0])):
        dst[:, :main] = own[:, :main]
        dst[:, main:2 * main] = its[:, :main]
        dst[:, 2 * main:] = jnp.concatenate([own[:, main:].astype(F32), its[:, main:].astype(F32)], 1).astype(BF)

    cm, cr = cm_ref[0], cr_ref[0]
    odo, odi = od_own[0], od_its[0]
    ou = ou_ref[0]
    low_out = (nt(cm, odo) + nt(cr, odi)).astype(BF)
    att = nn(cm, wo[0:half]) + nn(cr, wo[half:]) + nn(low_out, ou)
    middle = x_ref[0].astype(F32) + att
    mid_ref[...] = middle
    c, rstd = norm_stats(middle)
    gain = gain_ref[...].astype(F32)
    nm = (c * rstd * gain).astype(BF)
    nm_ref[...] = nm
    g = g_ref[0]
    low_in = nt(nm, id_ref[0]).astype(BF)
    glm = nt(g, fu_ref[0]).astype(BF)
    acc_o[...] = jnp.zeros_like(acc_o)
    acc_n[...] = jnp.zeros_like(acc_n)
    acc_lm[...] = jnp.zeros_like(acc_lm)
    acc_li[...] = jnp.zeros_like(acc_li)

    @pl.when(s == 0)
    def _():
        for c_ in copies[2:]: c_.wait()

    def step(first, size):
        rows = pl.ds(first, size)
        nm = nm_ref[...]
        g = g_ref[0]
        w0, w1, wfc = wi[0, rows], wi[1, rows], wf[rows]
        iu0, iu1, mdc = iu[0, :, rows], iu[1, :, rows], md[:, rows]
        u = nt(nm, w0) + nn(low_in, iu0)
        v = nt(nm, w1) + nn(low_in, iu1)
        gh = nt(g, wfc) + nn(glm, mdc)
        cdf = 0.5 * (1.0 + lax.erf(u * (1.0 / math.sqrt(2.0))))
        pdf = jnp.exp(-0.5 * u * u) * (1.0 / math.sqrt(2.0 * math.pi))
        gel = u * cdf
        h = (gel * v).astype(BF)
        gu = (gh * v * (cdf + u * pdf)).astype(BF)
        gv = (gh * gel).astype(BF)
        acc_o[...] += nn(h, wfc)
        acc_n[...] += nn(gu, w0) + nn(gv, w1)
        acc_lm[...] += nt(h, mdc)
        acc_li[...] += nt(gu, iu0) + nt(gv, iu1)
        d_iu[0, :, rows] = tn(low_in, gu)
        d_iu[1, :, rows] = tn(low_in, gv)
        d_md[:, rows] = tn(glm, h)

    def loop(i, carry):
        step(pl.multiple_of(i * chunk, chunk), chunk)
        return carry
    lax.fori_loop(0, 2 * main // chunk, loop, 0)
    step(2 * main, 2 * tail)

    fu = fu_ref[0]
    low_mlp = acc_lm[...].astype(BF)
    out_ref[0] = (mid_ref[...] + acc_o[...] + nn(low_mlp, fu)).astype(BF)
    g = g_ref[0]
    d_w[0] = tn(low_mlp, g)
    gli = acc_li[...].astype(BF)
    d_w[1] = tn(gli, nm_ref[...])
    gnm = acc_n[...] + nn(gli, id_ref[0])
    c, rstd = norm_stats(mid_ref[...])
    gmid = g.astype(F32) + norm_back(gnm, c, rstd, gain)
    gmid_ref[0] = gmid
    ga = gmid.astype(BF)
    glo = nt(ga, ou).astype(BF)
    d_w[2] = tn(low_out, ga)
    gcm_ref[0] = (nt(ga, wo[0:half]) + nn(glo, odo)).astype(BF)
    gci_ref[0] = (nt(ga, wo[half:]) + nn(glo, odi)).astype(BF)

    sides = ((keep_ref, 0, at_ref[0], cm, F32), (send_ref, 1, 1 - at_ref[0], cr, BF))
    for ref, j, at, ctx, kind in sides:
        parts = (d_iu.at[0], d_iu.at[1], d_md)
        for i, d in enumerate(parts):
            ref[0, :, i * main:(i + 1) * main] = d[:, j * main:(j + 1) * main].astype(kind)
        o = 3 * main
        ref[0, :, o:o + half] = tn(glo, ctx).astype(kind)
        o += half
        for i in range(3):
            ref[0, :, o:o + half] = d_w[i, :, pl.ds(pl.multiple_of(at * half, half), half)].astype(kind)
            o += half
        lane = lax.broadcasted_iota(jnp.int32, (rank, 128 - 3 * tail), 1)
        tag = jnp.where((lane == ids[s]) & (j == 0), 1.0, 0.0)
        ends = [d[:, 2 * main + j * tail:2 * main + (j + 1) * tail] for d in parts]
        ref[0, :, o:] = jnp.concatenate(ends + [tag], 1).astype(kind)


def mlp_call(ids, at, x, cm, cr, g, gain, od_own, od_its, iu_own, iu_its, md_own, md_its, ou, idn, fu,
             wo_own, wo_its, wi_own, wi_its, wf_own, wf_its, chunk=512):
    S, R, D = x.shape
    half = wo_own.shape[0]
    ffh = wf_own.shape[0]
    main = ffh // 256 * 256
    tail = ffh - main
    rank = ou.shape[1]
    ff = 2 * ffh
    packed = 3 * main + 4 * half + 128
    seq = lambda *bs: pl.BlockSpec((1,) + bs, lambda s, *_: (s,) + (0,) * len(bs))
    tab = lambda *bs: pl.BlockSpec((1,) + bs, lambda s, ids, at: (ids[s],) + (0,) * len(bs))
    any_ = pl.BlockSpec(memory_space=pl.ANY)
    in_specs = [seq(R, D), seq(R, half), seq(R, half), seq(R, D), pl.BlockSpec((1, D), lambda s, *_: (0, 0)),
        tab(rank, half), tab(rank, half), tab(2, rank, ffh), tab(2, rank, ffh), tab(rank, ffh), tab(rank, ffh),
        tab(rank, D), tab(rank, D), tab(rank, D)] + [any_] * 6
    out_specs = [seq(R, D), seq(R, D), seq(R, half), seq(R, half), seq(rank, packed), seq(rank, packed)]
    sd = jax.ShapeDtypeStruct
    out_shape = [sd((S, R, D), BF), sd((S, R, D), F32), sd((S, R, half), BF), sd((S, R, half), BF),
        sd((S, rank, packed), F32), sd((S, rank, packed), BF)]
    scratch = [pltpu.VMEM((2 * half, D), BF), pltpu.VMEM((2, ff, D), BF), pltpu.VMEM((ff, D), BF),
        pltpu.VMEM((R, D), F32), pltpu.VMEM((R, D), F32), pltpu.VMEM((R, rank), F32), pltpu.VMEM((R, rank), F32),
        pltpu.VMEM((R, D), BF), pltpu.VMEM((R, D), F32), pltpu.VMEM((2, rank, ff), BF), pltpu.VMEM((rank, ff), BF),
        pltpu.VMEM((2, rank, ff), F32), pltpu.VMEM((rank, ff), F32), pltpu.VMEM((3, rank, D), F32), pltpu.SemaphoreType.DMA((14,))]
    return pl.pallas_call(functools.partial(mlp_kernel, chunk, main, tail),
        grid_spec=pltpu.PrefetchScalarGridSpec(num_scalar_prefetch=2, grid=(S,), in_specs=in_specs, out_specs=out_specs, scratch_shapes=scratch),
        out_shape=out_shape,
        compiler_params=pltpu.CompilerParams(dimension_semantics=("arbitrary",), vmem_limit_bytes=VMEM_LIMIT),
        cost_estimate=pl.CostEstimate(flops=40 * 10**9, bytes_accessed=40 * 10**6, transcendentals=3 * 10**6),
        name="mlp")(ids, at, x, cm, cr, g, gain, od_own, od_its, iu_own, iu_its, md_own, md_its, ou, idn, fu,
                    wo_own, wo_its, wi_own, wi_its, wf_own, wf_its)


LOG2E = 1.4426950408889634
QUERY_SCALE = LOG2E / 8.0

def lanes_of(head, shape):
    return (lax.broadcasted_iota(jnp.int32, shape, len(shape) - 1) // 64) == head

def column(row):
    return jnp.broadcast_to(row.astype(F32), (8, row.shape[1])).T[:, :1]

def swap(u):
    lane = lax.broadcasted_iota(jnp.int32, u.shape, 1)
    return jnp.where((lane & 63) < 32, pltpu.roll(u, 96, 1), pltpu.roll(u, 32, 1))


def qkv_kernel(ids, half_ref, x_ref, gain_ref, w_ref, ad_ref, up_ref, cos_ref, sin_ref, *rest):
    q_ref, k_ref, v_ref, low_ref, nm_ref = rest[-5:]
    c, rstd = norm_stats(x_ref[0].astype(F32))
    nm = (c * rstd * gain_ref[...].astype(F32)).astype(BF)
    nm_ref[0] = nm
    low = nt(nm, ad_ref[0]).astype(BF)
    low_ref[0] = low
    cos, sin = cos_ref[...], sin_ref[...]
    for b, ref in enumerate((q_ref, k_ref)):
        u = nn(nm, w_ref[b]) + nn(low, up_ref[0, b])
        if b == 0:
            u = u * QUERY_SCALE
        for p in range(u.shape[1] // 128):
            t = u[:, p * 128:(p + 1) * 128]
            ref[0, :, p * 128:(p + 1) * 128] = (t * cos + swap(t) * sin).astype(BF)
    v_ref[0] = (nn(nm, w_ref[2]) + nn(low, up_ref[0, 2])).astype(BF)

QKV_ROWS = 512


def qkv_call(ids, half_index, x, gain, w, ad, up, cos, sin, before=None, rows=None):
    S, R, D = x.shape
    W = w.shape[2]
    rank = ad.shape[1]
    L = cos.shape[0]
    rows = rows or QKV_ROWS
    n = R // rows
    tabl = lambda *bs: pl.BlockSpec((1,) + bs, lambda s, i, ids, h: (ids[s],) + (0,) * len(bs))
    turn = pl.BlockSpec((rows, 128), lambda s, i, ids, h: (h[0] * n + i, 0))
    in_specs = [pl.BlockSpec((1, rows, D), lambda s, i, ids, h: (s, i, 0)), pl.BlockSpec((1, D), lambda s, i, ids, h: (0, 0)),
        pl.BlockSpec((3, D, W), lambda s, i, ids, h: (0, 0, 0)), tabl(rank, D), tabl(3, rank, W), turn, turn]
    args = [ids, half_index, x, gain, w, ad, up, cos, sin]
    alias = {}
    if before is not None:
        for i, b in enumerate(before):
            alias[len(args)] = i
            args.append(b)
            in_specs.append(pl.BlockSpec(memory_space=pl.ANY))
    out = lambda m: pl.BlockSpec((1, rows, m), lambda s, i, ids, h: (s, h[0] * n + i, 0))
    sd = jax.ShapeDtypeStruct
    return pl.pallas_call(qkv_kernel,
        grid_spec=pltpu.PrefetchScalarGridSpec(num_scalar_prefetch=2, grid=(S, n), in_specs=in_specs,
            out_specs=[out(W), out(W), out(W), out(rank), out(D)]),
        out_shape=[sd((S, L, W), BF)] * 3 + [sd((S, L, rank), BF), sd((S, L, D), BF)],
        input_output_aliases=alias,
        compiler_params=pltpu.CompilerParams(dimension_semantics=("arbitrary", "arbitrary"), vmem_limit_bytes=VMEM_LIMIT),
        cost_estimate=pl.CostEstimate(flops=5 * 10**9, bytes_accessed=10**7, transcendentals=10**5),
        name="qkv")(*args)

def window(seg, s, i, rows, blk, count):
    first, last = seg[s, i * rows], seg[s, i * rows + rows - 1]
    lo = jnp.int32(0); hi = jnp.int32(0)
    for j in range(count):
        lo += (seg[s, j * blk + blk - 1] < first).astype(jnp.int32)
        hi += (seg[s, j * blk] <= last).astype(jnp.int32)
    return lo, hi - lo

def att_kernel(blk, seg, half_ref, q_ref, k_ref, v_ref, seg_ref, o_ref, lse_ref):
    s = pl.program_id(0)
    R, L = q_ref.shape[1], k_ref.shape[1]
    count = L // blk
    single = seg[s, 0] == seg[s, L - 1]

    def attend(r0, rows, k0, keys, masked):
        k = k_ref[0, pl.ds(k0, keys)]
        v = v_ref[0, pl.ds(k0, keys)]
        sub = min(rows, 256)
        units = [(h, b) for b in range(rows // sub) for h in range(2)]

        def scores(h, b):
            q = q_ref[0, pl.ds(r0 + b * sub, sub)]
            sc = nt(jnp.where(lanes_of(h, q.shape), q, jnp.zeros_like(q)), k)
            if masked:
                allowed = column(seg_ref[pl.ds(s, 1), pl.ds(half_ref[0] * R + r0 + b * sub, sub)]) == seg_ref[pl.ds(s, 1), pl.ds(k0, keys)].astype(F32)
                sc = jnp.where(allowed, sc, -1e30)
            return sc

        ahead = scores(*units[0])
        outs = []
        for i, (h, b) in enumerate(units):
            sc = ahead
            if i + 1 < len(units):
                ahead = scores(*units[i + 1])
            m = jnp.max(sc, axis=-1, keepdims=True)
            p = jnp.exp2(sc - m)
            l = jnp.sum(p, axis=-1, keepdims=True)
            outs.append(nn(p.astype(BF), v) * (1.0 / l))
            lse = jnp.broadcast_to(m + jnp.log2(l), (sub, 128))
            lse_ref[0, 0, pl.ds(h, 1), pl.ds(r0 + b * sub, sub)] = lse.T[0:1]
            if h == 1:
                o_ref[0, pl.ds(r0 + b * sub, sub)] = jnp.where(lanes_of(0, outs[0].shape), outs[0], outs[1]).astype(BF)
                outs = []

    @pl.when(single)
    def _():
        attend(0, R, 0, L, False)

    @pl.when(jnp.logical_not(single))
    def _():
        def sub(i, carry):
            lo, n = window(seg, s, half_ref[0] * (R // blk) + i, blk, blk, count)
            r0 = pl.multiple_of(i * blk, blk)
            k0 = pl.multiple_of(lo * blk, blk)
            for m in range(1, count + 1):
                @pl.when(n == m)
                def _():
                    attend(r0, blk, k0, m * blk, True)
            return carry
        lax.fori_loop(0, R // blk, sub, 0)

def att_call(seg, half_index, q, k, v, blk=256):
    S, L, W = q.shape
    R = L // 2
    P = W // 128
    sd = jax.ShapeDtypeStruct
    return pl.pallas_call(functools.partial(att_kernel, blk),
        grid_spec=pltpu.PrefetchScalarGridSpec(num_scalar_prefetch=2, grid=(S, P),
            in_specs=[pl.BlockSpec((1, R, 128), lambda s, p, seg, h: (s, h[0], p)),
                pl.BlockSpec((1, L, 128), lambda s, p, seg, h: (s, 0, p)), pl.BlockSpec((1, L, 128), lambda s, p, seg, h: (s, 0, p)),
                pl.BlockSpec((S, L), lambda s, p, seg, h: (0, 0))],
            out_specs=[pl.BlockSpec((1, R, 128), lambda s, p, seg, h: (s, 0, p)),
                pl.BlockSpec((1, 1, 2, R), lambda s, p, seg, h: (s, p, 0, 0))]),
        out_shape=[sd((S, R, W), BF), sd((S, P, 2, R), F32)],
        compiler_params=pltpu.CompilerParams(dimension_semantics=("arbitrary", "arbitrary"), vmem_limit_bytes=VMEM_LIMIT),
        cost_estimate=pl.CostEstimate(flops=8 * 10**9, bytes_accessed=8 * 10**6, transcendentals=8 * 10**6),
        name="attend")(seg, half_index, q, k, v, seg)

def back_kernel(blk, s, seg, half_ref, ids, q_ref, k_ref, v_ref, dom_ref, doo_ref, om_ref, oo_ref, lsem_ref, lseo_ref, seg_ref,
        cos_ref, sin_ref, low_ref, up_ref, nm_hbm, *rest):
    gpm_ref, gpo_ref, pay_ref, lgm_ref, lgo_ref, dq_acc, dk_acc, dv_acc, lg_acc, nm_ref, sem = rest[-11:]
    pair = pl.program_id(0)
    L = q_ref.shape[1]
    R = L // 2
    count = L // blk
    single = seg[s, 0] == seg[s, L - 1]
    mine = half_ref[0]
    dk_acc[...] = jnp.zeros_like(dk_acc)
    dv_acc[...] = jnp.zeros_like(dv_acc)
    fetch = pltpu.make_async_copy(nm_hbm.at[s], nm_ref, sem)

    @pl.when(pair == 0)
    def _():
        fetch.start()

    def part(do_ref, o_ref, lse_ref, n0, r0, rows, k0, keys, masked):
        q = q_ref[0, pl.ds(n0, rows)]
        do = do_ref[0, pl.ds(r0, rows)]
        o = o_ref[0, pl.ds(r0, rows)]
        k = k_ref[0, pl.ds(k0, keys)]
        v = v_ref[0, pl.ds(k0, keys)]
        prod = (do.astype(F32) * o.astype(F32)).T
        zero = jnp.zeros_like(q)
        if masked:
            allowed = column(seg_ref[s:s + 1, pl.ds(k0, keys)]) == seg_ref[s:s + 1, pl.ds(n0, rows)].astype(F32)
        ps, dss, dos, qs, ks = [], [], [], [], []
        for h in range(2):
            qh = jnp.where(lanes_of(h, q.shape), q, zero)
            doh = jnp.where(lanes_of(h, q.shape), do, zero)
            kh = jnp.where(lanes_of(h, k.shape), k, jnp.zeros_like(k))
            delta = jnp.sum(prod[h * 64:(h + 1) * 64], axis=0, keepdims=True)
            lse = lse_ref[0, 0, pl.ds(h, 1), pl.ds(r0, rows)]
            st = nt(k, qh)
            p = jnp.exp2(st - lse)
            if masked:
                p = jnp.where(allowed, p, 0.0)
            ds = p * (nt(v, doh) - delta)
            ps.append(p.astype(BF)); dss.append(ds.astype(BF)); dos.append(doh); qs.append(qh); ks.append(kh)
        dv_acc[pl.ds(k0, keys)] += nn(jnp.concatenate(ps, 1), jnp.concatenate(dos, 0))
        dk_acc[pl.ds(k0, keys)] += nn(jnp.concatenate(dss, 1), jnp.concatenate(qs, 0))
        dq_acc[pl.ds(n0, rows)] = tn(jnp.concatenate(dss, 0), jnp.concatenate(ks, 0))

    halves = ((dom_ref, om_ref, lsem_ref, mine), (doo_ref, oo_ref, lseo_ref, 1 - mine))

    @pl.when(single)
    def _():
        for do_ref, o_ref, lse_ref, h in halves:
            part(do_ref, o_ref, lse_ref, pl.multiple_of(h * R, R), 0, R, 0, L, False)

    @pl.when(jnp.logical_not(single))
    def _():
        for do_ref, o_ref, lse_ref, h in halves:
            lo, n = window(seg, s, h, R, blk, count)
            for m in (count - 1, count):
                @pl.when(n == m)
                def _():
                    part(do_ref, o_ref, lse_ref, pl.multiple_of(h * R, R), 0, R, pl.multiple_of(lo * blk, blk), m * blk, True)

            @pl.when(n < count - 1)
            def _():
                def sub(i, carry):
                    lo, n = window(seg, s, h * (R // blk) + i, blk, blk, count)
                    r0 = pl.multiple_of(i * blk, blk)
                    n0 = pl.multiple_of(h * R + i * blk, blk)
                    k0 = pl.multiple_of(lo * blk, blk)
                    for m in range(1, count - 1):
                        @pl.when(n == m)
                        def _():
                            part(do_ref, o_ref, lse_ref, n0, r0, blk, k0, m * blk, True)
                    return carry
                lax.fori_loop(0, R // blk, sub, 0)

    cos, sin = cos_ref[...], sin_ref[...]
    def unrotate(g, factor):
        g = g * factor
        return (g * cos - swap(g) * sin).astype(BF)
    W = gpm_ref.shape[3] * pl.num_programs(0)
    grads = (unrotate(dq_acc[...], 0.125), unrotate(dk_acc[...], 1.0 / LOG2E), dv_acc[...].astype(BF))
    for h in range(2):
        @pl.when(mine == h)
        def _():
            for b, g in enumerate(grads):
                gpm_ref[0, b] = g[h * R:(h + 1) * R]
                gpo_ref[0, b] = g[(1 - h) * R:(2 - h) * R]
    grads = jnp.concatenate(grads, 1)
    lgs = nt(grads, jnp.concatenate([up_ref[0, b] for b in range(3)], 1))
    ups = tn(low_ref[0], grads).astype(BF)
    for b in range(3):
        pay_ref[0, :, pl.ds(pl.multiple_of(b * W + pair * 128, 128), 128)] = ups[:, b * 128:(b + 1) * 128]

    @pl.when(pair == 0)
    def _():
        lg_acc[...] = lgs

    @pl.when(pair > 0)
    def _():
        lg_acc[...] += lgs

    @pl.when(pair == pl.num_programs(0) - 1)
    def _():
        fetch.wait()
        D = nm_ref.shape[1]
        o = pay_ref.shape[2] - 128 - D
        pay_ref[0, :, o:o + D] = tn(lg_acc[...].astype(BF), nm_ref[...]).astype(BF)
        lane = lax.broadcasted_iota(jnp.int32, (lg_acc.shape[1], 128), 1)
        pay_ref[0, :, o + D:] = jnp.where(lane == ids[s], 1.0, 0.0).astype(BF)
        lgm_ref[0] = lg_acc[pl.ds(pl.multiple_of(mine * R, R), R)]
        lgo_ref[0] = lg_acc[pl.ds(pl.multiple_of((1 - mine) * R, R), R)]

def back_call(s, seg, half_index, ids, q, k, v, dom, doo, om, oo, lsem, lseo, cos, sin, low, up, nm, before=None, blk=256):
    S, L, W = q.shape
    R = L // 2
    P = W // 128
    rank = low.shape[2]
    sd = jax.ShapeDtypeStruct
    full = pl.BlockSpec((1, L, 128), lambda p, *_: (s, 0, p))
    hlf = pl.BlockSpec((1, R, 128), lambda p, *_: (s, 0, p))
    ls = pl.BlockSpec((1, 1, 2, R), lambda p, *_: (s, p, 0, 0))
    tb = pl.BlockSpec((L, 128), lambda p, *_: (0, 0))
    gp = pl.BlockSpec((1, 3, R, 128), lambda p, *_: (0, 0, 0, p))
    lg = pl.BlockSpec((1, R, rank), lambda p, *_: (0, 0, 0))
    pay = 3 * W + nm.shape[2] + 128
    any_ = pl.BlockSpec(memory_space=pl.ANY)
    args = [seg, half_index, ids, q, k, v, dom, doo, om, oo, lsem, lseo, seg, cos, sin, low, up, nm]
    alias = {}
    if before is not None:
        alias[len(args)] = 2
        args.append(before)
    return pl.pallas_call(functools.partial(back_kernel, blk, s),
        grid_spec=pltpu.PrefetchScalarGridSpec(num_scalar_prefetch=3, grid=(P,),
            in_specs=[full, full, full, hlf, hlf, hlf, hlf, ls, ls, pl.BlockSpec((S, L), lambda p, *_: (0, 0)),
                tb, tb, pl.BlockSpec((1, L, rank), lambda p, *_: (s, 0, 0)),
                pl.BlockSpec((1, 3, rank, 128), lambda p, seg, h, ids: (ids[s], 0, 0, p)), any_] + [any_] * len(alias),
            out_specs=[gp, gp, pl.BlockSpec((1, rank, pay), lambda p, *_: (s, 0, 0)), lg, lg],
            scratch_shapes=[pltpu.VMEM((L, 128), F32)] * 3 + [pltpu.VMEM((L, rank), F32), pltpu.VMEM(nm.shape[1:], BF), pltpu.SemaphoreType.DMA]),
        out_shape=[sd((1, 3, R, W), BF), sd((1, 3, R, W), BF), sd((S, rank, pay), BF), sd((1, R, rank), F32), sd((1, R, rank), F32)],
        input_output_aliases=alias,
        compiler_params=pltpu.CompilerParams(dimension_semantics=("arbitrary",), vmem_limit_bytes=VMEM_LIMIT),
        cost_estimate=pl.CostEstimate(flops=18 * 10**9, bytes_accessed=10**7, transcendentals=8 * 10**6),
        name="attend_back")(*args)

def final_kernel(ids, x_ref, gain_ref, wo_ref, wr_ref, ad_ref, mid_ref, gm_ref, gr_ref, lm_ref, lr_ref, *rest):
    gn = nn((lm_ref[0] + lr_ref[0]).astype(BF), ad_ref[0])
    for b in range(3):
        gn += nt(gm_ref[0, b], wo_ref[b]) + nt(gr_ref[0, b], wr_ref[b])
    c, rstd = norm_stats(x_ref[0].astype(F32))
    rest[-1][0] = mid_ref[0] + norm_back(gn, c, rstd, gain_ref[...].astype(F32))

def final_call(s, ids, x, gain, w_own, w_its, ad, mid, parts, before=None, rows=256):
    S, R, D = x.shape
    W = w_own.shape[2]
    rank = ad.shape[1]
    wsp = pl.BlockSpec((3, D, W), lambda i, ids: (0, 0, 0))
    row = pl.BlockSpec((1, rows, D), lambda i, ids: (s, i, 0))
    gp = pl.BlockSpec((1, 3, rows, W), lambda i, ids: (0, 0, i, 0))
    lg = pl.BlockSpec((1, rows, rank), lambda i, ids: (0, i, 0))
    in_specs = [row, pl.BlockSpec((1, D), lambda i, ids: (0, 0)), wsp, wsp, pl.BlockSpec((1, rank, D), lambda i, ids: (ids[s], 0, 0)), row,
        gp, gp, lg, lg]
    args = [ids, x, gain, w_own, w_its, ad, mid, *parts]
    alias = {}
    if before is not None:
        alias[len(args)] = 0
        args.append(before)
        in_specs.append(pl.BlockSpec(memory_space=pl.ANY))
    return pl.pallas_call(final_kernel,
        grid_spec=pltpu.PrefetchScalarGridSpec(num_scalar_prefetch=1, grid=(R // rows,), in_specs=in_specs, out_specs=row),
        out_shape=jax.ShapeDtypeStruct((S, R, D), F32),
        input_output_aliases=alias,
        compiler_params=pltpu.CompilerParams(dimension_semantics=("arbitrary",), vmem_limit_bytes=VMEM_LIMIT),
        cost_estimate=pl.CostEstimate(flops=4 * 10**9, bytes_accessed=10**7, transcendentals=10**4),
        name="final")(*args)

def unpack_kernel(in_ref, up_ref, down_ref):
    rank = in_ref.shape[0]
    W = up_ref.shape[3]
    for r in range(rank):
        for b in range(3):
            up_ref[:, b, r, :] = in_ref[r, :, b * W:(b + 1) * W].astype(F32)
        down_ref[:, r, :] = in_ref[r, :, 3 * W:].astype(F32)

def unpack_call(shares, W, D):
    rank, adapters, _ = shares.shape
    vm = pl.BlockSpec(memory_space=pltpu.VMEM)
    return pl.pallas_call(unpack_kernel, in_specs=[vm], out_specs=[vm, vm],
        out_shape=[jax.ShapeDtypeStruct((adapters, 3, rank, W), F32), jax.ShapeDtypeStruct((adapters, rank, D), F32)],
        compiler_params=pltpu.CompilerParams(vmem_limit_bytes=VMEM_LIMIT),
        cost_estimate=pl.CostEstimate(flops=10**6, bytes_accessed=2 * 10**6, transcendentals=0),
        name="unpack")(shares)


def unpack_units_kernel(at_ref, in_ref, iu_ref, md_ref, od_ref, *tables):
    rank = in_ref.shape[0]
    half = od_ref.shape[2]
    ffh = md_ref.shape[2]
    main = ffh // 256 * 256
    tail = ffh - main
    own_first = at_ref[0] == 0
    for r in range(rank):
        row = lambda a, n: in_ref[r, :, a:a + n].astype(F32)
        o = 3 * main + half
        ends = row(o + 6 * half, 3 * tail)
        for i in range(3):
            unit = jnp.concatenate([row(i * main, main), ends[:, i * tail:(i + 1) * tail]], 1)
            if i < 2:
                iu_ref[:, r, i, :] = unit
            else:
                md_ref[:, r, :] = unit
        od_ref[:, r, :] = row(3 * main, half)
        for i, ref in enumerate(tables):
            own, got = row(o + i * half, half), row(o + (3 + i) * half, half)
            ref[:, r, :half] = jnp.where(own_first, own, got)
            ref[:, r, half:] = jnp.where(own_first, got, own)

def unpack_units_call(at, shares, half, ffh):
    rank, adapters, _ = shares.shape
    vm = pl.BlockSpec(memory_space=pltpu.VMEM)
    sd = lambda *sh: jax.ShapeDtypeStruct((adapters, rank) + sh, F32)
    return pl.pallas_call(unpack_units_kernel, in_specs=[pl.BlockSpec(memory_space=pltpu.SMEM), vm], out_specs=[vm] * 6,
        out_shape=[sd(2, ffh), sd(ffh), sd(half)] + [sd(2 * half)] * 3,
        compiler_params=pltpu.CompilerParams(vmem_limit_bytes=VMEM_LIMIT),
        cost_estimate=pl.CostEstimate(flops=10**6, bytes_accessed=6 * 10**6, transcendentals=0),
        name="unpack_units")(at, shares)


HEAD_DIM = 64
ROPE_BASE = 160000.0


def rotary_tables(length):
    inverse = 1.0 / ROPE_BASE ** (np.arange(0, HEAD_DIM, 2) / HEAD_DIM)
    angles = np.arange(length)[:, None] * inverse[None, :]
    cos, sin = np.cos(angles), np.sin(angles)
    return (
        jnp.asarray(np.concatenate([cos, cos, cos, cos], 1), F32),
        jnp.asarray(np.concatenate([-sin, sin, -sin, sin], 1), F32),
    )


def spread(packed, tag_at, tags, groups, shards):
    S, rank, m = packed.shape
    if shards != rank:
        flat = [packed[:, :, a:b].reshape(S, shards, -1) for a, b in groups]
        packed = jnp.concatenate(flat + [jnp.broadcast_to(packed[:, :1, tag_at:tag_at + tags], (S, shards, tags))], -1)
        tag_at = packed.shape[2] - tags
    got = lax.all_to_all(packed, "dp", 1, 1, tiled=True).reshape(S * shards, -1)
    sums = lax.dot_general(got[:, tag_at:tag_at + tags], got, (((0,), (0,)), ((), ())), preferred_element_type=F32)
    if shards != rank:
        return sums[:, :tag_at]
    return jnp.concatenate([sums[:, a:b] for a, b in groups], -1)


def collect(shares, shards):
    wide = jnp.broadcast_to(shares.astype(BF), (shards,) + shares.shape)
    return lax.all_to_all(wide, "dp", 0, 0, tiled=True)


def body(x, cotangent, norm_in, norm_mid, w_qkv, w_out, w_in, w_ff, qkv_down, qkv_up, out_down, out_up, in_down, in_up,
         mlp_down, ff_up, segs, ids):
    other = lambda a: lax.ppermute(a, "tensor", [(0, 1), (1, 0)])
    tie = lax.optimization_barrier
    t = lax.axis_index("tensor")
    shards = lax.axis_size("dp")
    mine, its = t.astype(jnp.int32).reshape(1), (1 - t).astype(jnp.int32).reshape(1)
    S, R, D = x.shape
    L = segs.shape[1]
    x_its = other(x)
    w_qkv = w_qkv.transpose(1, 0, 2)
    w_in = w_in.transpose(1, 2, 0)
    qkv_down, out_down, in_down, mlp_down = (a.transpose(0, 2, 1) for a in (qkv_down, out_down, in_down, mlp_down))
    qkv_up, in_up = qkv_up.transpose(0, 2, 1, 3), in_up.transpose(0, 2, 1, 3)
    gain_in, gain_mid = norm_in.reshape(1, D), norm_mid.reshape(1, D)
    half = w_out.shape[0]
    ffh = w_ff.shape[0]
    main = ffh // 256 * 256
    tail = ffh - main
    rank = out_up.shape[1]
    adapters = out_up.shape[0]

    w_out_its, w_in_its, w_ff_its, w_qkv_its = other(w_out), other(w_in), other(w_ff), other(w_qkv)
    out_down_its, in_up_its, mlp_down_its = other(out_down), other(in_up), other(mlp_down)

    cos, sin = rotary_tables(L)
    first = qkv_call(ids, mine, x, gain_in, w_qkv, qkv_down, qkv_up, cos, sin)
    q, k, v, low, normed = qkv_call(ids, its, x_its, gain_in, w_qkv, qkv_down, qkv_up, cos, sin, before=first)
    ctx_its, lse_its = att_call(segs, its, q, k, v)
    ctx_got = other(ctx_its)
    ctx_mine, lse_mine = att_call(segs, mine, q, k, v)
    output, grad_mid, gc_mine, gc_its, keep, send = mlp_call(
        ids, mine, x, ctx_mine, ctx_got, cotangent, gain_mid, out_down, out_down_its, in_up, in_up_its, mlp_down, mlp_down_its,
        out_up, in_down, ff_up, w_out, w_out_its, w_in, w_in_its, w_ff, w_ff_its)
    gc_got = other(gc_its)

    packed = (keep + other(send).astype(F32)).astype(BF)
    lanes = 3 * main + 4 * half
    units = lanes - 3 * half
    shares = spread(packed, lanes + 3 * tail, adapters, ((0, units), (units, lanes), (lanes, lanes + 3 * tail)), shards)

    back = lambda s, gc_got, before=None: back_call(
        s, segs, mine, ids, q, k, v, gc_mine, gc_got, ctx_mine, ctx_its, lse_mine, lse_its, cos, sin, low, qkv_up, normed, before)
    gp_mine0, gp_its0, packed, lg_mine0, lg_its0 = back(0, gc_got)
    gp_got0, lg_got0 = other(gp_its0), other(lg_its0)
    shares, packed = tie((shares.astype(BF), packed))
    c0, c1 = rank * units // shards, rank * lanes // shards
    halves = shares[:, c0:c1]
    sums = collect(jnp.concatenate([shares[:, :c1], other(halves), shares[:, c1:]], -1), shards)
    gp_mine1, gp_its1, packed, lg_mine1, lg_its1 = back(1, gc_got, packed)
    sums, packed = tie((sums, packed))
    gp_got1, lg_got1 = other(gp_its1), other(lg_its1)
    m = packed.shape[2] - 128
    shares = spread(packed, m, adapters, ((0, m - D), (m - D, m)), shards)
    grad_input = final_call(0, ids, x, gain_in, w_qkv, w_qkv_its, qkv_down, grad_mid, (gp_mine0, gp_got0, lg_mine0, lg_got0))
    shares, grad_input = tie((shares, grad_input))
    cut = rank * (m - D) // shards
    downs = shares[:, cut:]
    shares = jnp.concatenate([shares[:, :cut], downs + other(downs)], -1)
    shares, sums, gp_got1 = tie((shares, sums, gp_got1))
    qsums = collect(shares, shards)
    grad_input = final_call(1, ids, x, gain_in, w_qkv, w_qkv_its, qkv_down, grad_mid, (gp_mine1, gp_got1, lg_mine1, lg_got1), grad_input)

    whole = lambda a: a.transpose(1, 0, 2).reshape(adapters, rank, -1)
    if shards == rank:
        g_in_up, g_mlp_down, g_out_down, g_ff_up, g_in_down, g_out_up = unpack_units_call(mine, sums, half, ffh)
    else:
        a, own, got, b = (whole(z) for z in jnp.split(sums, (c0, c1, 2 * c1 - c0), axis=2))
        unit = lambda i: jnp.concatenate([a[..., i * main:(i + 1) * main], b[..., i * tail:(i + 1) * tail]], -1).astype(F32)
        g_in_up, g_mlp_down = jnp.stack([unit(0), unit(1)], 2), unit(2)
        g_out_down = a[..., 3 * main:].astype(F32)
        lo, hi = jnp.where(t == 0, own, got), jnp.where(t == 0, got, own)
        g_ff_up, g_in_down, g_out_up = (
            jnp.concatenate([lo[..., i * half:(i + 1) * half], hi[..., i * half:(i + 1) * half]], -1).astype(F32) for i in range(3))
    g_mlp_down, g_out_down = g_mlp_down.transpose(0, 2, 1), g_out_down.transpose(0, 2, 1)
    if shards == rank:
        g_qkv_up, g_qkv_down = unpack_call(qsums, (m - D) // 3, D)
    else:
        g_qkv_up = whole(qsums[..., :cut]).astype(F32).reshape(adapters, rank, 3, -1).transpose(0, 2, 1, 3)
        g_qkv_down = whole(qsums[..., cut:]).astype(F32)
    g_qkv_up, g_qkv_down = g_qkv_up.transpose(0, 2, 1, 3), g_qkv_down.transpose(0, 2, 1)
    return (output, grad_input, g_qkv_down, g_qkv_up, g_out_down, g_out_up, g_in_down.transpose(0, 2, 1), g_in_up, g_mlp_down, g_ff_up)


def solution(mesh):
    return jax.shard_map(
        body,
        mesh=mesh,
        in_specs=(
            P("dp", "tensor", None),
            P("dp", "tensor", None),
            P(),
            P(),
            P(None, None, "tensor"),
            P("tensor", None),
            P(None, None, "tensor"),
            P("tensor", None),
            P(),
            P(None, None, None, "tensor"),
            P(None, "tensor", None),
            P(),
            P(),
            P(None, None, None, "tensor"),
            P(None, "tensor", None),
            P(),
            P("dp", None),
            P("dp"),
        ),
        out_specs=(
            P("dp", "tensor", None),
            P("dp", "tensor", None),
            P(),
            P(None, None, None, "tensor"),
            P(None, "tensor", None),
            P(),
            P(),
            P(None, None, None, "tensor"),
            P(None, "tensor", None),
            P(),
        ),
        check_vma=False,
    )
```

```python
import functools
import math

import jax
import jax.numpy as jnp
import numpy as np
from jax import lax
from jax.experimental import pallas as pl
from jax.experimental.pallas import tpu as pltpu
from jax.sharding import PartitionSpec as P

F32, BF = jnp.float32, jnp.bfloat16
EPS = 1e-05
VMEM_LIMIT = 65280 * 1024

def nn(a, b): return lax.dot_general(a, b, (((1,), (0,)), ((), ())), preferred_element_type=F32)
def nt(a, b): return lax.dot_general(a, b, (((1,), (1,)), ((), ())), preferred_element_type=F32)
def tn(a, b): return lax.dot_general(a, b, (((0,), (0,)), ((), ())), preferred_element_type=F32)

def norm_stats(v):
    mean = jnp.mean(v, axis=-1, keepdims=True)
    c = v - mean
    var = jnp.mean(c * c, axis=-1, keepdims=True)
    return c, lax.rsqrt(var + EPS)

def norm_back(e, c, rstd, gain):
    n = c * rstd
    h = e * gain
    return (h - jnp.mean(h, axis=-1, keepdims=True) - n * jnp.mean(h * n, axis=-1, keepdims=True)) * rstd

def mlp_kernel(chunk, main, tail,
        ids, at_ref, x_ref, cm_ref, cr_ref, g_ref, gain_ref,
        od_own, od_its, iu_own, iu_its, md_own, md_its, ou_ref, id_ref, fu_ref,
        wo_own, wo_its, wi_own, wi_its, wf_own, wf_its,
        out_ref, gmid_ref, gcm_ref, gci_ref, keep_ref, send_ref,
        wo, wi, wf, acc_o, acc_n, acc_lm, acc_li, nm_ref, mid_ref, iu, md, d_iu, d_md, d_w, sem):
    s = pl.program_id(0)
    half = wo_own.shape[0]
    rank = ou_ref.shape[1]
    copies = []
    def cp(src, dst):
        copies.append(pltpu.make_async_copy(src, dst, sem.at[len(copies)]))
    cp(wo_own, wo.at[pl.ds(0, half)])
    cp(wo_its, wo.at[pl.ds(half, half)])
    for j, (wi_h, wf_h) in enumerate(((wi_own, wf_own), (wi_its, wf_its))):
        for b in range(2):
            cp(wi_h.at[b, pl.ds(0, main)], wi.at[b, pl.ds(j * main, main)])
        cp(wf_h.at[pl.ds(0, main)], wf.at[pl.ds(j * main, main)])
        for b in range(2):
            cp(wi_h.at[b, pl.ds(main, tail)], wi.at[b, pl.ds(2 * main + j * tail, tail)])
        cp(wf_h.at[pl.ds(main, tail)], wf.at[pl.ds(2 * main + j * tail, tail)])

    @pl.when(s == 0)
    def _():
        for c in copies: c.start()
        for c in copies[:2]: c.wait()

    for dst, own, its in ((iu.at[0], iu_own[0, 0], iu_its[0, 0]), (iu.at[1], iu_own[0, 1], iu_its[0, 1]), (md, md_own[0], md_its[0])):
        dst[:, :main] = own[:, :main]
        dst[:, main:2 * main] = its[:, :main]
        dst[:, 2 * main:] = jnp.concatenate([own[:, main:].astype(F32), its[:, main:].astype(F32)], 1).astype(BF)

    cm, cr = cm_ref[0], cr_ref[0]
    odo, odi = od_own[0], od_its[0]
    ou = ou_ref[0]
    low_out = (nt(cm, odo) + nt(cr, odi)).astype(BF)
    att = nn(cm, wo[0:half]) + nn(cr, wo[half:]) + nn(low_out, ou)
    middle = x_ref[0].astype(F32) + att
    mid_ref[...] = middle
    c, rstd = norm_stats(middle)
    gain = gain_ref[...].astype(F32)[None, :]
    nm = (c * rstd * gain).astype(BF)
    nm_ref[...] = nm
    g = g_ref[0]
    low_in = nt(nm, id_ref[0]).astype(BF)
    glm = nt(g, fu_ref[0]).astype(BF)
    acc_o[...] = jnp.zeros_like(acc_o)
    acc_n[...] = jnp.zeros_like(acc_n)
    acc_lm[...] = jnp.zeros_like(acc_lm)
    acc_li[...] = jnp.zeros_like(acc_li)

    @pl.when(s == 0)
    def _():
        for c_ in copies[2:]: c_.wait()

    def step(first, size):
        rows = pl.ds(first, size)
        nm = nm_ref[...]
        g = g_ref[0]
        w0, w1, wfc = wi[0, rows], wi[1, rows], wf[rows]
        iu0, iu1, mdc = iu[0, :, rows], iu[1, :, rows], md[:, rows]
        u = nt(nm, w0) + nn(low_in, iu0)
        v = nt(nm, w1) + nn(low_in, iu1)
        gh = nt(g, wfc) + nn(glm, mdc)
        cdf = 0.5 * (1.0 + lax.erf(u * (1.0 / math.sqrt(2.0))))
        pdf = jnp.exp(-0.5 * u * u) * (1.0 / math.sqrt(2.0 * math.pi))
        gel = u * cdf
        h = (gel * v).astype(BF)
        gu = (gh * v * (cdf + u * pdf)).astype(BF)
        gv = (gh * gel).astype(BF)
        acc_o[...] += nn(h, wfc)
        acc_n[...] += nn(gu, w0) + nn(gv, w1)
        acc_lm[...] += nt(h, mdc)
        acc_li[...] += nt(gu, iu0) + nt(gv, iu1)
        d_iu[0, :, rows] = tn(low_in, gu)
        d_iu[1, :, rows] = tn(low_in, gv)
        d_md[:, rows] = tn(glm, h)

    def loop(i, carry):
        step(pl.multiple_of(i * chunk, chunk), chunk)
        return carry
    lax.fori_loop(0, 2 * main // chunk, loop, 0)
    step(2 * main, 2 * tail)

    fu = fu_ref[0]
    low_mlp = acc_lm[...].astype(BF)
    out_ref[0] = (mid_ref[...] + acc_o[...] + nn(low_mlp, fu)).astype(BF)
    g = g_ref[0]
    d_w[0] = tn(low_mlp, g)
    gli = acc_li[...].astype(BF)
    d_w[1] = tn(gli, nm_ref[...])
    gnm = acc_n[...] + nn(gli, id_ref[0])
    c, rstd = norm_stats(mid_ref[...])
    gmid = g.astype(F32) + norm_back(gnm, c, rstd, gain)
    gmid_ref[0] = gmid
    ga = gmid.astype(BF)
    glo = nt(ga, ou).astype(BF)
    d_w[2] = tn(low_out, ga)
    gcm_ref[0] = (nt(ga, wo[0:half]) + nn(glo, odo)).astype(BF)
    gci_ref[0] = (nt(ga, wo[half:]) + nn(glo, odi)).astype(BF)

    sides = ((keep_ref, 0, at_ref[0], cm, F32), (send_ref, 1, 1 - at_ref[0], cr, BF))
    for ref, j, at, ctx, kind in sides:
        parts = (d_iu.at[0], d_iu.at[1], d_md)
        for i, d in enumerate(parts):
            ref[0, :, i * main:(i + 1) * main] = d[:, j * main:(j + 1) * main].astype(kind)
        o = 3 * main
        ref[0, :, o:o + half] = tn(glo, ctx).astype(kind)
        o += half
        for i in range(3):
            ref[0, :, o:o + half] = d_w[i, :, pl.ds(pl.multiple_of(at * half, half), half)].astype(kind)
            o += half
        lane = lax.broadcasted_iota(jnp.int32, (rank, 128 - 3 * tail), 1)
        tag = jnp.where((lane == ids[s]) & (j == 0), 1.0, 0.0)
        ends = [d[:, 2 * main + j * tail:2 * main + (j + 1) * tail] for d in parts]
        ref[0, :, o:] = jnp.concatenate(ends + [tag], 1).astype(kind)


def mlp_call(ids, at, x, cm, cr, g, gain, od_own, od_its, iu_own, iu_its, md_own, md_its, ou, idn, fu,
             wo_own, wo_its, wi_own, wi_its, wf_own, wf_its, chunk=512):
    S, R, D = x.shape
    half = wo_own.shape[0]
    ffh = wf_own.shape[0]
    main = ffh // 256 * 256
    tail = ffh - main
    rank = ou.shape[1]
    ff = 2 * ffh
    packed = 3 * main + 4 * half + 128
    seq = lambda *bs: pl.BlockSpec((1,) + bs, lambda s, *_: (s,) + (0,) * len(bs))
    tab = lambda *bs: pl.BlockSpec((1,) + bs, lambda s, ids, at: (ids[s],) + (0,) * len(bs))
    any_ = pl.BlockSpec(memory_space=pl.ANY)
    in_specs = [seq(R, D), seq(R, half), seq(R, half), seq(R, D), pl.BlockSpec((D,), lambda s, *_: (0,)),
        tab(rank, half), tab(rank, half), tab(2, rank, ffh), tab(2, rank, ffh), tab(rank, ffh), tab(rank, ffh),
        tab(rank, D), tab(rank, D), tab(rank, D)] + [any_] * 6
    out_specs = [seq(R, D), seq(R, D), seq(R, half), seq(R, half), seq(rank, packed), seq(rank, packed)]
    sd = jax.ShapeDtypeStruct
    out_shape = [sd((S, R, D), BF), sd((S, R, D), F32), sd((S, R, half), BF), sd((S, R, half), BF),
        sd((S, rank, packed), F32), sd((S, rank, packed), BF)]
    scratch = [pltpu.VMEM((2 * half, D), BF), pltpu.VMEM((2, ff, D), BF), pltpu.VMEM((ff, D), BF),
        pltpu.VMEM((R, D), F32), pltpu.VMEM((R, D), F32), pltpu.VMEM((R, rank), F32), pltpu.VMEM((R, rank), F32),
        pltpu.VMEM((R, D), BF), pltpu.VMEM((R, D), F32), pltpu.VMEM((2, rank, ff), BF), pltpu.VMEM((rank, ff), BF),
        pltpu.VMEM((2, rank, ff), F32), pltpu.VMEM((rank, ff), F32), pltpu.VMEM((3, rank, D), F32), pltpu.SemaphoreType.DMA((14,))]
    return pl.pallas_call(functools.partial(mlp_kernel, chunk, main, tail),
        grid_spec=pltpu.PrefetchScalarGridSpec(num_scalar_prefetch=2, grid=(S,), in_specs=in_specs, out_specs=out_specs, scratch_shapes=scratch),
        out_shape=out_shape,
        compiler_params=pltpu.CompilerParams(dimension_semantics=("arbitrary",), vmem_limit_bytes=VMEM_LIMIT),
        cost_estimate=pl.CostEstimate(flops=40 * 10**9, bytes_accessed=40 * 10**6, transcendentals=3 * 10**6),
        name="mlp")(ids, at, x, cm, cr, g, gain, od_own, od_its, iu_own, iu_its, md_own, md_its, ou, idn, fu,
                    wo_own, wo_its, wi_own, wi_its, wf_own, wf_its)


LOG2E = 1.4426950408889634
QUERY_SCALE = LOG2E / 8.0

def lanes_of(head, shape):
    return (lax.broadcasted_iota(jnp.int32, shape, len(shape) - 1) // 64) == head

def column(row):
    return jnp.broadcast_to(row.astype(F32), (8, row.shape[1])).T[:, :1]

def swap(u):
    lane = lax.broadcasted_iota(jnp.int32, u.shape, 1)
    return jnp.where((lane & 63) < 32, pltpu.roll(u, 96, 1), pltpu.roll(u, 32, 1))


def qkv_kernel(ids, half_ref, x_ref, gain_ref, w_ref, ad_ref, up_ref, cos_ref, sin_ref, *rest):
    q_ref, k_ref, v_ref, low_ref, nm_ref = rest[-5:]
    c, rstd = norm_stats(x_ref[0].astype(F32))
    nm = (c * rstd * gain_ref[...].astype(F32)[None, :]).astype(BF)
    nm_ref[0] = nm
    low = nt(nm, ad_ref[0]).astype(BF)
    low_ref[0] = low
    cos, sin = cos_ref[...], sin_ref[...]
    for b, ref in enumerate((q_ref, k_ref)):
        u = nn(nm, w_ref[b]) + nn(low, up_ref[0, b])
        if b == 0:
            u = u * QUERY_SCALE
        for p in range(u.shape[1] // 128):
            t = u[:, p * 128:(p + 1) * 128]
            ref[0, :, p * 128:(p + 1) * 128] = (t * cos + swap(t) * sin).astype(BF)
    v_ref[0] = (nn(nm, w_ref[2]) + nn(low, up_ref[0, 2])).astype(BF)

QKV_ROWS = 512


def qkv_call(ids, half_index, x, gain, w, ad, up, cos, sin, before=None, rows=None):
    S, R, D = x.shape
    W = w.shape[2]
    rank = ad.shape[1]
    L = cos.shape[0]
    rows = rows or QKV_ROWS
    n = R // rows
    tabl = lambda *bs: pl.BlockSpec((1,) + bs, lambda s, i, ids, h: (ids[s],) + (0,) * len(bs))
    turn = pl.BlockSpec((rows, 128), lambda s, i, ids, h: (h[0] * n + i, 0))
    in_specs = [pl.BlockSpec((1, rows, D), lambda s, i, ids, h: (s, i, 0)), pl.BlockSpec((D,), lambda s, i, ids, h: (0,)),
        pl.BlockSpec((3, D, W), lambda s, i, ids, h: (0, 0, 0)), tabl(rank, D), tabl(3, rank, W), turn, turn]
    args = [ids, half_index, x, gain, w, ad, up, cos, sin]
    alias = {}
    if before is not None:
        for i, b in enumerate(before):
            alias[len(args)] = i
            args.append(b)
            in_specs.append(pl.BlockSpec(memory_space=pl.ANY))
    out = lambda m: pl.BlockSpec((1, rows, m), lambda s, i, ids, h: (s, h[0] * n + i, 0))
    sd = jax.ShapeDtypeStruct
    return pl.pallas_call(qkv_kernel,
        grid_spec=pltpu.PrefetchScalarGridSpec(num_scalar_prefetch=2, grid=(S, n), in_specs=in_specs,
            out_specs=[out(W), out(W), out(W), out(rank), out(D)]),
        out_shape=[sd((S, L, W), BF)] * 3 + [sd((S, L, rank), BF), sd((S, L, D), BF)],
        input_output_aliases=alias,
        compiler_params=pltpu.CompilerParams(dimension_semantics=("arbitrary", "arbitrary"), vmem_limit_bytes=VMEM_LIMIT),
        cost_estimate=pl.CostEstimate(flops=5 * 10**9, bytes_accessed=10**7, transcendentals=10**5),
        name="qkv")(*args)

def window(seg, s, i, rows, blk, count):
    first, last = seg[s, i * rows], seg[s, i * rows + rows - 1]
    lo = jnp.int32(0); hi = jnp.int32(0)
    for j in range(count):
        lo += (seg[s, j * blk + blk - 1] < first).astype(jnp.int32)
        hi += (seg[s, j * blk] <= last).astype(jnp.int32)
    return lo, hi - lo

def att_kernel(blk, seg, half_ref, q_ref, k_ref, v_ref, seg_ref, o_ref, lse_ref):
    s = pl.program_id(0)
    R, L = q_ref.shape[1], k_ref.shape[1]
    count = L // blk
    single = seg[s, 0] == seg[s, L - 1]

    def attend(r0, rows, k0, keys, masked):
        k = k_ref[0, pl.ds(k0, keys)]
        v = v_ref[0, pl.ds(k0, keys)]
        sub = min(rows, 256)
        units = [(h, b) for b in range(rows // sub) for h in range(2)]

        def scores(h, b):
            q = q_ref[0, pl.ds(r0 + b * sub, sub)]
            sc = nt(jnp.where(lanes_of(h, q.shape), q, jnp.zeros_like(q)), k)
            if masked:
                allowed = column(seg_ref[pl.ds(s, 1), pl.ds(half_ref[0] * R + r0 + b * sub, sub)]) == seg_ref[pl.ds(s, 1), pl.ds(k0, keys)].astype(F32)
                sc = jnp.where(allowed, sc, -1e30)
            return sc

        ahead = scores(*units[0])
        outs = []
        for i, (h, b) in enumerate(units):
            sc = ahead
            if i + 1 < len(units):
                ahead = scores(*units[i + 1])
            m = jnp.max(sc, axis=-1, keepdims=True)
            p = jnp.exp2(sc - m)
            l = jnp.sum(p, axis=-1, keepdims=True)
            outs.append(nn(p.astype(BF), v) * (1.0 / l))
            lse = jnp.broadcast_to(m + jnp.log2(l), (sub, 128))
            lse_ref[0, 0, pl.ds(h, 1), pl.ds(r0 + b * sub, sub)] = lse.T[0:1]
            if h == 1:
                o_ref[0, pl.ds(r0 + b * sub, sub)] = jnp.where(lanes_of(0, outs[0].shape), outs[0], outs[1]).astype(BF)
                outs = []

    @pl.when(single)
    def _():
        attend(0, R, 0, L, False)

    @pl.when(jnp.logical_not(single))
    def _():
        def sub(i, carry):
            lo, n = window(seg, s, half_ref[0] * (R // blk) + i, blk, blk, count)
            r0 = pl.multiple_of(i * blk, blk)
            k0 = pl.multiple_of(lo * blk, blk)
            for m in range(1, count + 1):
                @pl.when(n == m)
                def _():
                    attend(r0, blk, k0, m * blk, True)
            return carry
        lax.fori_loop(0, R // blk, sub, 0)

def att_call(seg, half_index, q, k, v, blk=256):
    S, L, W = q.shape
    R = L // 2
    P = W // 128
    sd = jax.ShapeDtypeStruct
    return pl.pallas_call(functools.partial(att_kernel, blk),
        grid_spec=pltpu.PrefetchScalarGridSpec(num_scalar_prefetch=2, grid=(S, P),
            in_specs=[pl.BlockSpec((1, R, 128), lambda s, p, seg, h: (s, h[0], p)),
                pl.BlockSpec((1, L, 128), lambda s, p, seg, h: (s, 0, p)), pl.BlockSpec((1, L, 128), lambda s, p, seg, h: (s, 0, p)),
                pl.BlockSpec((S, L), lambda s, p, seg, h: (0, 0))],
            out_specs=[pl.BlockSpec((1, R, 128), lambda s, p, seg, h: (s, 0, p)),
                pl.BlockSpec((1, 1, 2, R), lambda s, p, seg, h: (s, p, 0, 0))]),
        out_shape=[sd((S, R, W), BF), sd((S, P, 2, R), F32)],
        compiler_params=pltpu.CompilerParams(dimension_semantics=("arbitrary", "arbitrary"), vmem_limit_bytes=VMEM_LIMIT),
        cost_estimate=pl.CostEstimate(flops=8 * 10**9, bytes_accessed=8 * 10**6, transcendentals=8 * 10**6),
        name="attend")(seg, half_index, q, k, v, seg)

def back_kernel(blk, s, seg, half_ref, ids, q_ref, k_ref, v_ref, dom_ref, doo_ref, om_ref, oo_ref, lsem_ref, lseo_ref, seg_ref,
        cos_ref, sin_ref, low_ref, up_ref, nm_hbm, *rest):
    gpm_ref, gpo_ref, pay_ref, lgm_ref, lgo_ref, dq_acc, dk_acc, dv_acc, lg_acc, nm_ref, sem = rest[-11:]
    pair = pl.program_id(0)
    L = q_ref.shape[1]
    R = L // 2
    count = L // blk
    single = seg[s, 0] == seg[s, L - 1]
    mine = half_ref[0]
    dk_acc[...] = jnp.zeros_like(dk_acc)
    dv_acc[...] = jnp.zeros_like(dv_acc)
    fetch = pltpu.make_async_copy(nm_hbm.at[s], nm_ref, sem)

    @pl.when(pair == 0)
    def _():
        fetch.start()

    def part(do_ref, o_ref, lse_ref, n0, r0, rows, k0, keys, masked):
        q = q_ref[0, pl.ds(n0, rows)]
        do = do_ref[0, pl.ds(r0, rows)]
        o = o_ref[0, pl.ds(r0, rows)]
        k = k_ref[0, pl.ds(k0, keys)]
        v = v_ref[0, pl.ds(k0, keys)]
        prod = (do.astype(F32) * o.astype(F32)).T
        zero = jnp.zeros_like(q)
        if masked:
            allowed = column(seg_ref[s:s + 1, pl.ds(k0, keys)]) == seg_ref[s:s + 1, pl.ds(n0, rows)].astype(F32)
        ps, dss, dos, qs, ks = [], [], [], [], []
        for h in range(2):
            qh = jnp.where(lanes_of(h, q.shape), q, zero)
            doh = jnp.where(lanes_of(h, q.shape), do, zero)
            kh = jnp.where(lanes_of(h, k.shape), k, jnp.zeros_like(k))
            delta = jnp.sum(prod[h * 64:(h + 1) * 64], axis=0, keepdims=True)
            lse = lse_ref[0, 0, pl.ds(h, 1), pl.ds(r0, rows)]
            st = nt(k, qh)
            p = jnp.exp2(st - lse)
            if masked:
                p = jnp.where(allowed, p, 0.0)
            ds = p * (nt(v, doh) - delta)
            ps.append(p.astype(BF)); dss.append(ds.astype(BF)); dos.append(doh); qs.append(qh); ks.append(kh)
        dv_acc[pl.ds(k0, keys)] += nn(jnp.concatenate(ps, 1), jnp.concatenate(dos, 0))
        dk_acc[pl.ds(k0, keys)] += nn(jnp.concatenate(dss, 1), jnp.concatenate(qs, 0))
        dq_acc[pl.ds(n0, rows)] = tn(jnp.concatenate(dss, 0), jnp.concatenate(ks, 0))

    halves = ((dom_ref, om_ref, lsem_ref, mine), (doo_ref, oo_ref, lseo_ref, 1 - mine))

    @pl.when(single)
    def _():
        for do_ref, o_ref, lse_ref, h in halves:
            part(do_ref, o_ref, lse_ref, pl.multiple_of(h * R, R), 0, R, 0, L, False)

    @pl.when(jnp.logical_not(single))
    def _():
        for do_ref, o_ref, lse_ref, h in halves:
            lo, n = window(seg, s, h, R, blk, count)
            for m in (count - 1, count):
                @pl.when(n == m)
                def _():
                    part(do_ref, o_ref, lse_ref, pl.multiple_of(h * R, R), 0, R, pl.multiple_of(lo * blk, blk), m * blk, True)

            @pl.when(n < count - 1)
            def _():
                def sub(i, carry):
                    lo, n = window(seg, s, h * (R // blk) + i, blk, blk, count)
                    r0 = pl.multiple_of(i * blk, blk)
                    n0 = pl.multiple_of(h * R + i * blk, blk)
                    k0 = pl.multiple_of(lo * blk, blk)
                    for m in range(1, count - 1):
                        @pl.when(n == m)
                        def _():
                            part(do_ref, o_ref, lse_ref, n0, r0, blk, k0, m * blk, True)
                    return carry
                lax.fori_loop(0, R // blk, sub, 0)

    cos, sin = cos_ref[...], sin_ref[...]
    def unrotate(g, factor):
        g = g * factor
        return (g * cos - swap(g) * sin).astype(BF)
    W = gpm_ref.shape[3] * pl.num_programs(0)
    grads = (unrotate(dq_acc[...], 0.125), unrotate(dk_acc[...], 1.0 / LOG2E), dv_acc[...].astype(BF))
    for h in range(2):
        @pl.when(mine == h)
        def _():
            for b, g in enumerate(grads):
                gpm_ref[0, b] = g[h * R:(h + 1) * R]
                gpo_ref[0, b] = g[(1 - h) * R:(2 - h) * R]
    grads = jnp.concatenate(grads, 1)
    lgs = nt(grads, jnp.concatenate([up_ref[0, b] for b in range(3)], 1))
    ups = tn(low_ref[0], grads).astype(BF)
    for b in range(3):
        pay_ref[0, :, pl.ds(pl.multiple_of(b * W + pair * 128, 128), 128)] = ups[:, b * 128:(b + 1) * 128]

    @pl.when(pair == 0)
    def _():
        lg_acc[...] = lgs

    @pl.when(pair > 0)
    def _():
        lg_acc[...] += lgs

    @pl.when(pair == pl.num_programs(0) - 1)
    def _():
        fetch.wait()
        D = nm_ref.shape[1]
        o = pay_ref.shape[2] - 128 - D
        pay_ref[0, :, o:o + D] = tn(lg_acc[...].astype(BF), nm_ref[...]).astype(BF)
        lane = lax.broadcasted_iota(jnp.int32, (lg_acc.shape[1], 128), 1)
        pay_ref[0, :, o + D:] = jnp.where(lane == ids[s], 1.0, 0.0).astype(BF)
        lgm_ref[0] = lg_acc[pl.ds(pl.multiple_of(mine * R, R), R)]
        lgo_ref[0] = lg_acc[pl.ds(pl.multiple_of((1 - mine) * R, R), R)]

def back_call(s, seg, half_index, ids, q, k, v, dom, doo, om, oo, lsem, lseo, cos, sin, low, up, nm, before=None, blk=256):
    S, L, W = q.shape
    R = L // 2
    P = W // 128
    rank = low.shape[2]
    sd = jax.ShapeDtypeStruct
    full = pl.BlockSpec((1, L, 128), lambda p, *_: (s, 0, p))
    hlf = pl.BlockSpec((1, R, 128), lambda p, *_: (s, 0, p))
    ls = pl.BlockSpec((1, 1, 2, R), lambda p, *_: (s, p, 0, 0))
    tb = pl.BlockSpec((L, 128), lambda p, *_: (0, 0))
    gp = pl.BlockSpec((1, 3, R, 128), lambda p, *_: (0, 0, 0, p))
    lg = pl.BlockSpec((1, R, rank), lambda p, *_: (0, 0, 0))
    pay = 3 * W + nm.shape[2] + 128
    any_ = pl.BlockSpec(memory_space=pl.ANY)
    args = [seg, half_index, ids, q, k, v, dom, doo, om, oo, lsem, lseo, seg, cos, sin, low, up, nm]
    alias = {}
    if before is not None:
        alias[len(args)] = 2
        args.append(before)
    return pl.pallas_call(functools.partial(back_kernel, blk, s),
        grid_spec=pltpu.PrefetchScalarGridSpec(num_scalar_prefetch=3, grid=(P,),
            in_specs=[full, full, full, hlf, hlf, hlf, hlf, ls, ls, pl.BlockSpec((S, L), lambda p, *_: (0, 0)),
                tb, tb, pl.BlockSpec((1, L, rank), lambda p, *_: (s, 0, 0)),
                pl.BlockSpec((1, 3, rank, 128), lambda p, seg, h, ids: (ids[s], 0, 0, p)), any_] + [any_] * len(alias),
            out_specs=[gp, gp, pl.BlockSpec((1, rank, pay), lambda p, *_: (s, 0, 0)), lg, lg],
            scratch_shapes=[pltpu.VMEM((L, 128), F32)] * 3 + [pltpu.VMEM((L, rank), F32), pltpu.VMEM(nm.shape[1:], BF), pltpu.SemaphoreType.DMA]),
        out_shape=[sd((1, 3, R, W), BF), sd((1, 3, R, W), BF), sd((S, rank, pay), BF), sd((1, R, rank), F32), sd((1, R, rank), F32)],
        input_output_aliases=alias,
        compiler_params=pltpu.CompilerParams(dimension_semantics=("arbitrary",), vmem_limit_bytes=VMEM_LIMIT),
        cost_estimate=pl.CostEstimate(flops=18 * 10**9, bytes_accessed=10**7, transcendentals=8 * 10**6),
        name="attend_back")(*args)

def final_kernel(ids, x_ref, gain_ref, wo_ref, wr_ref, ad_ref, mid_ref, gm_ref, gr_ref, lm_ref, lr_ref, *rest):
    gn = nn((lm_ref[0] + lr_ref[0]).astype(BF), ad_ref[0])
    for b in range(3):
        gn += nt(gm_ref[0, b], wo_ref[b]) + nt(gr_ref[0, b], wr_ref[b])
    c, rstd = norm_stats(x_ref[0].astype(F32))
    rest[-1][0] = mid_ref[0] + norm_back(gn, c, rstd, gain_ref[...].astype(F32)[None, :])

def final_call(s, ids, x, gain, w_own, w_its, ad, mid, parts, before=None, rows=256):
    S, R, D = x.shape
    W = w_own.shape[2]
    rank = ad.shape[1]
    wsp = pl.BlockSpec((3, D, W), lambda i, ids: (0, 0, 0))
    row = pl.BlockSpec((1, rows, D), lambda i, ids: (s, i, 0))
    gp = pl.BlockSpec((1, 3, rows, W), lambda i, ids: (0, 0, i, 0))
    lg = pl.BlockSpec((1, rows, rank), lambda i, ids: (0, i, 0))
    in_specs = [row, pl.BlockSpec((D,), lambda i, ids: (0,)), wsp, wsp, pl.BlockSpec((1, rank, D), lambda i, ids: (ids[s], 0, 0)), row,
        gp, gp, lg, lg]
    args = [ids, x, gain, w_own, w_its, ad, mid, *parts]
    alias = {}
    if before is not None:
        alias[len(args)] = 0
        args.append(before)
        in_specs.append(pl.BlockSpec(memory_space=pl.ANY))
    return pl.pallas_call(final_kernel,
        grid_spec=pltpu.PrefetchScalarGridSpec(num_scalar_prefetch=1, grid=(R // rows,), in_specs=in_specs, out_specs=row),
        out_shape=jax.ShapeDtypeStruct((S, R, D), F32),
        input_output_aliases=alias,
        compiler_params=pltpu.CompilerParams(dimension_semantics=("arbitrary",), vmem_limit_bytes=VMEM_LIMIT),
        cost_estimate=pl.CostEstimate(flops=4 * 10**9, bytes_accessed=10**7, transcendentals=10**4),
        name="final")(*args)

def unpack_kernel(in_ref, up_ref, down_ref):
    rank = in_ref.shape[0]
    W = up_ref.shape[3]
    for r in range(rank):
        for b in range(3):
            up_ref[:, b, r, :] = in_ref[r, :, b * W:(b + 1) * W].astype(F32)
        down_ref[:, r, :] = in_ref[r, :, 3 * W:].astype(F32)

def unpack_call(shares, W, D):
    rank, adapters, _ = shares.shape
    vm = pl.BlockSpec(memory_space=pltpu.VMEM)
    return pl.pallas_call(unpack_kernel, in_specs=[vm], out_specs=[vm, vm],
        out_shape=[jax.ShapeDtypeStruct((adapters, 3, rank, W), F32), jax.ShapeDtypeStruct((adapters, rank, D), F32)],
        compiler_params=pltpu.CompilerParams(vmem_limit_bytes=VMEM_LIMIT),
        cost_estimate=pl.CostEstimate(flops=10**6, bytes_accessed=2 * 10**6, transcendentals=0),
        name="unpack")(shares)


def unpack_units_kernel(at_ref, in_ref, iu_ref, md_ref, od_ref, *tables):
    rank = in_ref.shape[0]
    half = od_ref.shape[2]
    ffh = md_ref.shape[2]
    main = ffh // 256 * 256
    tail = ffh - main
    own_first = at_ref[0] == 0
    for r in range(rank):
        row = lambda a, n: in_ref[r, :, a:a + n].astype(F32)
        o = 3 * main + half
        ends = row(o + 6 * half, 3 * tail)
        for i in range(3):
            unit = jnp.concatenate([row(i * main, main), ends[:, i * tail:(i + 1) * tail]], 1)
            if i < 2:
                iu_ref[:, r, i, :] = unit
            else:
                md_ref[:, r, :] = unit
        od_ref[:, r, :] = row(3 * main, half)
        for i, ref in enumerate(tables):
            own, got = row(o + i * half, half), row(o + (3 + i) * half, half)
            ref[:, r, :half] = jnp.where(own_first, own, got)
            ref[:, r, half:] = jnp.where(own_first, got, own)

def unpack_units_call(at, shares, half, ffh):
    rank, adapters, _ = shares.shape
    vm = pl.BlockSpec(memory_space=pltpu.VMEM)
    sd = lambda *sh: jax.ShapeDtypeStruct((adapters, rank) + sh, F32)
    return pl.pallas_call(unpack_units_kernel, in_specs=[pl.BlockSpec(memory_space=pltpu.SMEM), vm], out_specs=[vm] * 6,
        out_shape=[sd(2, ffh), sd(ffh), sd(half)] + [sd(2 * half)] * 3,
        compiler_params=pltpu.CompilerParams(vmem_limit_bytes=VMEM_LIMIT),
        cost_estimate=pl.CostEstimate(flops=10**6, bytes_accessed=6 * 10**6, transcendentals=0),
        name="unpack_units")(at, shares)


HEAD_DIM = 64
ROPE_BASE = 160000.0


def rotary_tables(length):
    inverse = 1.0 / ROPE_BASE ** (np.arange(0, HEAD_DIM, 2) / HEAD_DIM)
    angles = np.arange(length)[:, None] * inverse[None, :]
    cos, sin = np.cos(angles), np.sin(angles)
    return (
        jnp.asarray(np.concatenate([cos, cos, cos, cos], 1), F32),
        jnp.asarray(np.concatenate([-sin, sin, -sin, sin], 1), F32),
    )


def spread(packed, tag_at, tags, groups, shards):
    S, rank, m = packed.shape
    if shards != rank:
        flat = [packed[:, :, a:b].reshape(S, shards, -1) for a, b in groups]
        packed = jnp.concatenate(flat + [jnp.broadcast_to(packed[:, :1, tag_at:tag_at + tags], (S, shards, tags))], -1)
        tag_at = packed.shape[2] - tags
    got = lax.all_to_all(packed, "dp", 1, 1, tiled=True).reshape(S * shards, -1)
    sums = lax.dot_general(got[:, tag_at:tag_at + tags], got, (((0,), (0,)), ((), ())), preferred_element_type=F32)
    if shards != rank:
        return sums[:, :tag_at]
    return jnp.concatenate([sums[:, a:b] for a, b in groups], -1)


def collect(shares, shards):
    wide = jnp.broadcast_to(shares.astype(BF), (shards,) + shares.shape)
    return lax.all_to_all(wide, "dp", 0, 0, tiled=True)


def body(x, cotangent, norm_in, norm_mid, w_qkv, w_out, w_in, w_ff, qkv_down, qkv_up, out_down, out_up, in_down, in_up,
         mlp_down, ff_up, segs, ids):
    other = lambda a: lax.ppermute(a, "tensor", [(0, 1), (1, 0)])
    tie = lax.optimization_barrier
    t = lax.axis_index("tensor")
    shards = lax.axis_size("dp")
    mine, its = t.astype(jnp.int32).reshape(1), (1 - t).astype(jnp.int32).reshape(1)
    S, R, D = x.shape
    L = segs.shape[1]
    x_its = other(x)
    w_qkv = w_qkv.transpose(1, 0, 2)
    w_in = w_in.transpose(1, 2, 0)
    qkv_down, out_down, in_down, mlp_down = (a.transpose(0, 2, 1) for a in (qkv_down, out_down, in_down, mlp_down))
    qkv_up, in_up = qkv_up.transpose(0, 2, 1, 3), in_up.transpose(0, 2, 1, 3)
    gain_in, gain_mid = norm_in, norm_mid
    half = w_out.shape[0]
    ffh = w_ff.shape[0]
    main = ffh // 256 * 256
    tail = ffh - main
    rank = out_up.shape[1]
    adapters = out_up.shape[0]

    w_out_its, w_in_its, w_ff_its, w_qkv_its = other(w_out), other(w_in), other(w_ff), other(w_qkv)
    out_down_its, in_up_its, mlp_down_its = other(out_down), other(in_up), other(mlp_down)

    cos, sin = rotary_tables(L)
    first = qkv_call(ids, mine, x, gain_in, w_qkv, qkv_down, qkv_up, cos, sin)
    q, k, v, low, normed = qkv_call(ids, its, x_its, gain_in, w_qkv, qkv_down, qkv_up, cos, sin, before=first)
    ctx_its, lse_its = att_call(segs, its, q, k, v)
    ctx_got = other(ctx_its)
    ctx_mine, lse_mine = att_call(segs, mine, q, k, v)
    output, grad_mid, gc_mine, gc_its, keep, send = mlp_call(
        ids, mine, x, ctx_mine, ctx_got, cotangent, gain_mid, out_down, out_down_its, in_up, in_up_its, mlp_down, mlp_down_its,
        out_up, in_down, ff_up, w_out, w_out_its, w_in, w_in_its, w_ff, w_ff_its)
    gc_got = other(gc_its)

    packed = (keep + other(send).astype(F32)).astype(BF)
    lanes = 3 * main + 4 * half
    units = lanes - 3 * half
    shares = spread(packed, lanes + 3 * tail, adapters, ((0, units), (units, lanes), (lanes, lanes + 3 * tail)), shards)

    back = lambda s, gc_got, before=None: back_call(
        s, segs, mine, ids, q, k, v, gc_mine, gc_got, ctx_mine, ctx_its, lse_mine, lse_its, cos, sin, low, qkv_up, normed, before)
    gp_mine0, gp_its0, packed, lg_mine0, lg_its0 = back(0, gc_got)
    gp_got0, lg_got0 = other(gp_its0), other(lg_its0)
    shares, packed = tie((shares.astype(BF), packed))
    c0, c1 = rank * units // shards, rank * lanes // shards
    halves = shares[:, c0:c1]
    sums = collect(jnp.concatenate([shares[:, :c1], other(halves), shares[:, c1:]], -1), shards)
    gp_mine1, gp_its1, packed, lg_mine1, lg_its1 = back(1, gc_got, packed)
    sums, packed = tie((sums, packed))
    gp_got1, lg_got1 = other(gp_its1), other(lg_its1)
    m = packed.shape[2] - 128
    shares = spread(packed, m, adapters, ((0, m - D), (m - D, m)), shards)
    grad_input = final_call(0, ids, x, gain_in, w_qkv, w_qkv_its, qkv_down, grad_mid, (gp_mine0, gp_got0, lg_mine0, lg_got0))
    shares, grad_input = tie((shares, grad_input))
    cut = rank * (m - D) // shards
    downs = shares[:, cut:]
    shares = jnp.concatenate([shares[:, :cut], downs + other(downs)], -1)
    shares, sums, gp_got1 = tie((shares, sums, gp_got1))
    qsums = collect(shares, shards)
    grad_input = final_call(1, ids, x, gain_in, w_qkv, w_qkv_its, qkv_down, grad_mid, (gp_mine1, gp_got1, lg_mine1, lg_got1), grad_input)

    whole = lambda a: a.transpose(1, 0, 2).reshape(adapters, rank, -1)
    if shards == rank:
        g_in_up, g_mlp_down, g_out_down, g_ff_up, g_in_down, g_out_up = unpack_units_call(mine, sums, half, ffh)
    else:
        a, own, got, b = (whole(z) for z in jnp.split(sums, (c0, c1, 2 * c1 - c0), axis=2))
        unit = lambda i: jnp.concatenate([a[..., i * main:(i + 1) * main], b[..., i * tail:(i + 1) * tail]], -1).astype(F32)
        g_in_up, g_mlp_down = jnp.stack([unit(0), unit(1)], 2), unit(2)
        g_out_down = a[..., 3 * main:].astype(F32)
        lo, hi = jnp.where(t == 0, own, got), jnp.where(t == 0, got, own)
        g_ff_up, g_in_down, g_out_up = (
            jnp.concatenate([lo[..., i * half:(i + 1) * half], hi[..., i * half:(i + 1) * half]], -1).astype(F32) for i in range(3))
    g_mlp_down, g_out_down = g_mlp_down.transpose(0, 2, 1), g_out_down.transpose(0, 2, 1)
    if shards == rank:
        g_qkv_up, g_qkv_down = unpack_call(qsums, (m - D) // 3, D)
    else:
        g_qkv_up = whole(qsums[..., :cut]).astype(F32).reshape(adapters, rank, 3, -1).transpose(0, 2, 1, 3)
        g_qkv_down = whole(qsums[..., cut:]).astype(F32)
    g_qkv_up, g_qkv_down = g_qkv_up.transpose(0, 2, 1, 3), g_qkv_down.transpose(0, 2, 1)
    return (output, grad_input, g_qkv_down, g_qkv_up, g_out_down, g_out_up, g_in_down.transpose(0, 2, 1), g_in_up, g_mlp_down, g_ff_up)


def solution(mesh):
    return jax.shard_map(
        body,
        mesh=mesh,
        in_specs=(
            P("dp", "tensor", None),
            P("dp", "tensor", None),
            P(),
            P(),
            P(None, None, "tensor"),
            P("tensor", None),
            P(None, None, "tensor"),
            P("tensor", None),
            P(),
            P(None, None, None, "tensor"),
            P(None, "tensor", None),
            P(),
            P(),
            P(None, None, None, "tensor"),
            P(None, "tensor", None),
            P(),
            P("dp", None),
            P("dp"),
        ),
        out_specs=(
            P("dp", "tensor", None),
            P("dp", "tensor", None),
            P(),
            P(None, None, None, "tensor"),
            P(None, "tensor", None),
            P(),
            P(),
            P(None, None, None, "tensor"),
            P(None, "tensor", None),
            P(),
        ),
        check_vma=False,
    )
```

```python
import functools
import math

import jax
import jax.numpy as jnp
import numpy as np
from jax import lax
from jax.experimental import pallas as pl
from jax.experimental.pallas import tpu as pltpu
from jax.sharding import PartitionSpec as P

F32, BF = jnp.float32, jnp.bfloat16
EPS = 1e-05
VMEM_LIMIT = 65280 * 1024

def nn(a, b): return lax.dot_general(a, b, (((1,), (0,)), ((), ())), preferred_element_type=F32)
def nt(a, b): return lax.dot_general(a, b, (((1,), (1,)), ((), ())), preferred_element_type=F32)
def tn(a, b): return lax.dot_general(a, b, (((0,), (0,)), ((), ())), preferred_element_type=F32)

def norm_stats(v):
    mean = jnp.mean(v, axis=-1, keepdims=True)
    c = v - mean
    var = jnp.mean(c * c, axis=-1, keepdims=True)
    return c, lax.rsqrt(var + EPS)

def norm_back(e, c, rstd, gain):
    n = c * rstd
    h = e * gain
    return (h - jnp.mean(h, axis=-1, keepdims=True) - n * jnp.mean(h * n, axis=-1, keepdims=True)) * rstd

def mlp_kernel(chunk, main, tail,
        ids, at_ref, x_ref, cm_ref, cr_ref, g_ref, gain_ref,
        od_own, od_its, iu_own, iu_its, md_own, md_its, ou_ref, id_ref, fu_ref,
        wo_own, wo_its, wi_own, wi_its, wf_own, wf_its,
        out_ref, gmid_ref, gcm_ref, gci_ref, keep_ref, send_ref,
        wo, wi, wf, acc_o, acc_n, acc_lm, acc_li, nm_ref, mid_ref, iu, md, d_iu, d_md, d_w, sem):
    s = pl.program_id(0)
    half = wo_own.shape[0]
    rank = ou_ref.shape[1]
    copies = []
    def cp(src, dst):
        copies.append(pltpu.make_async_copy(src, dst, sem.at[len(copies)]))
    cp(wo_own, wo.at[pl.ds(0, half)])
    cp(wo_its, wo.at[pl.ds(half, half)])
    for j, (wi_h, wf_h) in enumerate(((wi_own, wf_own), (wi_its, wf_its))):
        for b in range(2):
            cp(wi_h.at[b, pl.ds(0, main)], wi.at[b, pl.ds(j * main, main)])
        cp(wf_h.at[pl.ds(0, main)], wf.at[pl.ds(j * main, main)])
        for b in range(2):
            cp(wi_h.at[b, pl.ds(main, tail)], wi.at[b, pl.ds(2 * main + j * tail, tail)])
        cp(wf_h.at[pl.ds(main, tail)], wf.at[pl.ds(2 * main + j * tail, tail)])

    @pl.when(s == 0)
    def _():
        for c in copies: c.start()
        for c in copies[:2]: c.wait()

    for dst, own, its in ((iu.at[0], iu_own[0, 0], iu_its[0, 0]), (iu.at[1], iu_own[0, 1], iu_its[0, 1]), (md, md_own[0], md_its[0])):
        dst[:, :main] = own[:, :main]
        dst[:, main:2 * main] = its[:, :main]
        dst[:, 2 * main:] = jnp.concatenate([own[:, main:].astype(F32), its[:, main:].astype(F32)], 1).astype(BF)

    cm, cr = cm_ref[0], cr_ref[0]
    odo, odi = od_own[0], od_its[0]
    ou = ou_ref[0]
    low_out = (nt(cm, odo) + nt(cr, odi)).astype(BF)
    att = nn(cm, wo[0:half]) + nn(cr, wo[half:]) + nn(low_out, ou)
    middle = x_ref[0].astype(F32) + att
    mid_ref[...] = middle
    c, rstd = norm_stats(middle)
    gain = gain_ref[...].astype(F32)[None, :]
    nm = (c * rstd * gain).astype(BF)
    nm_ref[...] = nm
    g = g_ref[0]
    low_in = nt(nm, id_ref[0]).astype(BF)
    glm = nt(g, fu_ref[0]).astype(BF)
    acc_o[...] = jnp.zeros_like(acc_o)
    acc_n[...] = jnp.zeros_like(acc_n)
    acc_lm[...] = jnp.zeros_like(acc_lm)
    acc_li[...] = jnp.zeros_like(acc_li)

    @pl.when(s == 0)
    def _():
        for c_ in copies[2:]: c_.wait()

    def step(first, size):
        rows = pl.ds(first, size)
        nm = nm_ref[...]
        g = g_ref[0]
        w0, w1, wfc = wi[0, rows], wi[1, rows], wf[rows]
        iu0, iu1, mdc = iu[0, :, rows], iu[1, :, rows], md[:, rows]
        u = nt(nm, w0) + nn(low_in, iu0)
        v = nt(nm, w1) + nn(low_in, iu1)
        gh = nt(g, wfc) + nn(glm, mdc)
        cdf = 0.5 * (1.0 + lax.erf(u * (1.0 / math.sqrt(2.0))))
        pdf = jnp.exp(-0.5 * u * u) * (1.0 / math.sqrt(2.0 * math.pi))
        gel = u * cdf
        h = (gel * v).astype(BF)
        gu = (gh * v * (cdf + u * pdf)).astype(BF)
        gv = (gh * gel).astype(BF)
        acc_o[...] += nn(h, wfc)
        acc_n[...] += nn(gu, w0) + nn(gv, w1)
        acc_lm[...] += nt(h, mdc)
        acc_li[...] += nt(gu, iu0) + nt(gv, iu1)
        d_iu[0, :, rows] = tn(low_in, gu)
        d_iu[1, :, rows] = tn(low_in, gv)
        d_md[:, rows] = tn(glm, h)

    def loop(i, carry):
        step(pl.multiple_of(i * chunk, chunk), chunk)
        return carry
    lax.fori_loop(0, 2 * main // chunk, loop, 0)
    step(2 * main, 2 * tail)

    fu = fu_ref[0]
    low_mlp = acc_lm[...].astype(BF)
    out_ref[0] = (mid_ref[...] + acc_o[...] + nn(low_mlp, fu)).astype(BF)
    g = g_ref[0]
    d_w[0] = tn(low_mlp, g)
    gli = acc_li[...].astype(BF)
    d_w[1] = tn(gli, nm_ref[...])
    gnm = acc_n[...] + nn(gli, id_ref[0])
    c, rstd = norm_stats(mid_ref[...])
    gmid = g.astype(F32) + norm_back(gnm, c, rstd, gain)
    gmid_ref[0] = gmid
    ga = gmid.astype(BF)
    glo = nt(ga, ou).astype(BF)
    d_w[2] = tn(low_out, ga)
    gcm_ref[0] = (nt(ga, wo[0:half]) + nn(glo, odo)).astype(BF)
    gci_ref[0] = (nt(ga, wo[half:]) + nn(glo, odi)).astype(BF)

    sides = ((keep_ref, 0, at_ref[0], cm, F32), (send_ref, 1, 1 - at_ref[0], cr, BF))
    for ref, j, at, ctx, kind in sides:
        parts = (d_iu.at[0], d_iu.at[1], d_md)
        for i, d in enumerate(parts):
            ref[0, :, i * main:(i + 1) * main] = d[:, j * main:(j + 1) * main].astype(kind)
        o = 3 * main
        ref[0, :, o:o + half] = tn(glo, ctx).astype(kind)
        o += half
        for i in range(3):
            ref[0, :, o:o + half] = d_w[i, :, pl.ds(pl.multiple_of(at * half, half), half)].astype(kind)
            o += half
        lane = lax.broadcasted_iota(jnp.int32, (rank, 128 - 3 * tail), 1)
        tag = jnp.where((lane == ids[s]) & (j == 0), 1.0, 0.0)
        ends = [d[:, 2 * main + j * tail:2 * main + (j + 1) * tail] for d in parts]
        ref[0, :, o:] = jnp.concatenate(ends + [tag], 1).astype(kind)


def mlp_call(ids, at, x, cm, cr, g, gain, od_own, od_its, iu_own, iu_its, md_own, md_its, ou, idn, fu,
             wo_own, wo_its, wi_own, wi_its, wf_own, wf_its, chunk=512):
    S, R, D = x.shape
    half = wo_own.shape[0]
    ffh = wf_own.shape[0]
    main = ffh // 256 * 256
    tail = ffh - main
    rank = ou.shape[1]
    ff = 2 * ffh
    packed = 3 * main + 4 * half + 128
    seq = lambda *bs: pl.BlockSpec((1,) + bs, lambda s, *_: (s,) + (0,) * len(bs))
    tab = lambda *bs: pl.BlockSpec((1,) + bs, lambda s, ids, at: (ids[s],) + (0,) * len(bs))
    any_ = pl.BlockSpec(memory_space=pl.ANY)
    in_specs = [seq(R, D), seq(R, half), seq(R, half), seq(R, D), pl.BlockSpec((D,), lambda s, *_: (0,)),
        tab(rank, half), tab(rank, half), tab(2, rank, ffh), tab(2, rank, ffh), tab(rank, ffh), tab(rank, ffh),
        tab(rank, D), tab(rank, D), tab(rank, D)] + [any_] * 6
    out_specs = [seq(R, D), seq(R, D), seq(R, half), seq(R, half), seq(rank, packed), seq(rank, packed)]
    sd = jax.ShapeDtypeStruct
    out_shape = [sd((S, R, D), BF), sd((S, R, D), F32), sd((S, R, half), BF), sd((S, R, half), BF),
        sd((S, rank, packed), F32), sd((S, rank, packed), BF)]
    scratch = [pltpu.VMEM((2 * half, D), BF), pltpu.VMEM((2, ff, D), BF), pltpu.VMEM((ff, D), BF),
        pltpu.VMEM((R, D), F32), pltpu.VMEM((R, D), F32), pltpu.VMEM((R, rank), F32), pltpu.VMEM((R, rank), F32),
        pltpu.VMEM((R, D), BF), pltpu.VMEM((R, D), F32), pltpu.VMEM((2, rank, ff), BF), pltpu.VMEM((rank, ff), BF),
        pltpu.VMEM((2, rank, ff), F32), pltpu.VMEM((rank, ff), F32), pltpu.VMEM((3, rank, D), F32), pltpu.SemaphoreType.DMA((14,))]
    return pl.pallas_call(functools.partial(mlp_kernel, chunk, main, tail),
        grid_spec=pltpu.PrefetchScalarGridSpec(num_scalar_prefetch=2, grid=(S,), in_specs=in_specs, out_specs=out_specs, scratch_shapes=scratch),
        out_shape=out_shape,
        compiler_params=pltpu.CompilerParams(dimension_semantics=("arbitrary",), vmem_limit_bytes=VMEM_LIMIT),
        cost_estimate=pl.CostEstimate(flops=40 * 10**9, bytes_accessed=40 * 10**6, transcendentals=3 * 10**6),
        name="mlp")(ids, at, x, cm, cr, g, gain, od_own, od_its, iu_own, iu_its, md_own, md_its, ou, idn, fu,
                    wo_own, wo_its, wi_own, wi_its, wf_own, wf_its)


LOG2E = 1.4426950408889634
QUERY_SCALE = LOG2E / 8.0

def lanes_of(head, shape):
    return (lax.broadcasted_iota(jnp.int32, shape, len(shape) - 1) // 64) == head

def column(row):
    return jnp.broadcast_to(row.astype(F32), (8, row.shape[1])).T[:, :1]

def swap(u):
    lane = lax.broadcasted_iota(jnp.int32, u.shape, 1)
    return jnp.where((lane & 63) < 32, pltpu.roll(u, 96, 1), pltpu.roll(u, 32, 1))


def qkv_kernel(ids, half_ref, x_ref, gain_ref, w_ref, ad_ref, up_ref, cos_ref, sin_ref, *rest):
    q_ref, k_ref, v_ref, low_ref, nm_ref = rest[-5:]
    c, rstd = norm_stats(x_ref[0].astype(F32))
    nm = (c * rstd * gain_ref[...].astype(F32)[None, :]).astype(BF)
    nm_ref[0] = nm
    low = nt(nm, ad_ref[0]).astype(BF)
    low_ref[0] = low
    cos, sin = cos_ref[...], sin_ref[...]
    for b, ref in enumerate((q_ref, k_ref)):
        u = nn(nm, w_ref[b]) + nn(low, up_ref[0, b])
        if b == 0:
            u = u * QUERY_SCALE
        for p in range(u.shape[1] // 128):
            t = u[:, p * 128:(p + 1) * 128]
            ref[0, :, p * 128:(p + 1) * 128] = (t * cos + swap(t) * sin).astype(BF)
    v_ref[0] = (nn(nm, w_ref[2]) + nn(low, up_ref[0, 2])).astype(BF)

QKV_ROWS = 512


def qkv_call(ids, half_index, x, gain, w, ad, up, cos, sin, before=None, rows=None):
    S, R, D = x.shape
    W = w.shape[2]
    rank = ad.shape[1]
    L = cos.shape[0]
    rows = rows or QKV_ROWS
    n = R // rows
    tabl = lambda *bs: pl.BlockSpec((1,) + bs, lambda s, i, ids, h: (ids[s],) + (0,) * len(bs))
    turn = pl.BlockSpec((rows, 128), lambda s, i, ids, h: (h[0] * n + i, 0))
    in_specs = [pl.BlockSpec((1, rows, D), lambda s, i, ids, h: (s, i, 0)), pl.BlockSpec((D,), lambda s, i, ids, h: (0,)),
        pl.BlockSpec((3, D, W), lambda s, i, ids, h: (0, 0, 0)), tabl(rank, D), tabl(3, rank, W), turn, turn]
    args = [ids, half_index, x, gain, w, ad, up, cos, sin]
    alias = {}
    if before is not None:
        for i, b in enumerate(before):
            alias[len(args)] = i
            args.append(b)
            in_specs.append(pl.BlockSpec(memory_space=pl.ANY))
    out = lambda m: pl.BlockSpec((1, rows, m), lambda s, i, ids, h: (s, h[0] * n + i, 0))
    sd = jax.ShapeDtypeStruct
    return pl.pallas_call(qkv_kernel,
        grid_spec=pltpu.PrefetchScalarGridSpec(num_scalar_prefetch=2, grid=(S, n), in_specs=in_specs,
            out_specs=[out(W), out(W), out(W), out(rank), out(D)]),
        out_shape=[sd((S, L, W), BF)] * 3 + [sd((S, L, rank), BF), sd((S, L, D), BF)],
        input_output_aliases=alias,
        compiler_params=pltpu.CompilerParams(dimension_semantics=("arbitrary", "arbitrary"), vmem_limit_bytes=VMEM_LIMIT),
        cost_estimate=pl.CostEstimate(flops=5 * 10**9, bytes_accessed=10**7, transcendentals=10**5),
        name="qkv")(*args)

def window(seg, s, i, rows, blk, count):
    first, last = seg[s, i * rows], seg[s, i * rows + rows - 1]
    lo = jnp.int32(0); hi = jnp.int32(0)
    for j in range(count):
        lo += (seg[s, j * blk + blk - 1] < first).astype(jnp.int32)
        hi += (seg[s, j * blk] <= last).astype(jnp.int32)
    return lo, hi - lo

def att_kernel(blk, seg, half_ref, q_ref, k_ref, v_ref, seg_ref, o_ref, lse_ref):
    s = pl.program_id(0)
    R, L = q_ref.shape[1], k_ref.shape[1]
    count = L // blk
    single = seg[s, 0] == seg[s, L - 1]

    def attend(r0, rows, k0, keys, masked):
        k = k_ref[0, pl.ds(k0, keys)]
        v = v_ref[0, pl.ds(k0, keys)]
        sub = min(rows, 256)
        units = [(h, b) for b in range(rows // sub) for h in range(2)]

        def scores(h, b):
            q = q_ref[0, pl.ds(r0 + b * sub, sub)]
            sc = nt(jnp.where(lanes_of(h, q.shape), q, jnp.zeros_like(q)), k)
            if masked:
                allowed = column(seg_ref[pl.ds(s, 1), pl.ds(half_ref[0] * R + r0 + b * sub, sub)]) == seg_ref[pl.ds(s, 1), pl.ds(k0, keys)].astype(F32)
                sc = jnp.where(allowed, sc, -1e30)
            return sc

        ahead = scores(*units[0])
        outs = []
        for i, (h, b) in enumerate(units):
            sc = ahead
            if i + 1 < len(units):
                ahead = scores(*units[i + 1])
            m = jnp.max(sc, axis=-1, keepdims=True)
            p = jnp.exp2(sc - m)
            l = jnp.sum(p, axis=-1, keepdims=True)
            outs.append(nn(p.astype(BF), v) * (1.0 / l))
            lse = jnp.broadcast_to(m + jnp.log2(l), (sub, 128))
            lse_ref[0, 0, pl.ds(h, 1), pl.ds(r0 + b * sub, sub)] = lse.T[0:1]
            if h == 1:
                o_ref[0, pl.ds(r0 + b * sub, sub)] = jnp.where(lanes_of(0, outs[0].shape), outs[0], outs[1]).astype(BF)
                outs = []

    @pl.when(single)
    def _():
        attend(0, R, 0, L, False)

    @pl.when(jnp.logical_not(single))
    def _():
        def sub(i, carry):
            lo, n = window(seg, s, half_ref[0] * (R // blk) + i, blk, blk, count)
            r0 = pl.multiple_of(i * blk, blk)
            k0 = pl.multiple_of(lo * blk, blk)
            for m in range(1, count + 1):
                @pl.when(n == m)
                def _():
                    attend(r0, blk, k0, m * blk, True)
            return carry
        lax.fori_loop(0, R // blk, sub, 0)

def att_call(seg, half_index, q, k, v, blk=256):
    S, L, W = q.shape
    R = L // 2
    P = W // 128
    sd = jax.ShapeDtypeStruct
    return pl.pallas_call(functools.partial(att_kernel, blk),
        grid_spec=pltpu.PrefetchScalarGridSpec(num_scalar_prefetch=2, grid=(S, P),
            in_specs=[pl.BlockSpec((1, R, 128), lambda s, p, seg, h: (s, h[0], p)),
                pl.BlockSpec((1, L, 128), lambda s, p, seg, h: (s, 0, p)), pl.BlockSpec((1, L, 128), lambda s, p, seg, h: (s, 0, p)),
                pl.BlockSpec((S, L), lambda s, p, seg, h: (0, 0))],
            out_specs=[pl.BlockSpec((1, R, 128), lambda s, p, seg, h: (s, 0, p)),
                pl.BlockSpec((1, 1, 2, R), lambda s, p, seg, h: (s, p, 0, 0))]),
        out_shape=[sd((S, R, W), BF), sd((S, P, 2, R), F32)],
        compiler_params=pltpu.CompilerParams(dimension_semantics=("arbitrary", "arbitrary"), vmem_limit_bytes=VMEM_LIMIT),
        cost_estimate=pl.CostEstimate(flops=8 * 10**9, bytes_accessed=8 * 10**6, transcendentals=8 * 10**6),
        name="attend")(seg, half_index, q, k, v, seg)

def back_kernel(blk, s, seg, half_ref, ids, q_ref, k_ref, v_ref, dom_ref, doo_ref, om_ref, oo_ref, lsem_ref, lseo_ref, seg_ref,
        cos_ref, sin_ref, low_ref, up_ref, nm_hbm, *rest):
    gpm_ref, gpo_ref, pay_ref, lgm_ref, lgo_ref, dq_acc, dk_acc, dv_acc, lg_acc, nm_ref, sem = rest[-11:]
    pair = pl.program_id(0)
    L = q_ref.shape[1]
    R = L // 2
    count = L // blk
    single = seg[s, 0] == seg[s, L - 1]
    mine = half_ref[0]
    dk_acc[...] = jnp.zeros_like(dk_acc)
    dv_acc[...] = jnp.zeros_like(dv_acc)
    fetch = pltpu.make_async_copy(nm_hbm.at[s], nm_ref, sem)

    @pl.when(pair == 0)
    def _():
        fetch.start()

    def part(do_ref, o_ref, lse_ref, n0, r0, rows, k0, keys):
        q = q_ref[0, pl.ds(n0, rows)]
        do = do_ref[0, pl.ds(r0, rows)]
        o = o_ref[0, pl.ds(r0, rows)]
        k = k_ref[0, pl.ds(k0, keys)]
        v = v_ref[0, pl.ds(k0, keys)]
        prod = (do.astype(F32) * o.astype(F32)).T
        zero = jnp.zeros_like(q)
        ps, dss, dos, qs, ks = [], [], [], [], []
        for h in range(2):
            qh = jnp.where(lanes_of(h, q.shape), q, zero)
            doh = jnp.where(lanes_of(h, q.shape), do, zero)
            kh = jnp.where(lanes_of(h, k.shape), k, jnp.zeros_like(k))
            delta = jnp.sum(prod[h * 64:(h + 1) * 64], axis=0, keepdims=True)
            lse = lse_ref[0, 0, pl.ds(h, 1), pl.ds(r0, rows)]
            st = nt(k, qh)
            p = jnp.exp2(st - lse)
            ds = p * (nt(v, doh) - delta)
            ps.append(p.astype(BF)); dss.append(ds.astype(BF)); dos.append(doh); qs.append(qh); ks.append(kh)
        dv_acc[pl.ds(k0, keys)] += nn(jnp.concatenate(ps, 1), jnp.concatenate(dos, 0))
        dk_acc[pl.ds(k0, keys)] += nn(jnp.concatenate(dss, 1), jnp.concatenate(qs, 0))
        dq_acc[pl.ds(n0, rows)] = tn(jnp.concatenate(dss, 0), jnp.concatenate(ks, 0))

    def masked_part(do_ref, o_ref, lse_ref, n0, r0, rows, k0, keys):
        def products(h):
            q = q_ref[0, pl.ds(n0, rows)]
            do = do_ref[0, pl.ds(r0, rows)]
            qh = jnp.where(lanes_of(h, q.shape), q, jnp.zeros_like(q))
            doh = jnp.where(lanes_of(h, q.shape), do, jnp.zeros_like(q))
            st = nt(k_ref[0, pl.ds(k0, keys)], qh)
            dp = nt(v_ref[0, pl.ds(k0, keys)], doh)
            return st, dp, qh, doh

        ahead = products(0)
        for h in range(2):
            st, dp, qh, doh = ahead
            if h == 0:
                ahead = products(1)
            k = k_ref[0, pl.ds(k0, keys)]
            kh = jnp.where(lanes_of(h, k.shape), k, jnp.zeros_like(k))
            if h == 0:
                prod = (do_ref[0, pl.ds(r0, rows)].astype(F32) * o_ref[0, pl.ds(r0, rows)].astype(F32)).T
                allowed = column(seg_ref[s:s + 1, pl.ds(k0, keys)]) == seg_ref[s:s + 1, pl.ds(n0, rows)].astype(F32)
            delta = jnp.sum(prod[h * 64:(h + 1) * 64], axis=0, keepdims=True)
            p = jnp.where(allowed, jnp.exp2(st - lse_ref[0, 0, pl.ds(h, 1), pl.ds(r0, rows)]), 0.0)
            ds = (p * (dp - delta)).astype(BF)
            dv_acc[pl.ds(k0, keys)] += nn(p.astype(BF), doh)
            dk_acc[pl.ds(k0, keys)] += nn(ds, qh)
            dq = tn(ds, kh)
            if h == 0:
                dq0 = dq
            else:
                dq_acc[pl.ds(n0, rows)] = dq0 + dq

    halves = ((dom_ref, om_ref, lsem_ref, mine), (doo_ref, oo_ref, lseo_ref, 1 - mine))

    @pl.when(single)
    def _():
        for do_ref, o_ref, lse_ref, h in halves:
            part(do_ref, o_ref, lse_ref, pl.multiple_of(h * R, R), 0, R, 0, L)

    @pl.when(jnp.logical_not(single))
    def _():
        for do_ref, o_ref, lse_ref, h in halves:
            lo, n = window(seg, s, h, R, blk, count)
            for m in (count - 1, count):
                @pl.when(n == m)
                def _():
                    masked_part(do_ref, o_ref, lse_ref, pl.multiple_of(h * R, R), 0, R, pl.multiple_of(lo * blk, blk), m * blk)

            @pl.when(n < count - 1)
            def _():
                def sub(i, carry):
                    lo, n = window(seg, s, h * (R // blk) + i, blk, blk, count)
                    r0 = pl.multiple_of(i * blk, blk)
                    n0 = pl.multiple_of(h * R + i * blk, blk)
                    k0 = pl.multiple_of(lo * blk, blk)
                    for m in range(1, count - 1):
                        @pl.when(n == m)
                        def _():
                            masked_part(do_ref, o_ref, lse_ref, n0, r0, blk, k0, m * blk)
                    return carry
                lax.fori_loop(0, R // blk, sub, 0)

    cos, sin = cos_ref[...], sin_ref[...]
    def unrotate(g, factor):
        g = g * factor
        return (g * cos - swap(g) * sin).astype(BF)
    W = gpm_ref.shape[3] * pl.num_programs(0)
    grads = (unrotate(dq_acc[...], 0.125), unrotate(dk_acc[...], 1.0 / LOG2E), dv_acc[...].astype(BF))
    for h in range(2):
        @pl.when(mine == h)
        def _():
            for b, g in enumerate(grads):
                gpm_ref[0, b] = g[h * R:(h + 1) * R]
                gpo_ref[0, b] = g[(1 - h) * R:(2 - h) * R]
    grads = jnp.concatenate(grads, 1)
    lgs = nt(grads, jnp.concatenate([up_ref[0, b] for b in range(3)], 1))
    ups = tn(low_ref[0], grads).astype(BF)
    for b in range(3):
        pay_ref[0, :, pl.ds(pl.multiple_of(b * W + pair * 128, 128), 128)] = ups[:, b * 128:(b + 1) * 128]

    @pl.when(pair == 0)
    def _():
        lg_acc[...] = lgs

    @pl.when(pair > 0)
    def _():
        lg_acc[...] += lgs

    @pl.when(pair == pl.num_programs(0) - 1)
    def _():
        fetch.wait()
        D = nm_ref.shape[1]
        o = pay_ref.shape[2] - 128 - D
        pay_ref[0, :, o:o + D] = tn(lg_acc[...].astype(BF), nm_ref[...]).astype(BF)
        lane = lax.broadcasted_iota(jnp.int32, (lg_acc.shape[1], 128), 1)
        pay_ref[0, :, o + D:] = jnp.where(lane == ids[s], 1.0, 0.0).astype(BF)
        lgm_ref[0] = lg_acc[pl.ds(pl.multiple_of(mine * R, R), R)]
        lgo_ref[0] = lg_acc[pl.ds(pl.multiple_of((1 - mine) * R, R), R)]

def back_call(s, seg, half_index, ids, q, k, v, dom, doo, om, oo, lsem, lseo, cos, sin, low, up, nm, before=None, blk=256):
    S, L, W = q.shape
    R = L // 2
    P = W // 128
    rank = low.shape[2]
    sd = jax.ShapeDtypeStruct
    full = pl.BlockSpec((1, L, 128), lambda p, *_: (s, 0, p))
    hlf = pl.BlockSpec((1, R, 128), lambda p, *_: (s, 0, p))
    ls = pl.BlockSpec((1, 1, 2, R), lambda p, *_: (s, p, 0, 0))
    tb = pl.BlockSpec((L, 128), lambda p, *_: (0, 0))
    gp = pl.BlockSpec((1, 3, R, 128), lambda p, *_: (0, 0, 0, p))
    lg = pl.BlockSpec((1, R, rank), lambda p, *_: (0, 0, 0))
    pay = 3 * W + nm.shape[2] + 128
    any_ = pl.BlockSpec(memory_space=pl.ANY)
    args = [seg, half_index, ids, q, k, v, dom, doo, om, oo, lsem, lseo, seg, cos, sin, low, up, nm]
    alias = {}
    if before is not None:
        alias[len(args)] = 2
        args.append(before)
    return pl.pallas_call(functools.partial(back_kernel, blk, s),
        grid_spec=pltpu.PrefetchScalarGridSpec(num_scalar_prefetch=3, grid=(P,),
            in_specs=[full, full, full, hlf, hlf, hlf, hlf, ls, ls, pl.BlockSpec((S, L), lambda p, *_: (0, 0)),
                tb, tb, pl.BlockSpec((1, L, rank), lambda p, *_: (s, 0, 0)),
                pl.BlockSpec((1, 3, rank, 128), lambda p, seg, h, ids: (ids[s], 0, 0, p)), any_] + [any_] * len(alias),
            out_specs=[gp, gp, pl.BlockSpec((1, rank, pay), lambda p, *_: (s, 0, 0)), lg, lg],
            scratch_shapes=[pltpu.VMEM((L, 128), F32)] * 3 + [pltpu.VMEM((L, rank), F32), pltpu.VMEM(nm.shape[1:], BF), pltpu.SemaphoreType.DMA]),
        out_shape=[sd((1, 3, R, W), BF), sd((1, 3, R, W), BF), sd((S, rank, pay), BF), sd((1, R, rank), F32), sd((1, R, rank), F32)],
        input_output_aliases=alias,
        compiler_params=pltpu.CompilerParams(dimension_semantics=("arbitrary",), vmem_limit_bytes=VMEM_LIMIT),
        cost_estimate=pl.CostEstimate(flops=18 * 10**9, bytes_accessed=10**7, transcendentals=8 * 10**6),
        name="attend_back")(*args)

def final_kernel(ids, x_ref, gain_ref, wo_ref, wr_ref, ad_ref, mid_ref, gm_ref, gr_ref, lm_ref, lr_ref, *rest):
    gn = nn((lm_ref[0] + lr_ref[0]).astype(BF), ad_ref[0])
    for b in range(3):
        gn += nt(gm_ref[0, b], wo_ref[b]) + nt(gr_ref[0, b], wr_ref[b])
    c, rstd = norm_stats(x_ref[0].astype(F32))
    rest[-1][0] = mid_ref[0] + norm_back(gn, c, rstd, gain_ref[...].astype(F32)[None, :])

def final_call(s, ids, x, gain, w_own, w_its, ad, mid, parts, before=None, rows=256):
    S, R, D = x.shape
    W = w_own.shape[2]
    rank = ad.shape[1]
    wsp = pl.BlockSpec((3, D, W), lambda i, ids: (0, 0, 0))
    row = pl.BlockSpec((1, rows, D), lambda i, ids: (s, i, 0))
    gp = pl.BlockSpec((1, 3, rows, W), lambda i, ids: (0, 0, i, 0))
    lg = pl.BlockSpec((1, rows, rank), lambda i, ids: (0, i, 0))
    in_specs = [row, pl.BlockSpec((D,), lambda i, ids: (0,)), wsp, wsp, pl.BlockSpec((1, rank, D), lambda i, ids: (ids[s], 0, 0)), row,
        gp, gp, lg, lg]
    args = [ids, x, gain, w_own, w_its, ad, mid, *parts]
    alias = {}
    if before is not None:
        alias[len(args)] = 0
        args.append(before)
        in_specs.append(pl.BlockSpec(memory_space=pl.ANY))
    return pl.pallas_call(final_kernel,
        grid_spec=pltpu.PrefetchScalarGridSpec(num_scalar_prefetch=1, grid=(R // rows,), in_specs=in_specs, out_specs=row),
        out_shape=jax.ShapeDtypeStruct((S, R, D), F32),
        input_output_aliases=alias,
        compiler_params=pltpu.CompilerParams(dimension_semantics=("arbitrary",), vmem_limit_bytes=VMEM_LIMIT),
        cost_estimate=pl.CostEstimate(flops=4 * 10**9, bytes_accessed=10**7, transcendentals=10**4),
        name="final")(*args)

def unpack_kernel(in_ref, up_ref, down_ref):
    rank = in_ref.shape[0]
    W = up_ref.shape[3]
    for r in range(rank):
        for b in range(3):
            up_ref[:, b, r, :] = in_ref[r, :, b * W:(b + 1) * W].astype(F32)
        down_ref[:, r, :] = in_ref[r, :, 3 * W:].astype(F32)

def unpack_call(shares, W, D):
    rank, adapters, _ = shares.shape
    vm = pl.BlockSpec(memory_space=pltpu.VMEM)
    return pl.pallas_call(unpack_kernel, in_specs=[vm], out_specs=[vm, vm],
        out_shape=[jax.ShapeDtypeStruct((adapters, 3, rank, W), F32), jax.ShapeDtypeStruct((adapters, rank, D), F32)],
        compiler_params=pltpu.CompilerParams(vmem_limit_bytes=VMEM_LIMIT),
        cost_estimate=pl.CostEstimate(flops=10**6, bytes_accessed=2 * 10**6, transcendentals=0),
        name="unpack")(shares)


def unpack_units_kernel(at_ref, in_ref, iu_ref, md_ref, od_ref, *tables):
    rank = in_ref.shape[0]
    half = od_ref.shape[2]
    ffh = md_ref.shape[2]
    main = ffh // 256 * 256
    tail = ffh - main
    own_first = at_ref[0] == 0
    for r in range(rank):
        row = lambda a, n: in_ref[r, :, a:a + n].astype(F32)
        o = 3 * main + half
        ends = row(o + 6 * half, 3 * tail)
        for i in range(3):
            unit = jnp.concatenate([row(i * main, main), ends[:, i * tail:(i + 1) * tail]], 1)
            if i < 2:
                iu_ref[:, r, i, :] = unit
            else:
                md_ref[:, r, :] = unit
        od_ref[:, r, :] = row(3 * main, half)
        for i, ref in enumerate(tables):
            own, got = row(o + i * half, half), row(o + (3 + i) * half, half)
            ref[:, r, :half] = jnp.where(own_first, own, got)
            ref[:, r, half:] = jnp.where(own_first, got, own)

def unpack_units_call(at, shares, half, ffh):
    rank, adapters, _ = shares.shape
    vm = pl.BlockSpec(memory_space=pltpu.VMEM)
    sd = lambda *sh: jax.ShapeDtypeStruct((adapters, rank) + sh, F32)
    return pl.pallas_call(unpack_units_kernel, in_specs=[pl.BlockSpec(memory_space=pltpu.SMEM), vm], out_specs=[vm] * 6,
        out_shape=[sd(2, ffh), sd(ffh), sd(half)] + [sd(2 * half)] * 3,
        compiler_params=pltpu.CompilerParams(vmem_limit_bytes=VMEM_LIMIT),
        cost_estimate=pl.CostEstimate(flops=10**6, bytes_accessed=6 * 10**6, transcendentals=0),
        name="unpack_units")(at, shares)


HEAD_DIM = 64
ROPE_BASE = 160000.0


def rotary_tables(length):
    inverse = 1.0 / ROPE_BASE ** (np.arange(0, HEAD_DIM, 2) / HEAD_DIM)
    angles = np.arange(length)[:, None] * inverse[None, :]
    cos, sin = np.cos(angles), np.sin(angles)
    return (
        jnp.asarray(np.concatenate([cos, cos, cos, cos], 1), F32),
        jnp.asarray(np.concatenate([-sin, sin, -sin, sin], 1), F32),
    )


def spread(packed, tag_at, tags, groups, shards):
    S, rank, m = packed.shape
    if shards != rank:
        flat = [packed[:, :, a:b].reshape(S, shards, -1) for a, b in groups]
        packed = jnp.concatenate(flat + [jnp.broadcast_to(packed[:, :1, tag_at:tag_at + tags], (S, shards, tags))], -1)
        tag_at = packed.shape[2] - tags
    got = lax.all_to_all(packed, "dp", 1, 1, tiled=True).reshape(S * shards, -1)
    sums = lax.dot_general(got[:, tag_at:tag_at + tags], got, (((0,), (0,)), ((), ())), preferred_element_type=F32)
    if shards != rank:
        return sums[:, :tag_at]
    return jnp.concatenate([sums[:, a:b] for a, b in groups], -1)


def collect(shares, shards):
    wide = jnp.broadcast_to(shares.astype(BF), (shards,) + shares.shape)
    return lax.all_to_all(wide, "dp", 0, 0, tiled=True)


def body(x, cotangent, norm_in, norm_mid, w_qkv, w_out, w_in, w_ff, qkv_down, qkv_up, out_down, out_up, in_down, in_up,
         mlp_down, ff_up, segs, ids):
    other = lambda a: lax.ppermute(a, "tensor", [(0, 1), (1, 0)])
    tie = lax.optimization_barrier
    t = lax.axis_index("tensor")
    shards = lax.axis_size("dp")
    mine, its = t.astype(jnp.int32).reshape(1), (1 - t).astype(jnp.int32).reshape(1)
    S, R, D = x.shape
    L = segs.shape[1]
    x_its = other(x)
    w_qkv = w_qkv.transpose(1, 0, 2)
    w_in = w_in.transpose(1, 2, 0)
    qkv_down, out_down, in_down, mlp_down = (a.transpose(0, 2, 1) for a in (qkv_down, out_down, in_down, mlp_down))
    qkv_up, in_up = qkv_up.transpose(0, 2, 1, 3), in_up.transpose(0, 2, 1, 3)
    gain_in, gain_mid = norm_in, norm_mid
    half = w_out.shape[0]
    ffh = w_ff.shape[0]
    main = ffh // 256 * 256
    tail = ffh - main
    rank = out_up.shape[1]
    adapters = out_up.shape[0]

    w_out_its, w_in_its, w_ff_its, w_qkv_its = other(w_out), other(w_in), other(w_ff), other(w_qkv)
    out_down_its, in_up_its, mlp_down_its = other(out_down), other(in_up), other(mlp_down)

    cos, sin = rotary_tables(L)
    first = qkv_call(ids, mine, x, gain_in, w_qkv, qkv_down, qkv_up, cos, sin)
    q, k, v, low, normed = qkv_call(ids, its, x_its, gain_in, w_qkv, qkv_down, qkv_up, cos, sin, before=first)
    ctx_its, lse_its = att_call(segs, its, q, k, v)
    ctx_got = other(ctx_its)
    ctx_mine, lse_mine = att_call(segs, mine, q, k, v)
    output, grad_mid, gc_mine, gc_its, keep, send = mlp_call(
        ids, mine, x, ctx_mine, ctx_got, cotangent, gain_mid, out_down, out_down_its, in_up, in_up_its, mlp_down, mlp_down_its,
        out_up, in_down, ff_up, w_out, w_out_its, w_in, w_in_its, w_ff, w_ff_its)
    gc_got = other(gc_its)

    packed = (keep + other(send).astype(F32)).astype(BF)
    lanes = 3 * main + 4 * half
    units = lanes - 3 * half
    shares = spread(packed, lanes + 3 * tail, adapters, ((0, units), (units, lanes), (lanes, lanes + 3 * tail)), shards)

    back = lambda s, gc_got, before=None: back_call(
        s, segs, mine, ids, q, k, v, gc_mine, gc_got, ctx_mine, ctx_its, lse_mine, lse_its, cos, sin, low, qkv_up, normed, before)
    gp_mine0, gp_its0, packed, lg_mine0, lg_its0 = back(0, gc_got)
    gp_got0, lg_got0 = other(gp_its0), other(lg_its0)
    shares, packed = tie((shares.astype(BF), packed))
    c0, c1 = rank * units // shards, rank * lanes // shards
    halves = shares[:, c0:c1]
    sums = collect(jnp.concatenate([shares[:, :c1], other(halves), shares[:, c1:]], -1), shards)
    gp_mine1, gp_its1, packed, lg_mine1, lg_its1 = back(1, gc_got, packed)
    sums, packed = tie((sums, packed))
    gp_got1, lg_got1 = other(gp_its1), other(lg_its1)
    m = packed.shape[2] - 128
    shares = spread(packed, m, adapters, ((0, m - D), (m - D, m)), shards)
    grad_input = final_call(0, ids, x, gain_in, w_qkv, w_qkv_its, qkv_down, grad_mid, (gp_mine0, gp_got0, lg_mine0, lg_got0))
    shares, grad_input = tie((shares, grad_input))
    cut = rank * (m - D) // shards
    downs = shares[:, cut:]
    shares = jnp.concatenate([shares[:, :cut], downs + other(downs)], -1)
    shares, sums, gp_got1 = tie((shares, sums, gp_got1))
    qsums = collect(shares, shards)
    grad_input = final_call(1, ids, x, gain_in, w_qkv, w_qkv_its, qkv_down, grad_mid, (gp_mine1, gp_got1, lg_mine1, lg_got1), grad_input)

    whole = lambda a: a.transpose(1, 0, 2).reshape(adapters, rank, -1)
    if shards == rank:
        g_in_up, g_mlp_down, g_out_down, g_ff_up, g_in_down, g_out_up = unpack_units_call(mine, sums, half, ffh)
    else:
        a, own, got, b = (whole(z) for z in jnp.split(sums, (c0, c1, 2 * c1 - c0), axis=2))
        unit = lambda i: jnp.concatenate([a[..., i * main:(i + 1) * main], b[..., i * tail:(i + 1) * tail]], -1).astype(F32)
        g_in_up, g_mlp_down = jnp.stack([unit(0), unit(1)], 2), unit(2)
        g_out_down = a[..., 3 * main:].astype(F32)
        lo, hi = jnp.where(t == 0, own, got), jnp.where(t == 0, got, own)
        g_ff_up, g_in_down, g_out_up = (
            jnp.concatenate([lo[..., i * half:(i + 1) * half], hi[..., i * half:(i + 1) * half]], -1).astype(F32) for i in range(3))
    g_mlp_down, g_out_down = g_mlp_down.transpose(0, 2, 1), g_out_down.transpose(0, 2, 1)
    if shards == rank:
        g_qkv_up, g_qkv_down = unpack_call(qsums, (m - D) // 3, D)
    else:
        g_qkv_up = whole(qsums[..., :cut]).astype(F32).reshape(adapters, rank, 3, -1).transpose(0, 2, 1, 3)
        g_qkv_down = whole(qsums[..., cut:]).astype(F32)
    g_qkv_up, g_qkv_down = g_qkv_up.transpose(0, 2, 1, 3), g_qkv_down.transpose(0, 2, 1)
    return (output, grad_input, g_qkv_down, g_qkv_up, g_out_down, g_out_up, g_in_down.transpose(0, 2, 1), g_in_up, g_mlp_down, g_ff_up)


def solution(mesh):
    return jax.shard_map(
        body,
        mesh=mesh,
        in_specs=(
            P("dp", "tensor", None),
            P("dp", "tensor", None),
            P(),
            P(),
            P(None, None, "tensor"),
            P("tensor", None),
            P(None, None, "tensor"),
            P("tensor", None),
            P(),
            P(None, None, None, "tensor"),
            P(None, "tensor", None),
            P(),
            P(),
            P(None, None, None, "tensor"),
            P(None, "tensor", None),
            P(),
            P("dp", None),
            P("dp"),
        ),
        out_specs=(
            P("dp", "tensor", None),
            P("dp", "tensor", None),
            P(),
            P(None, None, None, "tensor"),
            P(None, "tensor", None),
            P(),
            P(),
            P(None, None, None, "tensor"),
            P(None, "tensor", None),
            P(),
        ),
        check_vma=False,
    )
```

```python
import functools
import math

import jax
import jax.numpy as jnp
import numpy as np
from jax import lax
from jax.experimental import pallas as pl
from jax.experimental.pallas import tpu as pltpu
from jax.sharding import PartitionSpec as P

F32, BF = jnp.float32, jnp.bfloat16
EPS = 1e-05
VMEM_LIMIT = 65280 * 1024

def nn(a, b): return lax.dot_general(a, b, (((1,), (0,)), ((), ())), preferred_element_type=F32)
def nt(a, b): return lax.dot_general(a, b, (((1,), (1,)), ((), ())), preferred_element_type=F32)
def tn(a, b): return lax.dot_general(a, b, (((0,), (0,)), ((), ())), preferred_element_type=F32)

def norm_stats(v):
    mean = jnp.mean(v, axis=-1, keepdims=True)
    c = v - mean
    var = jnp.mean(c * c, axis=-1, keepdims=True)
    return c, lax.rsqrt(var + EPS)

def norm_back(e, c, rstd, gain):
    n = c * rstd
    h = e * gain
    return (h - jnp.mean(h, axis=-1, keepdims=True) - n * jnp.mean(h * n, axis=-1, keepdims=True)) * rstd

def mlp_kernel(chunk, main, tail,
        ids, at_ref, x_ref, cm_ref, cr_ref, g_ref, gain_ref,
        od_own, od_its, iu_own, iu_its, md_own, md_its, ou_ref, id_ref, fu_ref,
        wo_own, wo_its, wi_own, wi_its, wf_own, wf_its,
        out_ref, gmid_ref, gcm_ref, gci_ref, pack_ref,
        wo, wi, wf, acc_o, acc_n, acc_lm, acc_li, nm_ref, mid_ref, iu, md, d_iu, d_md, d_w, sem):
    s = pl.program_id(0)
    half = wo_own.shape[0]
    rank = ou_ref.shape[1]
    copies = []
    def cp(src, dst):
        copies.append(pltpu.make_async_copy(src, dst, sem.at[len(copies)]))
    cp(wo_own, wo.at[pl.ds(0, half)])
    cp(wo_its, wo.at[pl.ds(half, half)])
    for j, (wi_h, wf_h) in enumerate(((wi_own, wf_own), (wi_its, wf_its))):
        for b in range(2):
            cp(wi_h.at[b, pl.ds(0, main)], wi.at[b, pl.ds(j * main, main)])
        cp(wf_h.at[pl.ds(0, main)], wf.at[pl.ds(j * main, main)])
        for b in range(2):
            cp(wi_h.at[b, pl.ds(main, tail)], wi.at[b, pl.ds(2 * main + j * tail, tail)])
        cp(wf_h.at[pl.ds(main, tail)], wf.at[pl.ds(2 * main + j * tail, tail)])

    @pl.when(s == 0)
    def _():
        for c in copies: c.start()
        for c in copies[:2]: c.wait()

    for dst, own, its in ((iu.at[0], iu_own[0, 0], iu_its[0, 0]), (iu.at[1], iu_own[0, 1], iu_its[0, 1]), (md, md_own[0], md_its[0])):
        dst[:, :main] = own[:, :main]
        dst[:, main:2 * main] = its[:, :main]
        dst[:, 2 * main:] = jnp.concatenate([own[:, main:].astype(F32), its[:, main:].astype(F32)], 1).astype(BF)

    cm, cr = cm_ref[0], cr_ref[0]
    odo, odi = od_own[0], od_its[0]
    ou = ou_ref[0]
    low_out = (nt(cm, odo) + nt(cr, odi)).astype(BF)
    att = nn(cm, wo[0:half]) + nn(cr, wo[half:]) + nn(low_out, ou)
    middle = x_ref[0].astype(F32) + att
    mid_ref[...] = middle
    c, rstd = norm_stats(middle)
    gain = gain_ref[...].astype(F32)[None, :]
    nm = (c * rstd * gain).astype(BF)
    nm_ref[...] = nm
    g = g_ref[0]
    low_in = nt(nm, id_ref[0]).astype(BF)
    glm = nt(g, fu_ref[0]).astype(BF)
    acc_o[...] = jnp.zeros_like(acc_o)
    acc_n[...] = jnp.zeros_like(acc_n)
    acc_lm[...] = jnp.zeros_like(acc_lm)
    acc_li[...] = jnp.zeros_like(acc_li)

    @pl.when(s == 0)
    def _():
        for c_ in copies[2:]: c_.wait()

    def step(first, size):
        rows = pl.ds(first, size)
        nm = nm_ref[...]
        g = g_ref[0]
        w0, w1, wfc = wi[0, rows], wi[1, rows], wf[rows]
        iu0, iu1, mdc = iu[0, :, rows], iu[1, :, rows], md[:, rows]
        u = nt(nm, w0) + nn(low_in, iu0)
        v = nt(nm, w1) + nn(low_in, iu1)
        gh = nt(g, wfc) + nn(glm, mdc)
        cdf = 0.5 * (1.0 + lax.erf(u * (1.0 / math.sqrt(2.0))))
        pdf = jnp.exp(-0.5 * u * u) * (1.0 / math.sqrt(2.0 * math.pi))
        gel = u * cdf
        h = (gel * v).astype(BF)
        gu = (gh * v * (cdf + u * pdf)).astype(BF)
        gv = (gh * gel).astype(BF)
        acc_o[...] += nn(h, wfc)
        acc_n[...] += nn(gu, w0) + nn(gv, w1)
        acc_lm[...] += nt(h, mdc)
        acc_li[...] += nt(gu, iu0) + nt(gv, iu1)
        d_iu[0, :, rows] = tn(low_in, gu)
        d_iu[1, :, rows] = tn(low_in, gv)
        d_md[:, rows] = tn(glm, h)

    def loop(i, carry):
        step(pl.multiple_of(i * chunk, chunk), chunk)
        return carry
    lax.fori_loop(0, 2 * main // chunk, loop, 0)
    step(2 * main, 2 * tail)

    fu = fu_ref[0]
    low_mlp = acc_lm[...].astype(BF)
    out_ref[0] = (mid_ref[...] + acc_o[...] + nn(low_mlp, fu)).astype(BF)
    g = g_ref[0]
    d_w[0] = tn(low_mlp, g)
    gli = acc_li[...].astype(BF)
    d_w[1] = tn(gli, nm_ref[...])
    gnm = acc_n[...] + nn(gli, id_ref[0])
    c, rstd = norm_stats(mid_ref[...])
    gmid = g.astype(F32) + norm_back(gnm, c, rstd, gain)
    gmid_ref[0] = gmid
    ga = gmid.astype(BF)
    glo = nt(ga, ou).astype(BF)
    d_w[2] = tn(low_out, ga)
    gcm_ref[0] = (nt(ga, wo[0:half]) + nn(glo, odo)).astype(BF)
    gci_ref[0] = (nt(ga, wo[half:]) + nn(glo, odi)).astype(BF)

    size = pack_ref.shape[2] // 2
    sides = ((pack_ref.at[:, :, :size], 0, at_ref[0], cm, BF), (pack_ref.at[:, :, size:], 1, 1 - at_ref[0], cr, BF))
    for ref, j, at, ctx, kind in sides:
        parts = (d_iu.at[0], d_iu.at[1], d_md)
        for i, d in enumerate(parts):
            ref[0, :, i * main:(i + 1) * main] = d[:, j * main:(j + 1) * main].astype(kind)
        o = 3 * main
        ref[0, :, o:o + half] = tn(glo, ctx).astype(kind)
        o += half
        for i in range(3):
            ref[0, :, o:o + half] = d_w[i, :, pl.ds(pl.multiple_of(at * half, half), half)].astype(kind)
            o += half
        lane = lax.broadcasted_iota(jnp.int32, (rank, 128 - 3 * tail), 1)
        tag = jnp.where((lane == ids[s]) & (j == 0), 1.0, 0.0)
        ends = [d[:, 2 * main + j * tail:2 * main + (j + 1) * tail] for d in parts]
        ref[0, :, o:] = jnp.concatenate(ends + [tag], 1).astype(kind)


def mlp_call(ids, at, x, cm, cr, g, gain, od_own, od_its, iu_own, iu_its, md_own, md_its, ou, idn, fu,
             wo_own, wo_its, wi_own, wi_its, wf_own, wf_its, chunk=512):
    S, R, D = x.shape
    half = wo_own.shape[0]
    ffh = wf_own.shape[0]
    main = ffh // 256 * 256
    tail = ffh - main
    rank = ou.shape[1]
    ff = 2 * ffh
    packed = 3 * main + 4 * half + 128
    seq = lambda *bs: pl.BlockSpec((1,) + bs, lambda s, *_: (s,) + (0,) * len(bs))
    tab = lambda *bs: pl.BlockSpec((1,) + bs, lambda s, ids, at: (ids[s],) + (0,) * len(bs))
    any_ = pl.BlockSpec(memory_space=pl.ANY)
    in_specs = [seq(R, D), seq(R, half), seq(R, half), seq(R, D), pl.BlockSpec((D,), lambda s, *_: (0,)),
        tab(rank, half), tab(rank, half), tab(2, rank, ffh), tab(2, rank, ffh), tab(rank, ffh), tab(rank, ffh),
        tab(rank, D), tab(rank, D), tab(rank, D)] + [any_] * 6
    out_specs = [seq(R, D), seq(R, D), seq(R, half), seq(R, half), seq(rank, 2 * packed)]
    sd = jax.ShapeDtypeStruct
    out_shape = [sd((S, R, D), BF), sd((S, R, D), F32), sd((S, R, half), BF), sd((S, R, half), BF),
        sd((S, rank, 2 * packed), BF)]
    scratch = [pltpu.VMEM((2 * half, D), BF), pltpu.VMEM((2, ff, D), BF), pltpu.VMEM((ff, D), BF),
        pltpu.VMEM((R, D), F32), pltpu.VMEM((R, D), F32), pltpu.VMEM((R, rank), F32), pltpu.VMEM((R, rank), F32),
        pltpu.VMEM((R, D), BF), pltpu.VMEM((R, D), F32), pltpu.VMEM((2, rank, ff), BF), pltpu.VMEM((rank, ff), BF),
        pltpu.VMEM((2, rank, ff), F32), pltpu.VMEM((rank, ff), F32), pltpu.VMEM((3, rank, D), F32), pltpu.SemaphoreType.DMA((14,))]
    return pl.pallas_call(functools.partial(mlp_kernel, chunk, main, tail),
        grid_spec=pltpu.PrefetchScalarGridSpec(num_scalar_prefetch=2, grid=(S,), in_specs=in_specs, out_specs=out_specs, scratch_shapes=scratch),
        out_shape=out_shape,
        compiler_params=pltpu.CompilerParams(dimension_semantics=("arbitrary",), vmem_limit_bytes=VMEM_LIMIT),
        cost_estimate=pl.CostEstimate(flops=40 * 10**9, bytes_accessed=40 * 10**6, transcendentals=3 * 10**6),
        name="mlp")(ids, at, x, cm, cr, g, gain, od_own, od_its, iu_own, iu_its, md_own, md_its, ou, idn, fu,
                    wo_own, wo_its, wi_own, wi_its, wf_own, wf_its)


LOG2E = 1.4426950408889634
QUERY_SCALE = LOG2E / 8.0

def lanes_of(head, shape):
    return (lax.broadcasted_iota(jnp.int32, shape, len(shape) - 1) // 64) == head

def column(row):
    return jnp.broadcast_to(row.astype(F32), (8, row.shape[1])).T[:, :1]

def swap(u):
    lane = lax.broadcasted_iota(jnp.int32, u.shape, 1)
    return jnp.where((lane & 63) < 32, pltpu.roll(u, 96, 1), pltpu.roll(u, 32, 1))


def qkv_kernel(ids, half_ref, x_ref, gain_ref, w_ref, ad_ref, up_ref, cos_ref, sin_ref, *rest):
    q_ref, k_ref, v_ref, low_ref, nm_ref = rest[-5:]
    c, rstd = norm_stats(x_ref[0].astype(F32))
    nm = (c * rstd * gain_ref[...].astype(F32)[None, :]).astype(BF)
    nm_ref[0] = nm
    low = nt(nm, ad_ref[0]).astype(BF)
    low_ref[0] = low
    cos, sin = cos_ref[...], sin_ref[...]
    for b, ref in enumerate((q_ref, k_ref)):
        u = nn(nm, w_ref[b]) + nn(low, up_ref[0, b])
        if b == 0:
            u = u * QUERY_SCALE
        for p in range(u.shape[1] // 128):
            t = u[:, p * 128:(p + 1) * 128]
            ref[0, :, p * 128:(p + 1) * 128] = (t * cos + swap(t) * sin).astype(BF)
    v_ref[0] = (nn(nm, w_ref[2]) + nn(low, up_ref[0, 2])).astype(BF)

QKV_ROWS = 512


def qkv_call(ids, half_index, x, gain, w, ad, up, cos, sin, before=None, rows=None):
    S, R, D = x.shape
    W = w.shape[2]
    rank = ad.shape[1]
    L = cos.shape[0]
    rows = rows or QKV_ROWS
    n = R // rows
    tabl = lambda *bs: pl.BlockSpec((1,) + bs, lambda s, i, ids, h: (ids[s],) + (0,) * len(bs))
    turn = pl.BlockSpec((rows, 128), lambda s, i, ids, h: (h[0] * n + i, 0))
    in_specs = [pl.BlockSpec((1, rows, D), lambda s, i, ids, h: (s, i, 0)), pl.BlockSpec((D,), lambda s, i, ids, h: (0,)),
        pl.BlockSpec((3, D, W), lambda s, i, ids, h: (0, 0, 0)), tabl(rank, D), tabl(3, rank, W), turn, turn]
    args = [ids, half_index, x, gain, w, ad, up, cos, sin]
    alias = {}
    if before is not None:
        for i, b in enumerate(before):
            alias[len(args)] = i
            args.append(b)
            in_specs.append(pl.BlockSpec(memory_space=pl.ANY))
    out = lambda m: pl.BlockSpec((1, rows, m), lambda s, i, ids, h: (s, h[0] * n + i, 0))
    sd = jax.ShapeDtypeStruct
    return pl.pallas_call(qkv_kernel,
        grid_spec=pltpu.PrefetchScalarGridSpec(num_scalar_prefetch=2, grid=(S, n), in_specs=in_specs,
            out_specs=[out(W), out(W), out(W), out(rank), out(D)]),
        out_shape=[sd((S, L, W), BF)] * 3 + [sd((S, L, rank), BF), sd((S, L, D), BF)],
        input_output_aliases=alias,
        compiler_params=pltpu.CompilerParams(dimension_semantics=("arbitrary", "arbitrary"), vmem_limit_bytes=VMEM_LIMIT),
        cost_estimate=pl.CostEstimate(flops=5 * 10**9, bytes_accessed=10**7, transcendentals=10**5),
        name="qkv")(*args)

def window(seg, s, i, rows, blk, count):
    first, last = seg[s, i * rows], seg[s, i * rows + rows - 1]
    lo = jnp.int32(0); hi = jnp.int32(0)
    for j in range(count):
        lo += (seg[s, j * blk + blk - 1] < first).astype(jnp.int32)
        hi += (seg[s, j * blk] <= last).astype(jnp.int32)
    return lo, hi - lo

def att_kernel(blk, seg, half_ref, q_ref, k_ref, v_ref, seg_ref, o_ref, lse_ref):
    s = pl.program_id(0)
    R, L = q_ref.shape[1], k_ref.shape[1]
    count = L // blk
    single = seg[s, 0] == seg[s, L - 1]

    def attend(r0, rows, k0, keys, masked):
        k = k_ref[0, pl.ds(k0, keys)]
        v = v_ref[0, pl.ds(k0, keys)]
        sub = min(rows, 256)
        units = [(h, b) for b in range(rows // sub) for h in range(2)]

        def scores(h, b):
            q = q_ref[0, pl.ds(r0 + b * sub, sub)]
            sc = nt(jnp.where(lanes_of(h, q.shape), q, jnp.zeros_like(q)), k)
            if masked:
                allowed = column(seg_ref[pl.ds(s, 1), pl.ds(half_ref[0] * R + r0 + b * sub, sub)]) == seg_ref[pl.ds(s, 1), pl.ds(k0, keys)].astype(F32)
                sc = jnp.where(allowed, sc, -1e30)
            return sc

        ahead = scores(*units[0])
        outs = []
        for i, (h, b) in enumerate(units):
            sc = ahead
            if i + 1 < len(units):
                ahead = scores(*units[i + 1])
            m = jnp.max(sc, axis=-1, keepdims=True)
            p = jnp.exp2(sc - m)
            l = jnp.sum(p, axis=-1, keepdims=True)
            outs.append(nn(p.astype(BF), v) * (1.0 / l))
            lse = jnp.broadcast_to(m + jnp.log2(l), (sub, 128))
            lse_ref[0, 0, pl.ds(h, 1), pl.ds(r0 + b * sub, sub)] = lse.T[0:1]
            if h == 1:
                o_ref[0, pl.ds(r0 + b * sub, sub)] = jnp.where(lanes_of(0, outs[0].shape), outs[0], outs[1]).astype(BF)
                outs = []

    @pl.when(single)
    def _():
        attend(0, R, 0, L, False)

    @pl.when(jnp.logical_not(single))
    def _():
        def sub(i, carry):
            lo, n = window(seg, s, half_ref[0] * (R // blk) + i, blk, blk, count)
            r0 = pl.multiple_of(i * blk, blk)
            k0 = pl.multiple_of(lo * blk, blk)
            for m in range(1, count + 1):
                @pl.when(n == m)
                def _():
                    attend(r0, blk, k0, m * blk, True)
            return carry
        lax.fori_loop(0, R // blk, sub, 0)

def att_call(seg, half_index, q, k, v, blk=256):
    S, L, W = q.shape
    R = L // 2
    P = W // 128
    sd = jax.ShapeDtypeStruct
    return pl.pallas_call(functools.partial(att_kernel, blk),
        grid_spec=pltpu.PrefetchScalarGridSpec(num_scalar_prefetch=2, grid=(S, P),
            in_specs=[pl.BlockSpec((1, R, 128), lambda s, p, seg, h: (s, h[0], p)),
                pl.BlockSpec((1, L, 128), lambda s, p, seg, h: (s, 0, p)), pl.BlockSpec((1, L, 128), lambda s, p, seg, h: (s, 0, p)),
                pl.BlockSpec((S, L), lambda s, p, seg, h: (0, 0))],
            out_specs=[pl.BlockSpec((1, R, 128), lambda s, p, seg, h: (s, 0, p)),
                pl.BlockSpec((1, 1, 2, R), lambda s, p, seg, h: (s, p, 0, 0))]),
        out_shape=[sd((S, R, W), BF), sd((S, P, 2, R), F32)],
        compiler_params=pltpu.CompilerParams(dimension_semantics=("arbitrary", "arbitrary"), vmem_limit_bytes=VMEM_LIMIT),
        cost_estimate=pl.CostEstimate(flops=8 * 10**9, bytes_accessed=8 * 10**6, transcendentals=8 * 10**6),
        name="attend")(seg, half_index, q, k, v, seg)

def back_kernel(blk, s, seg, half_ref, ids, q_ref, k_ref, v_ref, dom_ref, doo_ref, om_ref, oo_ref, lsem_ref, lseo_ref, seg_ref,
        cos_ref, sin_ref, low_ref, up_ref, nm_hbm, *rest):
    gpm_ref, gpo_ref, pay_ref, lgm_ref, lgo_ref, dq_acc, dk_acc, dv_acc, lg_acc, nm_ref, sem = rest[-11:]
    pair = pl.program_id(0)
    L = q_ref.shape[1]
    R = L // 2
    count = L // blk
    single = seg[s, 0] == seg[s, L - 1]
    mine = half_ref[0]
    dk_acc[...] = jnp.zeros_like(dk_acc)
    dv_acc[...] = jnp.zeros_like(dv_acc)
    fetch = pltpu.make_async_copy(nm_hbm.at[s], nm_ref, sem)

    @pl.when(pair == 0)
    def _():
        fetch.start()

    def part(do_ref, o_ref, lse_ref, n0, r0, rows, k0, keys):
        q = q_ref[0, pl.ds(n0, rows)]
        do = do_ref[0, pl.ds(r0, rows)]
        o = o_ref[0, pl.ds(r0, rows)]
        k = k_ref[0, pl.ds(k0, keys)]
        v = v_ref[0, pl.ds(k0, keys)]
        prod = (do.astype(F32) * o.astype(F32)).T
        zero = jnp.zeros_like(q)
        ps, dss, dos, qs, ks = [], [], [], [], []
        for h in range(2):
            qh = jnp.where(lanes_of(h, q.shape), q, zero)
            doh = jnp.where(lanes_of(h, q.shape), do, zero)
            kh = jnp.where(lanes_of(h, k.shape), k, jnp.zeros_like(k))
            delta = jnp.sum(prod[h * 64:(h + 1) * 64], axis=0, keepdims=True)
            lse = lse_ref[0, 0, pl.ds(h, 1), pl.ds(r0, rows)]
            st = nt(k, qh)
            p = jnp.exp2(st - lse)
            ds = p * (nt(v, doh) - delta)
            ps.append(p.astype(BF)); dss.append(ds.astype(BF)); dos.append(doh); qs.append(qh); ks.append(kh)
        dv_acc[pl.ds(k0, keys)] += nn(jnp.concatenate(ps, 1), jnp.concatenate(dos, 0))
        dk_acc[pl.ds(k0, keys)] += nn(jnp.concatenate(dss, 1), jnp.concatenate(qs, 0))
        dq_acc[pl.ds(n0, rows)] = tn(jnp.concatenate(dss, 0), jnp.concatenate(ks, 0))

    def masked_part(do_ref, o_ref, lse_ref, n0, r0, rows, k0, keys):
        def products(h):
            q = q_ref[0, pl.ds(n0, rows)]
            do = do_ref[0, pl.ds(r0, rows)]
            qh = jnp.where(lanes_of(h, q.shape), q, jnp.zeros_like(q))
            doh = jnp.where(lanes_of(h, q.shape), do, jnp.zeros_like(q))
            st = nt(k_ref[0, pl.ds(k0, keys)], qh)
            dp = nt(v_ref[0, pl.ds(k0, keys)], doh)
            return st, dp, qh, doh

        ahead = products(0)
        for h in range(2):
            st, dp, qh, doh = ahead
            if h == 0:
                ahead = products(1)
            k = k_ref[0, pl.ds(k0, keys)]
            kh = jnp.where(lanes_of(h, k.shape), k, jnp.zeros_like(k))
            if h == 0:
                prod = (do_ref[0, pl.ds(r0, rows)].astype(F32) * o_ref[0, pl.ds(r0, rows)].astype(F32)).T
                allowed = column(seg_ref[s:s + 1, pl.ds(k0, keys)]) == seg_ref[s:s + 1, pl.ds(n0, rows)].astype(F32)
            delta = jnp.sum(prod[h * 64:(h + 1) * 64], axis=0, keepdims=True)
            p = jnp.where(allowed, jnp.exp2(st - lse_ref[0, 0, pl.ds(h, 1), pl.ds(r0, rows)]), 0.0)
            ds = (p * (dp - delta)).astype(BF)
            dv_acc[pl.ds(k0, keys)] += nn(p.astype(BF), doh)
            dk_acc[pl.ds(k0, keys)] += nn(ds, qh)
            dq = tn(ds, kh)
            if h == 0:
                dq0 = dq
            else:
                dq_acc[pl.ds(n0, rows)] = dq0 + dq

    halves = ((dom_ref, om_ref, lsem_ref, mine), (doo_ref, oo_ref, lseo_ref, 1 - mine))

    @pl.when(single)
    def _():
        for do_ref, o_ref, lse_ref, h in halves:
            part(do_ref, o_ref, lse_ref, pl.multiple_of(h * R, R), 0, R, 0, L)

    @pl.when(jnp.logical_not(single))
    def _():
        for do_ref, o_ref, lse_ref, h in halves:
            lo, n = window(seg, s, h, R, blk, count)
            for m in (count - 1, count):
                @pl.when(n == m)
                def _():
                    masked_part(do_ref, o_ref, lse_ref, pl.multiple_of(h * R, R), 0, R, pl.multiple_of(lo * blk, blk), m * blk)

            @pl.when(n < count - 1)
            def _():
                def sub(i, carry):
                    lo, n = window(seg, s, h * (R // blk) + i, blk, blk, count)
                    r0 = pl.multiple_of(i * blk, blk)
                    n0 = pl.multiple_of(h * R + i * blk, blk)
                    k0 = pl.multiple_of(lo * blk, blk)
                    for m in range(1, count - 1):
                        @pl.when(n == m)
                        def _():
                            masked_part(do_ref, o_ref, lse_ref, n0, r0, blk, k0, m * blk)
                    return carry
                lax.fori_loop(0, R // blk, sub, 0)

    cos, sin = cos_ref[...], sin_ref[...]
    def unrotate(g, factor):
        g = g * factor
        return (g * cos - swap(g) * sin).astype(BF)
    W = gpm_ref.shape[3] * pl.num_programs(0)
    grads = (unrotate(dq_acc[...], 0.125), unrotate(dk_acc[...], 1.0 / LOG2E), dv_acc[...].astype(BF))
    for h in range(2):
        @pl.when(mine == h)
        def _():
            for b, g in enumerate(grads):
                gpm_ref[0, b] = g[h * R:(h + 1) * R]
                gpo_ref[0, b] = g[(1 - h) * R:(2 - h) * R]
    grads = jnp.concatenate(grads, 1)
    lgs = nt(grads, jnp.concatenate([up_ref[0, b] for b in range(3)], 1))
    ups = tn(low_ref[0], grads).astype(BF)
    for b in range(3):
        pay_ref[0, :, pl.ds(pl.multiple_of(b * W + pair * 128, 128), 128)] = ups[:, b * 128:(b + 1) * 128]

    @pl.when(pair == 0)
    def _():
        lg_acc[...] = lgs

    @pl.when(pair > 0)
    def _():
        lg_acc[...] += lgs

    @pl.when(pair == pl.num_programs(0) - 1)
    def _():
        fetch.wait()
        D = nm_ref.shape[1]
        o = pay_ref.shape[2] - 128 - D
        pay_ref[0, :, o:o + D] = tn(lg_acc[...].astype(BF), nm_ref[...]).astype(BF)
        lane = lax.broadcasted_iota(jnp.int32, (lg_acc.shape[1], 128), 1)
        pay_ref[0, :, o + D:] = jnp.where(lane == ids[s], 1.0, 0.0).astype(BF)
        lgm_ref[0] = lg_acc[pl.ds(pl.multiple_of(mine * R, R), R)]
        lgo_ref[0] = lg_acc[pl.ds(pl.multiple_of((1 - mine) * R, R), R)]

def back_call(s, seg, half_index, ids, q, k, v, dom, doo, om, oo, lsem, lseo, cos, sin, low, up, nm, before=None, blk=256):
    S, L, W = q.shape
    R = L // 2
    P = W // 128
    rank = low.shape[2]
    sd = jax.ShapeDtypeStruct
    full = pl.BlockSpec((1, L, 128), lambda p, *_: (s, 0, p))
    hlf = pl.BlockSpec((1, R, 128), lambda p, *_: (s, 0, p))
    ls = pl.BlockSpec((1, 1, 2, R), lambda p, *_: (s, p, 0, 0))
    tb = pl.BlockSpec((L, 128), lambda p, *_: (0, 0))
    gp = pl.BlockSpec((1, 3, R, 128), lambda p, *_: (0, 0, 0, p))
    lg = pl.BlockSpec((1, R, rank), lambda p, *_: (0, 0, 0))
    pay = 3 * W + nm.shape[2] + 128
    any_ = pl.BlockSpec(memory_space=pl.ANY)
    args = [seg, half_index, ids, q, k, v, dom, doo, om, oo, lsem, lseo, seg, cos, sin, low, up, nm]
    alias = {}
    if before is not None:
        alias[len(args)] = 2
        args.append(before)
    return pl.pallas_call(functools.partial(back_kernel, blk, s),
        grid_spec=pltpu.PrefetchScalarGridSpec(num_scalar_prefetch=3, grid=(P,),
            in_specs=[full, full, full, hlf, hlf, hlf, hlf, ls, ls, pl.BlockSpec((S, L), lambda p, *_: (0, 0)),
                tb, tb, pl.BlockSpec((1, L, rank), lambda p, *_: (s, 0, 0)),
                pl.BlockSpec((1, 3, rank, 128), lambda p, seg, h, ids: (ids[s], 0, 0, p)), any_] + [any_] * len(alias),
            out_specs=[gp, gp, pl.BlockSpec((1, rank, pay), lambda p, *_: (s, 0, 0)), lg, lg],
            scratch_shapes=[pltpu.VMEM((L, 128), F32)] * 3 + [pltpu.VMEM((L, rank), F32), pltpu.VMEM(nm.shape[1:], BF), pltpu.SemaphoreType.DMA]),
        out_shape=[sd((1, 3, R, W), BF), sd((1, 3, R, W), BF), sd((S, rank, pay), BF), sd((1, R, rank), F32), sd((1, R, rank), F32)],
        input_output_aliases=alias,
        compiler_params=pltpu.CompilerParams(dimension_semantics=("arbitrary",), vmem_limit_bytes=VMEM_LIMIT),
        cost_estimate=pl.CostEstimate(flops=18 * 10**9, bytes_accessed=10**7, transcendentals=8 * 10**6),
        name="attend_back")(*args)

def final_kernel(ids, x_ref, gain_ref, wo_ref, wr_ref, ad_ref, mid_ref, gm_ref, gr_ref, lm_ref, lr_ref, *rest):
    gn = nn((lm_ref[0] + lr_ref[0]).astype(BF), ad_ref[0])
    for b in range(3):
        gn += nt(gm_ref[0, b], wo_ref[b]) + nt(gr_ref[0, b], wr_ref[b])
    c, rstd = norm_stats(x_ref[0].astype(F32))
    rest[-1][0] = mid_ref[0] + norm_back(gn, c, rstd, gain_ref[...].astype(F32)[None, :])

def final_call(s, ids, x, gain, w_own, w_its, ad, mid, parts, before=None, rows=256):
    S, R, D = x.shape
    W = w_own.shape[2]
    rank = ad.shape[1]
    wsp = pl.BlockSpec((3, D, W), lambda i, ids: (0, 0, 0))
    row = pl.BlockSpec((1, rows, D), lambda i, ids: (s, i, 0))
    gp = pl.BlockSpec((1, 3, rows, W), lambda i, ids: (0, 0, i, 0))
    lg = pl.BlockSpec((1, rows, rank), lambda i, ids: (0, i, 0))
    in_specs = [row, pl.BlockSpec((D,), lambda i, ids: (0,)), wsp, wsp, pl.BlockSpec((1, rank, D), lambda i, ids: (ids[s], 0, 0)), row,
        gp, gp, lg, lg]
    args = [ids, x, gain, w_own, w_its, ad, mid, *parts]
    alias = {}
    if before is not None:
        alias[len(args)] = 0
        args.append(before)
        in_specs.append(pl.BlockSpec(memory_space=pl.ANY))
    return pl.pallas_call(final_kernel,
        grid_spec=pltpu.PrefetchScalarGridSpec(num_scalar_prefetch=1, grid=(R // rows,), in_specs=in_specs, out_specs=row),
        out_shape=jax.ShapeDtypeStruct((S, R, D), F32),
        input_output_aliases=alias,
        compiler_params=pltpu.CompilerParams(dimension_semantics=("arbitrary",), vmem_limit_bytes=VMEM_LIMIT),
        cost_estimate=pl.CostEstimate(flops=4 * 10**9, bytes_accessed=10**7, transcendentals=10**4),
        name="final")(*args)

def unpack_kernel(in_ref, up_ref, down_ref):
    rank = in_ref.shape[0]
    W = up_ref.shape[3]
    for r in range(rank):
        for b in range(3):
            up_ref[:, b, r, :] = in_ref[r, :, b * W:(b + 1) * W].astype(F32)
        down_ref[:, r, :] = in_ref[r, :, 3 * W:].astype(F32)

def unpack_call(shares, W, D):
    rank, adapters, _ = shares.shape
    vm = pl.BlockSpec(memory_space=pltpu.VMEM)
    return pl.pallas_call(unpack_kernel, in_specs=[vm], out_specs=[vm, vm],
        out_shape=[jax.ShapeDtypeStruct((adapters, 3, rank, W), F32), jax.ShapeDtypeStruct((adapters, rank, D), F32)],
        compiler_params=pltpu.CompilerParams(vmem_limit_bytes=VMEM_LIMIT),
        cost_estimate=pl.CostEstimate(flops=10**6, bytes_accessed=2 * 10**6, transcendentals=0),
        name="unpack")(shares)


def unpack_units_kernel(at_ref, in_ref, iu_ref, md_ref, od_ref, *tables):
    rank = in_ref.shape[0]
    half = od_ref.shape[2]
    ffh = md_ref.shape[2]
    main = ffh // 256 * 256
    tail = ffh - main
    own_first = at_ref[0] == 0
    for r in range(rank):
        row = lambda a, n: in_ref[r, :, a:a + n].astype(F32)
        o = 3 * main + half
        ends = row(o + 6 * half, 3 * tail)
        for i in range(3):
            unit = jnp.concatenate([row(i * main, main), ends[:, i * tail:(i + 1) * tail]], 1)
            if i < 2:
                iu_ref[:, r, i, :] = unit
            else:
                md_ref[:, r, :] = unit
        od_ref[:, r, :] = row(3 * main, half)
        for i, ref in enumerate(tables):
            own, got = row(o + i * half, half), row(o + (3 + i) * half, half)
            ref[:, r, :half] = jnp.where(own_first, own, got)
            ref[:, r, half:] = jnp.where(own_first, got, own)

def unpack_units_call(at, shares, half, ffh):
    rank, adapters, _ = shares.shape
    vm = pl.BlockSpec(memory_space=pltpu.VMEM)
    sd = lambda *sh: jax.ShapeDtypeStruct((adapters, rank) + sh, F32)
    return pl.pallas_call(unpack_units_kernel, in_specs=[pl.BlockSpec(memory_space=pltpu.SMEM), vm], out_specs=[vm] * 6,
        out_shape=[sd(2, ffh), sd(ffh), sd(half)] + [sd(2 * half)] * 3,
        compiler_params=pltpu.CompilerParams(vmem_limit_bytes=VMEM_LIMIT),
        cost_estimate=pl.CostEstimate(flops=10**6, bytes_accessed=6 * 10**6, transcendentals=0),
        name="unpack_units")(at, shares)


HEAD_DIM = 64
ROPE_BASE = 160000.0


def rotary_tables(length):
    inverse = 1.0 / ROPE_BASE ** (np.arange(0, HEAD_DIM, 2) / HEAD_DIM)
    angles = np.arange(length)[:, None] * inverse[None, :]
    cos, sin = np.cos(angles), np.sin(angles)
    return (
        jnp.asarray(np.concatenate([cos, cos, cos, cos], 1), F32),
        jnp.asarray(np.concatenate([-sin, sin, -sin, sin], 1), F32),
    )


def spread(packed, tag_at, tags, groups, shards):
    S, rank, m = packed.shape
    if shards != rank:
        flat = [packed[:, :, a:b].reshape(S, shards, -1) for a, b in groups]
        packed = jnp.concatenate(flat + [jnp.broadcast_to(packed[:, :1, tag_at:tag_at + tags], (S, shards, tags))], -1)
        tag_at = packed.shape[2] - tags
    got = lax.all_to_all(packed, "dp", 1, 1, tiled=True).reshape(S * shards, -1)
    sums = lax.dot_general(got[:, tag_at:tag_at + tags], got, (((0,), (0,)), ((), ())), preferred_element_type=F32)
    if shards != rank:
        return sums[:, :tag_at]
    return jnp.concatenate([sums[:, a:b] for a, b in groups], -1)


def collect(shares, shards):
    wide = jnp.broadcast_to(shares.astype(BF), (shards,) + shares.shape)
    return lax.all_to_all(wide, "dp", 0, 0, tiled=True)


def body(x, cotangent, norm_in, norm_mid, w_qkv, w_out, w_in, w_ff, qkv_down, qkv_up, out_down, out_up, in_down, in_up,
         mlp_down, ff_up, segs, ids):
    other = lambda a: lax.ppermute(a, "tensor", [(0, 1), (1, 0)])
    tie = lax.optimization_barrier
    t = lax.axis_index("tensor")
    shards = lax.axis_size("dp")
    mine, its = t.astype(jnp.int32).reshape(1), (1 - t).astype(jnp.int32).reshape(1)
    S, R, D = x.shape
    L = segs.shape[1]
    x_its = other(x)
    w_qkv = w_qkv.transpose(1, 0, 2)
    w_in = w_in.transpose(1, 2, 0)
    qkv_down, out_down, in_down, mlp_down = (a.transpose(0, 2, 1) for a in (qkv_down, out_down, in_down, mlp_down))
    qkv_up, in_up = qkv_up.transpose(0, 2, 1, 3), in_up.transpose(0, 2, 1, 3)
    gain_in, gain_mid = norm_in, norm_mid
    half = w_out.shape[0]
    ffh = w_ff.shape[0]
    main = ffh // 256 * 256
    tail = ffh - main
    rank = out_up.shape[1]
    adapters = out_up.shape[0]

    w_out_its, w_in_its, w_ff_its, w_qkv_its = other(w_out), other(w_in), other(w_ff), other(w_qkv)
    out_down_its, in_up_its, mlp_down_its = other(out_down), other(in_up), other(mlp_down)

    cos, sin = rotary_tables(L)
    first = qkv_call(ids, mine, x, gain_in, w_qkv, qkv_down, qkv_up, cos, sin)
    q, k, v, low, normed = qkv_call(ids, its, x_its, gain_in, w_qkv, qkv_down, qkv_up, cos, sin, before=first)
    ctx_its, lse_its = att_call(segs, its, q, k, v)
    ctx_got = other(ctx_its)
    ctx_mine, lse_mine = att_call(segs, mine, q, k, v)
    output, grad_mid, gc_mine, gc_its, packed = mlp_call(
        ids, mine, x, ctx_mine, ctx_got, cotangent, gain_mid, out_down, out_down_its, in_up, in_up_its, mlp_down, mlp_down_its,
        out_up, in_down, ff_up, w_out, w_out_its, w_in, w_in_its, w_ff, w_ff_its)
    gc_got = other(gc_its)

    lanes = 3 * main + 4 * half
    units = lanes - 3 * half
    units, ends = lanes - 3 * half, lanes + 3 * tail
    size = packed.shape[2] // 2
    groups = [(0, units), (units, lanes), (lanes, ends)]
    shares = spread(packed, ends, adapters, groups + [(size + a, size + b) for a, b in groups], shards)

    back = lambda s, gc_got, before=None: back_call(
        s, segs, mine, ids, q, k, v, gc_mine, gc_got, ctx_mine, ctx_its, lse_mine, lse_its, cos, sin, low, qkv_up, normed, before)
    gp_mine0, gp_its0, packed, lg_mine0, lg_its0 = back(0, gc_got)
    gp_got0, lg_got0 = other(gp_its0), other(lg_its0)
    shares, packed = tie((shares, packed))
    c0, c1, c2 = (rank * n // shards for n in (units, lanes, ends))
    own, its_part = shares[:, :c2], shares[:, c2:]
    got = other(jnp.concatenate([its_part, own[:, c0:c1]], -1).astype(BF)).astype(F32)
    own = own + got[:, :c2]
    sums = collect(jnp.concatenate([own[:, :c1], its_part[:, c0:c1] + got[:, c2:], own[:, c1:]], -1), shards)
    gp_mine1, gp_its1, packed, lg_mine1, lg_its1 = back(1, gc_got, packed)
    sums, packed = tie((sums, packed))
    gp_got1, lg_got1 = other(gp_its1), other(lg_its1)
    m = packed.shape[2] - 128
    shares = spread(packed, m, adapters, ((0, m - D), (m - D, m)), shards)
    grad_input = final_call(0, ids, x, gain_in, w_qkv, w_qkv_its, qkv_down, grad_mid, (gp_mine0, gp_got0, lg_mine0, lg_got0))
    shares, grad_input = tie((shares, grad_input))
    cut = rank * (m - D) // shards
    downs = shares[:, cut:]
    shares = jnp.concatenate([shares[:, :cut], downs + other(downs)], -1)
    shares, sums, gp_got1 = tie((shares, sums, gp_got1))
    qsums = collect(shares, shards)
    grad_input = final_call(1, ids, x, gain_in, w_qkv, w_qkv_its, qkv_down, grad_mid, (gp_mine1, gp_got1, lg_mine1, lg_got1), grad_input)

    whole = lambda a: a.transpose(1, 0, 2).reshape(adapters, rank, -1)
    if shards == rank:
        g_in_up, g_mlp_down, g_out_down, g_ff_up, g_in_down, g_out_up = unpack_units_call(mine, sums, half, ffh)
    else:
        a, own, got, b = (whole(z) for z in jnp.split(sums, (c0, c1, 2 * c1 - c0), axis=2))
        unit = lambda i: jnp.concatenate([a[..., i * main:(i + 1) * main], b[..., i * tail:(i + 1) * tail]], -1).astype(F32)
        g_in_up, g_mlp_down = jnp.stack([unit(0), unit(1)], 2), unit(2)
        g_out_down = a[..., 3 * main:].astype(F32)
        lo, hi = jnp.where(t == 0, own, got), jnp.where(t == 0, got, own)
        g_ff_up, g_in_down, g_out_up = (
            jnp.concatenate([lo[..., i * half:(i + 1) * half], hi[..., i * half:(i + 1) * half]], -1).astype(F32) for i in range(3))
    g_mlp_down, g_out_down = g_mlp_down.transpose(0, 2, 1), g_out_down.transpose(0, 2, 1)
    if shards == rank:
        g_qkv_up, g_qkv_down = unpack_call(qsums, (m - D) // 3, D)
    else:
        g_qkv_up = whole(qsums[..., :cut]).astype(F32).reshape(adapters, rank, 3, -1).transpose(0, 2, 1, 3)
        g_qkv_down = whole(qsums[..., cut:]).astype(F32)
    g_qkv_up, g_qkv_down = g_qkv_up.transpose(0, 2, 1, 3), g_qkv_down.transpose(0, 2, 1)
    return (output, grad_input, g_qkv_down, g_qkv_up, g_out_down, g_out_up, g_in_down.transpose(0, 2, 1), g_in_up, g_mlp_down, g_ff_up)


def solution(mesh):
    return jax.shard_map(
        body,
        mesh=mesh,
        in_specs=(
            P("dp", "tensor", None),
            P("dp", "tensor", None),
            P(),
            P(),
            P(None, None, "tensor"),
            P("tensor", None),
            P(None, None, "tensor"),
            P("tensor", None),
            P(),
            P(None, None, None, "tensor"),
            P(None, "tensor", None),
            P(),
            P(),
            P(None, None, None, "tensor"),
            P(None, "tensor", None),
            P(),
            P("dp", None),
            P("dp"),
        ),
        out_specs=(
            P("dp", "tensor", None),
            P("dp", "tensor", None),
            P(),
            P(None, None, None, "tensor"),
            P(None, "tensor", None),
            P(),
            P(),
            P(None, None, None, "tensor"),
            P(None, "tensor", None),
            P(),
        ),
        check_vma=False,
    )
```
